32 devices in a mesh: dp: 16 (over z, x, core), tensor: 2 (over y).
Axes of the slice: x: 2, y: 2, z: 4, core: 2. Of those that a mesh axis runs over, the one named last changes fastest.
Arguments:
- layer_in: bfloat16 [8192, 1536], P('dp'), may hold values from -6 to 6
- norm1_gain: float32 [1536], replicated, may hold values from 0.1 to 1.9
- w_query: bfloat16 [1536, 1536], P(None, 'tensor'), may hold values from -0.3125 to 0.3125
- w_key: bfloat16 [1536, 512], P(None, 'tensor'), may hold values from -0.15625 to 0.15625
- w_value: bfloat16 [1536, 512], P(None, 'tensor'), may hold values from -0.15625 to 0.15625
- w_out: bfloat16 [1536, 1536], P('tensor'), may hold values from -0.75 to 0.75
- norm2_gain: float32 [1536], replicated, may hold values from 0.1 to 1.9
- router: bfloat16 [1536, 16], replicated, may hold values from -0.10986328 to 0.10986328
- w_gate: bfloat16 [16, 1536, 1024], P(None, None, 'tensor'), may hold values from -0.15625 to 0.15625
- w_up: bfloat16 [16, 1536, 1024], P(None, None, 'tensor'), may hold values from -0.15625 to 0.15625
- w_down: bfloat16 [16, 1024, 1536], P(None, 'tensor'), may hold values from -0.375 to 0.375
- segments: int32 [8192], replicated, may hold values from 0 to 7, never falling along the last dimension, each value on 1 to 4096 neighbouring positions
- routes: int32 [8192, 2], P('dp'), may hold values from 0 to 15, all different within a row; in each aligned block of 512 rows (0 to 511, 512 to 1023, ...) at most 128 rows name the same one
- out_grad: bfloat16 [8192, 1536], P('dp'), may hold values from -6 to 6
Outputs:
- layer_out: bfloat16 [8192, 1536], P(('dp', 'tensor'))
- input_grad: float32 [8192, 1536], P(('dp', 'tensor'))
- norm1_gain_grad: float32 [1536], replicated
- w_query_grad: float32 [1536, 1536], P('dp', 'tensor')
- w_key_grad: float32 [1536, 512], P('dp', 'tensor')
- w_value_grad: float32 [1536, 512], P('dp', 'tensor')
- w_out_grad: float32 [1536, 1536], P('tensor', 'dp')
- norm2_gain_grad: float32 [1536], replicated
- router_grad: float32 [1536, 16], replicated
- w_gate_grad: float32 [16, 1536, 1024], P('dp', None, 'tensor')
- w_up_grad: float32 [16, 1536, 1024], P('dp', None, 'tensor')
- w_down_grad: float32 [16, 1024, 1536], P('dp', 'tensor')
The draws below stay inside these ranges and needn't reach their ends.
Inputs may be any that keep to these rules, and one draw needn't show every extreme that they name: `segments`: document numbers never fall along the tokens; each document has 1 to 4096 tokens, and one has exactly 4096. `routes`: each token names 2 different experts; among the tokens of one index of dp no expert is named more than 128 times, and in every draw some expert is named exactly 128 times there.
All inputs are finite; a program needn't handle non-finite values.
Results may differ from the reference program's by a relative error of at most 0.02.
The reference program's roundings to bfloat16 on the way count: a program that leaves them out, or rounds other values in their place, can miss the bound.
Values may be sent and summed in bfloat16 or wider, within the bound.
No kernel may reach another device: no remote copies, remote signals or barrier semaphores. Data moves between devices by JAX's collectives and lax.ppermute only.
A program may use at most 448 MiB of HBM per device.

```python
import math
import jax
import jax.numpy as jnp
import numpy as np
from jax import lax

D = 1536
H = 24
KVH = 8
HD = 64
E = 16
TOP = 2
FF = 1024
TOK_DEV = 512
SEQ_LEN = 4096
TOKENS = 8192
DOCS = 8
CAP = 128


def block_levels(stream_key, shape, shards, low, top_value):
    factor_of = 1.0
    for axis_at, shards_of in shards:
        heights = jax.random.uniform(jax.random.fold_in(jax.random.fold_in(stream_key, 6), axis_at), (shards_of,), jnp.float32, low / len(shards), top_value / len(shards))
        factor_of = factor_of * jnp.repeat(jnp.exp(heights), shape[axis_at] // shards_of).reshape((-1,) + (1,) * (len(shape) - 1 - axis_at))
    return factor_of


def split_up(number_of, total, reach, slope):
    loads = [(1 << 20) // math.isqrt(rank ** slope) + 1 for rank in range(2, number_of + 1)]
    spare, given = total - reach - (number_of - 1), [1] * (number_of - 1)
    while spare > 0:
        candidates = [i for i in range(number_of - 1) if given[i] < reach]
        pool, remaining = sum([loads[i] for i in candidates]), spare
        for i in candidates:
            addition = min(reach - given[i], max(1, remaining * loads[i] // pool), spare)
            given[i] = given[i] + addition
            spare = spare - addition
    return np.array([reach] + given)


def ragged(rng, number_of, total, limit, skew):
    if number_of == 2:
        one = jax.random.randint(rng, (), max(1, total - limit), min(limit, total - 1) + 1)
        return jnp.stack([one, total - one])
    lengths = jnp.asarray(split_up(number_of, total, limit, skew), jnp.int32)
    couples = (number_of - 1) // 2
    giver, sink = lengths[1:1 + 2 * couples:2], lengths[2:2 + 2 * couples:2]
    room = jnp.minimum(giver - 1, limit - sink)
    moved = jax.random.randint(jax.random.fold_in(rng, 1), (couples,), 0, 1 << 20) % (room + 1)
    lengths = lengths.at[1:1 + 2 * couples:2].set(giver - moved).at[2:2 + 2 * couples:2].set(sink + moved)
    return lengths[jax.random.permutation(jax.random.fold_in(rng, 2), number_of)]


def deal_out(own_key, own, number, rows, number_of, top, reach, slope):
    order = jax.random.permutation(own_key, number_of)
    crowded, common = portions_of(number_of, rows * top, reach, slope, True), portions_of(number_of, rows * top, reach, slope, False)
    places = jnp.arange(number_of)

    def named(lengths, offset_by):
        used = int((lengths > 0).sum())
        fixed = max(1, used // 4)
        passed = fixed + (places - fixed + offset_by * (used - fixed)) % max(1, number_of - fixed)
        return jnp.zeros((number_of,), jnp.int32).at[order[jnp.where(places < fixed, places, passed)]].set(jnp.asarray(lengths, jnp.int32))

    lengths = jnp.where(number % 4 == 0, named(crowded, number // 4), named(common, number - number // 4 - 1))
    mixed = jax.random.permutation(jax.random.fold_in(own, 3), number_of)
    giver, receiver = mixed[0:number_of // 2 * 2:2], mixed[1:number_of // 2 * 2:2]
    margin = jnp.minimum(lengths[giver] - 1, reach - lengths[receiver]) // 2
    margin = jnp.where((giver == order[0]) | (receiver == order[0]) | (lengths[receiver] == 0), 0, jnp.maximum(margin, 0))
    passed = jax.random.randint(jax.random.fold_in(own, 4), (number_of // 2,), 0, 1 << 20) % (margin + 1)
    lengths = lengths.at[giver].add(-passed).at[receiver].add(passed)
    items = jnp.searchsorted(jnp.cumsum(lengths), jnp.arange(rows * top), side="right").astype(jnp.int32)
    grid = items.reshape(top, rows).T
    grid = grid[jax.random.permutation(jax.random.fold_in(own, 1), rows)]
    offset_by = jax.random.randint(jax.random.fold_in(own, 2), (rows, 1), 0, top)
    return jnp.take_along_axis(grid, (jnp.arange(top)[None, :] + offset_by) % top, axis=1)


def portions_of(number_of, total, reach, lean, full):
    loads = [(1 << 20) // math.isqrt(rank ** lean) + 1 for rank in range(1, number_of + 1)]
    largest = reach if full else min(reach, max(-(-total // number_of), total * loads[0] // sum(loads)))
    least = 1 if total - largest >= number_of - 1 else 0
    holding, spare = [largest] + [least] * (number_of - 1), total - largest - least * (number_of - 1)
    while spare > 0:
        movable = [i for i in range(1, number_of) if holding[i] < largest] or [i for i in range(1, number_of) if holding[i] < reach]
        pool, left = sum([loads[i] for i in movable]), spare
        for i in movable:
            addition = min(reach - holding[i], max(1, left * loads[i] // pool), spare)
            holding[i] = holding[i] + addition
            spare = spare - addition
    return np.array(holding)


def bell_draw(rng, shape, deviation, bound, split=(), kind=jnp.bfloat16):
    loudness = block_levels(rng, shape, split, -0.22, 0.18) if split else 1.0
    drawn = jax.random.normal(rng, shape, jnp.float32) * deviation * loudness
    return jnp.minimum(jnp.maximum(drawn, -bound), bound).astype(kind)


def setup_inputs(seed: int = 0) -> dict:
    arg_keys = jax.random.split(jax.random.key(seed), 15)
    layer_in = bell_draw(arg_keys[0], (TOKENS, D), 1.0, 6.0, ((0, 16),))
    norm1_gain = jnp.clip(1.0 + 0.18 * jax.random.normal(arg_keys[1], (D,), jnp.float32), 0.1, 1.9)
    w_query = bell_draw(arg_keys[2], (D, H * HD), (D // 4) ** -0.5, 0.3125, ((1, 2),))
    w_key = bell_draw(arg_keys[3], (D, KVH * HD), D ** -0.5, 0.15625, ((1, 2),))
    w_value = bell_draw(arg_keys[4], (D, KVH * HD), D ** -0.5, 0.15625, ((1, 2),))
    w_out = bell_draw(arg_keys[5], (H * HD, D), HD ** -0.5, 0.75, ((0, 2),))
    norm2_gain = jnp.clip(1.0 + 0.18 * jax.random.normal(arg_keys[6], (D,), jnp.float32), 0.1, 1.9)
    router = bell_draw(arg_keys[7], (D, E), 0.018, 0.10986328)
    w_gate = bell_draw(arg_keys[8], (E, D, FF), D ** -0.5, 0.15625, ((2, 2),))
    w_up = bell_draw(arg_keys[9], (E, D, FF), D ** -0.5, 0.15625, ((2, 2),))
    w_down = bell_draw(arg_keys[10], (E, FF, D), (FF // 4) ** -0.5, 0.375, ((1, 2),))
    segments = jnp.searchsorted(jnp.cumsum(ragged(arg_keys[11], DOCS, TOKENS, SEQ_LEN, 2)), jnp.arange(TOKENS), side="right").astype(jnp.int32)
    routes_keys = jax.random.split(jax.random.fold_in(arg_keys[12], 1), TOKENS // TOK_DEV)
    routes_turns = jax.random.permutation(jax.random.fold_in(arg_keys[12], 3), TOKENS // TOK_DEV)
    routes = jax.vmap(lambda own, number: deal_out(jax.random.fold_in(arg_keys[12], 2), own, number, TOK_DEV, E, TOP, CAP, 2))(routes_keys, routes_turns).reshape((TOKENS, TOP))
    out_grad = bell_draw(arg_keys[13], (TOKENS, D), 1.0, 6.0, ((0, 16),))
    return {"layer_in": layer_in, "norm1_gain": norm1_gain, "w_query": w_query, "w_key": w_key, "w_value": w_value, "w_out": w_out, "norm2_gain": norm2_gain, "router": router, "w_gate": w_gate, "w_up": w_up, "w_down": w_down, "segments": segments, "routes": routes, "out_grad": out_grad}


EPS = 1e-05
HIGH = lax.Precision.HIGHEST

@jax.custom_vjp
def low(v):
    return lax.optimization_barrier(v.astype(jnp.bfloat16)).astype(jnp.float32)

@jax.custom_vjp
def low_back(v):
    return v

def low_keep(v):
    return (low(v), None)

def low_pass(kept, grad):
    return (grad,)

def back_keep(v):
    return (v, None)

def back_low(kept, grad):
    return (low(grad),)
low.defvjp(low_keep, low_pass)
low_back.defvjp(back_keep, back_low)

def rounded_both(value):
    return low_back(low(value))

def rms_norm(value, gain):
    factor = lax.rsqrt(lax.optimization_barrier(jnp.mean(value * value, axis=-1, keepdims=True)) + EPS)
    return value * factor * gain

def attention(query, keys, values, segments):
    total = query.shape[0]
    rows = min(512, total)
    group = H // KVH
    width = SEQ_LEN + rows
    seg_ints = segments.astype(jnp.int32)
    key_pad = jnp.concatenate([jnp.zeros((SEQ_LEN, KVH * HD), jnp.float32), keys], 0)
    val_pad = jnp.concatenate([jnp.zeros((SEQ_LEN, KVH * HD), jnp.float32), values], 0)
    seg_pad = jnp.concatenate([jnp.full((SEQ_LEN,), -1, jnp.int32), seg_ints], 0)

    def one_block(start):
        q_blk = lax.dynamic_slice_in_dim(query, start, rows, 0).reshape(rows, KVH, group, HD)
        k_blk = lax.dynamic_slice_in_dim(key_pad, start, width, 0).reshape(width, KVH, HD)
        v_blk = lax.dynamic_slice_in_dim(val_pad, start, width, 0).reshape(width, KVH, HD)
        seg_query = lax.dynamic_slice_in_dim(seg_ints, start, rows, 0)
        seg_key = lax.dynamic_slice_in_dim(seg_pad, start, width, 0)
        pos_query = start + jnp.arange(rows, dtype=jnp.int32)
        pos_key = start - SEQ_LEN + jnp.arange(width, dtype=jnp.int32)
        visible = (seg_query[:, None] == seg_key[None, :]) & (pos_key[None, :] <= pos_query[:, None])
        scores = low_back(jnp.einsum('qkgd,skd->kgqs', q_blk, k_blk, precision=HIGH) * 0.125)
        scores = jnp.where(visible[None, None], scores, -1000000000.0)
        probs = low(jax.nn.softmax(scores, axis=-1))
        result = jnp.einsum('kgqs,skd->qkgd', probs, v_blk, precision=HIGH)
        return result.reshape(rows, H * HD)
    starts = jnp.arange(total // rows, dtype=jnp.int32) * rows
    return lax.map(jax.checkpoint(one_block), starts).reshape(total, H * HD)

def feed_forward(hidden_blk, route_blk, norm2_gain, router, w_gate, w_up, w_down):
    normed_mid = low(rms_norm(hidden_blk, norm2_gain))
    logits = jnp.dot(normed_mid, router, precision=HIGH, preferred_element_type=jnp.float32)
    picks = (route_blk[:, :, None] == jnp.arange(E, dtype=jnp.int32)[None, None, :]).astype(jnp.float32)
    chosen = lax.optimization_barrier(jnp.sum(picks * logits[:, None, :], axis=-1))
    gates = jax.nn.softmax(chosen, axis=-1)
    combine = lax.optimization_barrier(jnp.sum(picks * gates[:, :, None], axis=1))
    result = hidden_blk
    for expert in range(E):
        gate_pre = low_back(jnp.dot(normed_mid, w_gate[expert], precision=HIGH, preferred_element_type=jnp.float32))
        up_pre = low_back(jnp.dot(normed_mid, w_up[expert], precision=HIGH, preferred_element_type=jnp.float32))
        act = low(jax.nn.silu(gate_pre) * up_pre)
        expert_out = low_back(jnp.dot(act, w_down[expert], precision=HIGH, preferred_element_type=jnp.float32))
        result = result + combine[:, expert:expert + 1] * expert_out
    return result

def forward(layer_in, norm1_gain, w_query, w_key, w_value, w_out, norm2_gain, router, w_gate, w_up, w_down, segments, routes):
    normed_in = low(rms_norm(layer_in, norm1_gain))
    query = rounded_both(jnp.dot(normed_in, w_query, precision=HIGH, preferred_element_type=jnp.float32))
    keys = rounded_both(jnp.dot(normed_in, w_key, precision=HIGH, preferred_element_type=jnp.float32))
    values = rounded_both(jnp.dot(normed_in, w_value, precision=HIGH, preferred_element_type=jnp.float32))
    mixed = rounded_both(attention(query, keys, values, segments))
    hidden = layer_in + low_back(jnp.dot(mixed, w_out, precision=HIGH, preferred_element_type=jnp.float32))
    total = hidden.shape[0]
    rows = min(4096, total)

    def post(pair):
        return feed_forward(pair[0], pair[1], norm2_gain, router, w_gate, w_up, w_down)
    result = lax.map(jax.checkpoint(post), (hidden.reshape(total // rows, rows, D), routes.reshape(total // rows, rows, TOP)))
    return result.reshape(total, D)

def reference(layer_in, norm1_gain, w_query, w_key, w_value, w_out, norm2_gain, router, w_gate, w_up, w_down, segments, routes, out_grad):

    def run(start_in, gain_one, query_weight, key_weight, value_weight, proj_weight, gain_two, router_weight, gate_weight, up_weight, down_weight):
        return forward(start_in, gain_one, query_weight, key_weight, value_weight, proj_weight, gain_two, router_weight, gate_weight, up_weight, down_weight, segments, routes)
    result, pull = jax.vjp(run, layer_in.astype(jnp.float32), norm1_gain.astype(jnp.float32), w_query.astype(jnp.float32), w_key.astype(jnp.float32), w_value.astype(jnp.float32), w_out.astype(jnp.float32), norm2_gain.astype(jnp.float32), router.astype(jnp.float32), w_gate.astype(jnp.float32), w_up.astype(jnp.float32), w_down.astype(jnp.float32))
    grads = pull(out_grad.astype(jnp.float32))
    return (result.astype(jnp.bfloat16), grads[0], grads[1], grads[2], grads[3], grads[4], grads[5], grads[6], grads[7], grads[8], grads[9], grads[10])
```

```python
import functools

import jax
import jax.numpy as jnp
from jax import lax
from jax.experimental import pallas as pl
from jax.experimental.pallas import tpu as pltpu
from jax.sharding import PartitionSpec as P

HD = 64
PAIR = 2 * HD
CAP = 128
EPS = 1e-05
HIGH = lax.Precision.HIGHEST
NEG = -1000000000.0
BF = jnp.bfloat16
F32 = jnp.float32

NT = (((1,), (1,)), ((), ()))
TN = (((0,), (0,)), ((), ()))


def dot(a, b, dims=None):
    if dims is None:
        return jnp.dot(a, b, preferred_element_type=F32)
    return lax.dot_general(a, b, dims, preferred_element_type=F32)


def across(x, axis, mask):
    n = lax.axis_size(axis)
    return lax.ppermute(x, axis, [(i, i ^ mask) for i in range(n)])


def bits_of(n):
    return [1 << k for k in range(n.bit_length() - 1)]


def after(x, y):
    return lax.optimization_barrier((x, y))


def to_owner(x):
    return lax.all_to_all(x, "dp", 0, 0, tiled=True)


def norm_factor(value):
    return lax.rsqrt(jnp.mean(value * value, axis=-1, keepdims=True) + EPS)


def norm_back(unit, factor, gain, grad):
    inner = gain * grad
    return factor * (inner - unit * jnp.mean(unit * inner, axis=-1, keepdims=True))


def total(x):
    for axis in ("dp", "tensor"):
        for bit in bits_of(lax.axis_size(axis)):
            x = x + across(x, axis, bit)
    return x


def scatter_tensor(x):
    n = lax.axis_size("tensor")
    if n != 2:
        return lax.psum_scatter(x.astype(BF), "tensor", scatter_dimension=0, tiled=True).astype(F32)
    me = lax.axis_index("tensor")
    part = x.shape[0] // 2
    sent = lax.dynamic_slice_in_dim(x, (1 - me) * part, part, 0).astype(BF)
    own = lax.dynamic_slice_in_dim(x, me * part, part, 0)
    return own.astype(F32) + across(sent, "tensor", 1).astype(F32)


def gather_tensor(x, dim):
    n = lax.axis_size("tensor")
    if n != 2:
        return lax.all_gather(x, "tensor", axis=dim, tiled=True)
    other = across(x, "tensor", 1)
    low = lax.axis_index("tensor") == 0
    return jnp.concatenate([jnp.where(low, x, other), jnp.where(low, other, x)], dim)


def xor_blocks(blocks, index):
    for bit in bits_of(len(blocks)):
        crossed = (index & bit) != 0
        blocks = [jnp.where(crossed, blocks[s ^ bit], block) for s, block in enumerate(blocks)]
    return blocks


def columns_of(x, count):
    size = x.shape[1] // count
    return [x[:, s * size : (s + 1) * size] for s in range(count)]


def scatter_rows(x):
    n = lax.axis_size("dp")
    at = lax.axis_index("dp")
    bits = bits_of(n)
    x = x.astype(BF)
    if not bits:
        return x.astype(F32)
    x = halve_first(x, at, n)
    half = x.shape[1] // 2
    outs = []
    for piece, order in ((x[:, :half], bits[1:]), (x[:, half:], bits[2:] + bits[1:2])):
        outs.append(halve_rest(piece, at, order))
    return jnp.concatenate(outs, 1).astype(F32)


def halve_first(x, at, n):
    size = x.shape[0] // n
    view = x.reshape(n // 2, 2, size, x.shape[1])
    mine = at % 2

    def pick(which):
        return lax.dynamic_index_in_dim(view, which, 1, keepdims=False)

    return (pick(mine) + across(pick(1 - mine), "dp", 1)).reshape(-1, x.shape[1])


def halve_rest(x, at, order):
    left = sorted(order)
    for bit in order:
        high = 1
        for other in left:
            if other > bit:
                high *= 2
        view = x.reshape(high, 2, -1, x.shape[1])
        mine = (at // bit) % 2
        kept = lax.dynamic_index_in_dim(view, mine, 1, keepdims=False)
        sent = lax.dynamic_index_in_dim(view, 1 - mine, 1, keepdims=False)
        x = (kept + across(sent, "dp", bit)).reshape(-1, x.shape[1])
        left.remove(bit)
    return x


def join_heads(x):
    lines, heads, rows, size = x.shape
    return x.transpose(0, 2, 1, 3).reshape(lines, rows, heads * size)


def attend_kernel(
    heads, rows, lines, stride, meta, q_ref, kv_ref, start_ref, raw_ref, log_ref, m_s, l_s, acc_s
):
    slot = pl.program_id(0)
    place = meta[0]
    own = meta[1 + slot]
    low = meta[1 + lines + slot]
    clear = meta[1 + 2 * lines + slot]
    m_s[...] = jnp.full_like(m_s, -3e38)
    l_s[...] = jnp.zeros_like(l_s)
    acc_s[...] = jnp.zeros_like(acc_s)

    def step(blk, masked):
        x = blk ^ place
        kv = kv_ref[(x % stride) * lines + x // stride]
        if masked:
            shape = (rows, rows)
            key_pos = lax.broadcasted_iota(jnp.int32, shape, 0) + blk * rows
            q_pos = lax.broadcasted_iota(jnp.int32, shape, 1) + own * rows
            seen = (key_pos >= start_ref[0]) & (key_pos <= q_pos)
        for h in range(heads):
            s = dot(kv, q_ref[0, h], NT)
            if masked:
                s = jnp.where(seen, s, NEG)
            m_old = m_s[h : h + 1, :]
            m_new = jnp.maximum(m_old, jnp.max(s, axis=0, keepdims=True))
            p = jnp.exp(s - m_new)
            alpha = jnp.exp(m_old - m_new)
            l_s[h : h + 1, :] = l_s[h : h + 1, :] * alpha + jnp.sum(p, axis=0, keepdims=True)
            acc_s[h] = acc_s[h] * alpha + dot(kv, p.astype(BF), TN)
            m_s[h : h + 1, :] = m_new

    def body(blk, carry):
        full = (blk >= clear) & (blk < own)

        @pl.when(full)
        def _():
            step(blk, False)

        @pl.when(jnp.logical_not(full))
        def _():
            step(blk, True)

        return carry

    lax.fori_loop(low, own + 1, body, 0)
    for h in range(heads):
        raw_ref[0, h] = (acc_s[h] / l_s[h : h + 1, :]).T
    log_ref[0] = m_s[...] + jnp.log(l_s[...])


def attend(meta, qz, kv, start_row, stride):
    lines, heads, rows, _ = qz.shape
    blocks = kv.shape[0]
    grid_spec = pltpu.PrefetchScalarGridSpec(
        num_scalar_prefetch=1,
        grid=(lines,),
        in_specs=[
            pl.BlockSpec((1, heads, rows, PAIR), lambda i, m: (i, 0, 0, 0)),
            pl.BlockSpec((blocks, rows, PAIR), lambda i, m: (0, 0, 0)),
            pl.BlockSpec((1, 1, rows), lambda i, m: (i, 0, 0)),
        ],
        out_specs=[
            pl.BlockSpec((1, heads, rows, PAIR), lambda i, m: (i, 0, 0, 0)),
            pl.BlockSpec((1, 8, rows), lambda i, m: (i, 0, 0)),
        ],
        scratch_shapes=[
            pltpu.VMEM((8, rows), F32),
            pltpu.VMEM((8, rows), F32),
            pltpu.VMEM((heads, PAIR, rows), F32),
        ],
    )
    return pl.pallas_call(
        functools.partial(attend_kernel, heads, rows, lines, stride),
        grid_spec=grid_spec,
        out_shape=[
            jax.ShapeDtypeStruct((lines, heads, rows, PAIR), F32),
            jax.ShapeDtypeStruct((lines, 8, rows), F32),
        ],
        compiler_params=pltpu.CompilerParams(vmem_limit_bytes=48 * 1024 * 1024),
        cost_estimate=pl.CostEstimate(
            flops=36 * 4 * rows * rows * PAIR * 2, bytes_accessed=8 << 20, transcendentals=36 * rows * rows
        ),
        name="attend",
    )(meta, qz, kv, start_row)


def attend_back_kernel(
    heads, rows, lines, stride, meta, q_ref, g_ref, raw_ref, log_ref, start_ref, kv_ref,
    dq_ref, dkv_ref, dq_s, dkv_s, delta_s,
):
    slot = pl.program_id(0)
    place = meta[0]
    own = meta[1 + slot]
    low = meta[1 + lines + slot]
    clear = meta[1 + 2 * lines + slot]

    @pl.when(slot == 0)
    def _():
        dkv_s[...] = jnp.zeros_like(dkv_s)

    dq_s[...] = jnp.zeros_like(dq_s)
    for h in range(heads):
        prod = raw_ref[0, h] * g_ref[0, h].astype(F32)
        delta_s[h : h + 1, :] = jnp.sum(prod.T, axis=0, keepdims=True)

    def step(blk, masked):
        x = blk ^ place
        index = (x % stride) * lines + x // stride
        kv = kv_ref[index]
        if masked:
            shape = (rows, rows)
            key_pos = lax.broadcasted_iota(jnp.int32, shape, 0) + blk * rows
            q_pos = lax.broadcasted_iota(jnp.int32, shape, 1) + own * rows
            seen = (key_pos >= start_ref[0]) & (key_pos <= q_pos)
        for h in range(heads):
            q = q_ref[0, h]
            g = g_ref[0, h]
            s = dot(kv, q, NT)
            if masked:
                s = jnp.where(seen, s, NEG)
            p = jnp.exp(s - log_ref[0, h : h + 1, :])
            gp = dot(kv, g, NT)
            gs = (p * (gp - delta_s[h : h + 1, :])).astype(BF)
            part = dot(gs, q) + dot(p.astype(BF), g)
            dkv_s[index] += part
            dq_s[h] += dot(gs, kv, TN)

    def body(blk, carry):
        full = (blk >= clear) & (blk < own)

        @pl.when(full)
        def _():
            step(blk, False)

        @pl.when(jnp.logical_not(full))
        def _():
            step(blk, True)

        return carry

    lax.fori_loop(low, own + 1, body, 0)
    dq_ref[0] = (dq_s[...] * 0.125).astype(BF)

    @pl.when(slot == lines - 1)
    def _():
        dkv_ref[...] = dkv_s[...].astype(BF)


def attend_back(meta, qz, gz, raw, logs, start_row, kv, stride):
    lines, heads, rows, _ = qz.shape
    blocks = kv.shape[0]
    wide = pl.BlockSpec((1, heads, rows, PAIR), lambda i, m: (i, 0, 0, 0))
    whole = pl.BlockSpec((blocks, rows, PAIR), lambda i, m: (0, 0, 0))
    grid_spec = pltpu.PrefetchScalarGridSpec(
        num_scalar_prefetch=1,
        grid=(lines,),
        in_specs=[
            wide,
            wide,
            wide,
            pl.BlockSpec((1, 8, rows), lambda i, m: (i, 0, 0)),
            pl.BlockSpec((1, 1, rows), lambda i, m: (i, 0, 0)),
            whole,
        ],
        out_specs=[wide, whole],
        scratch_shapes=[
            pltpu.VMEM((heads, rows, PAIR), F32),
            pltpu.VMEM((blocks, rows, PAIR), F32),
            pltpu.VMEM((8, rows), F32),
        ],
    )
    return pl.pallas_call(
        functools.partial(attend_back_kernel, heads, rows, lines, stride),
        grid_spec=grid_spec,
        out_shape=[
            jax.ShapeDtypeStruct((lines, heads, rows, PAIR), BF),
            jax.ShapeDtypeStruct((blocks, rows, PAIR), BF),
        ],
        compiler_params=pltpu.CompilerParams(vmem_limit_bytes=56 * 1024 * 1024),
        cost_estimate=pl.CostEstimate(
            flops=36 * 10 * rows * rows * PAIR * 2, bytes_accessed=10 << 20, transcendentals=36 * rows * rows
        ),
        name="attend_back",
    )(meta, qz, gz, raw, logs, start_row, kv)


def experts_kernel(x_ref, g_ref, gate_ref, wg_ref, wu_ref, wd_ref, out_ref, back_ref, inner_ref):
    x = x_ref[0]
    g = g_ref[0]
    gate = gate_ref[0]
    gate_pre = dot(x, wg_ref[0])
    up_pre = dot(x, wu_ref[0])
    sigma = jax.nn.sigmoid(gate_pre)
    silu = gate_pre * sigma
    act = (silu * up_pre).astype(BF)
    out = dot(act, wd_ref[0])
    g_float = g.astype(F32)
    inner = jnp.sum(out * g_float, axis=-1, keepdims=True)
    inner_ref[0] = jnp.broadcast_to(inner, (x.shape[0], 128)).T[:8]
    out_ref[0] = (gate * out).astype(BF)
    grad_expert = (gate * g_float).astype(BF)
    grad_act = dot(grad_expert, wd_ref[0], NT)
    grad_gate = (grad_act * up_pre * sigma * (1.0 + gate_pre * (1.0 - sigma))).astype(BF)
    grad_up = (grad_act * silu).astype(BF)
    back_ref[0] = (dot(grad_gate, wg_ref[0], NT) + dot(grad_up, wu_ref[0], NT)).astype(BF)


def run_experts(x, g, gate, w_gate, w_up, w_down):
    experts, cap, width = x.shape
    hidden = w_gate.shape[2]

    def of(*shape):
        return pl.BlockSpec((1,) + shape, lambda e: (e, 0, 0))

    return pl.pallas_call(
        experts_kernel,
        grid=(experts,),
        in_specs=[
            of(cap, width),
            of(cap, width),
            of(cap, 1),
            of(width, hidden),
            of(width, hidden),
            of(hidden, width),
        ],
        out_specs=[of(cap, width), of(cap, width), of(8, cap)],
        out_shape=[
            jax.ShapeDtypeStruct((experts, cap, width), BF),
            jax.ShapeDtypeStruct((experts, cap, width), BF),
            jax.ShapeDtypeStruct((experts, 8, cap), F32),
        ],
        compiler_params=pltpu.CompilerParams(vmem_limit_bytes=48 * 1024 * 1024),
        cost_estimate=pl.CostEstimate(
            flops=experts * cap * width * hidden * 12,
            bytes_accessed=experts * width * (hidden * 6 + cap * 8),
            transcendentals=experts * cap * hidden,
        ),
        name="experts",
    )(x, g, gate, w_gate, w_up, w_down)


def shards(
    layer_in,
    norm1_gain,
    w_query,
    w_key,
    w_value,
    w_out,
    norm2_gain,
    router,
    w_gate,
    w_up,
    w_down,
    segments,
    routes,
    out_grad,
):
    rows, width = layer_in.shape
    kv_heads = w_key.shape[1] // HD
    group = w_query.shape[1] // HD // kv_heads
    q_cols = group * HD
    experts = w_gate.shape[0]
    dp = lax.axis_size("dp")
    place = lax.axis_index("dp")
    tensor_size = lax.axis_size("tensor")
    tensor_at = lax.axis_index("tensor")
    lines = kv_heads
    stride = dp // lines
    line = place // stride
    part = rows // tensor_size
    first = tensor_at * part
    cols = width // tensor_size

    names = jnp.arange(experts, dtype=jnp.int32)
    named = jnp.any(routes[:, :, None] == names[None, None, :], axis=1)
    earlier = jnp.tril(jnp.ones((rows, rows), BF), -1)
    slots = jnp.where(named, dot(earlier, named.astype(BF)).astype(jnp.int32), -1)
    in_slot = slots.T[:, None, :] == jnp.arange(CAP, dtype=jnp.int32)[None, :, None]
    to_slots = in_slot.astype(BF).reshape(experts * CAP, rows)
    from_slots = (
        (slots[:, :, None] == jnp.arange(CAP, dtype=jnp.int32)[None, None, :])
        .astype(BF)
        .reshape(rows, experts * CAP)
    )

    def halves(x):
        own = lax.dynamic_slice_in_dim(x, tensor_at * cols, cols, 2)
        return own[..., : cols // 2], own[..., cols // 2 :]

    def whole_columns(one, two):
        size = one.shape[2] // tensor_size
        pieces = []
        for t in range(tensor_size):
            pieces += [one[..., t * size : (t + 1) * size], two[..., t * size : (t + 1) * size]]
        return jnp.concatenate(pieces, 2)

    q_blocks = place ^ (jnp.arange(lines, dtype=jnp.int32) * stride)
    seg_query = jnp.stack(
        [lax.dynamic_slice_in_dim(segments, q_blocks[s] * rows, rows, 0) for s in range(lines)]
    )
    starts = jnp.sum(
        (segments[None, None, :] < seg_query[:, :, None]).astype(jnp.int32), axis=-1
    )
    meta = jnp.concatenate(
        [place[None], q_blocks, starts[:, 0] // rows, (starts[:, -1] + rows - 1) // rows]
    ).astype(jnp.int32)

    lined = [xor_blocks(columns_of(w, lines), line) for w in (w_key, w_value, w_query)]
    w_kv = jnp.concatenate([w for pair in zip(*lined[:2]) for w in pair], 1)
    w_q = jnp.concatenate(lined[2], 1)
    w_o = jnp.concatenate(
        xor_blocks([w_out[s * q_cols : (s + 1) * q_cols] for s in range(lines)], line), 0
    )

    in_float = layer_in.astype(F32)
    factor_one = norm_factor(in_float)
    unit_one = in_float * factor_one
    normed_in = (unit_one * norm1_gain).astype(BF)
    kv_mine = dot(normed_in, w_kv).astype(BF)
    kv_mine, normed_late = after(kv_mine, normed_in)
    q_mine = dot(normed_late, w_q).astype(BF)

    def to_lines(x, size):
        return jnp.stack(
            [
                x[:, s * size : (s + 1) * size]
                if s == 0
                else across(x[:, s * size : (s + 1) * size], "dp", s * stride)
                for s in range(lines)
            ]
        )

    kv = to_lines(kv_mine, PAIR)
    kv = kv.reshape((1,) + kv.shape)
    for bit in reversed(bits_of(stride)):
        kv = jnp.stack([kv, across(kv, "dp", bit)], 1).reshape((-1,) + kv.shape[1:])
    kv = kv.reshape(dp, rows, PAIR)
    q = to_lines(q_mine, q_cols) * jnp.asarray(0.125, BF)
    q_heads = q.reshape(lines, rows, group, HD).transpose(0, 2, 1, 3)
    nothing = jnp.zeros_like(q_heads)
    q_wide = jnp.concatenate([q_heads, nothing], 3)
    g_slots = dot(to_slots, out_grad).astype(BF).reshape(experts, CAP, width)
    g_sent, kv = after(halves(g_slots), kv)
    g_first = to_owner(g_sent[0])
    raw, logs = attend(meta, q_wide, kv, starts[:, None, :], stride)
    raw, g_first = after(raw, g_first)
    mixed_far = join_heads(raw[..., HD:].astype(BF))

    def from_lines(x):
        return [x[s] if s == 0 else across(x[s], "dp", s * stride) for s in range(lines)]

    mixed = jnp.concatenate(from_lines(mixed_far), 1)
    g_late, mixed = after(g_sent[1], mixed)
    g_second = to_owner(g_late)
    attn = scatter_tensor(dot(mixed, w_o))
    hidden = lax.dynamic_slice_in_dim(layer_in, first, part, 0).astype(F32) + attn
    factor_two = norm_factor(hidden)
    unit_two = hidden * factor_two
    normed_mid = gather_tensor((unit_two * norm2_gain).astype(BF), 0)

    logits = dot(normed_mid, router)
    peak = jnp.max(jnp.where(named, logits, -jnp.inf), axis=1, keepdims=True)
    expo = jnp.where(named, jnp.exp(jnp.where(named, logits - peak, 0.0)), 0.0)
    gates = expo / jnp.sum(expo, axis=1, keepdims=True)
    slot_gate = jnp.sum(jnp.where(in_slot, gates.T[:, None, :], 0.0), axis=-1)

    x_slots = dot(to_slots, normed_mid).astype(BF).reshape(experts, CAP, width)
    x_sent = halves(x_slots)
    x_early, g_second = after(x_sent[0], g_second)
    x_first = to_owner(x_early)
    gate_owned = to_owner(slot_gate)
    g_first, x_slots = after(g_first, x_slots)
    g_first = gather_tensor(g_first, 2)

    out_slots, back_slots, inner_slots = run_experts(
        x_slots, g_slots, slot_gate[:, :, None], w_gate, w_up, w_down
    )
    back_slots, (x_first, g_first) = after(back_slots, (x_first, g_first))
    x_late, back_slots = after(x_sent[1], back_slots)
    x_second = to_owner(x_late)
    moe_part = dot(from_slots, out_slots.reshape(experts * CAP, width))
    grad_gates = jnp.sum(
        jnp.where(
            slots[:, :, None] == jnp.arange(CAP, dtype=jnp.int32)[None, None, :],
            inner_slots[None, :, 0, :],
            0.0,
        ),
        axis=-1,
    )
    grad_logits = gates * (grad_gates - jnp.sum(gates * grad_gates, axis=-1, keepdims=True))
    router_part = lax.dot_general(
        grad_logits, normed_mid.astype(F32), TN, precision=HIGH, preferred_element_type=F32
    )
    grad_mid_part = dot(from_slots, back_slots.reshape(experts * CAP, width)) + lax.dot_general(
        grad_logits, router.astype(F32), NT, precision=HIGH, preferred_element_type=F32
    )
    grad_mid = scatter_tensor(grad_mid_part)
    moe_part, grad_mid = after(moe_part, grad_mid)
    layer_out = (hidden + scatter_tensor(moe_part)).astype(BF)
    gain_two_part = jnp.sum(grad_mid * unit_two, axis=0)
    grad_rows = lax.dynamic_slice_in_dim(out_grad, first, part, 0).astype(F32)
    grad_hidden = grad_rows + norm_back(unit_two, factor_two, norm2_gain, grad_mid)
    hidden_low = gather_tensor(grad_hidden.astype(BF), 0)
    (x_first, g_second), hidden_low = after((x_first, g_second), hidden_low)
    x_first = gather_tensor(x_first, 2)
    g_second = gather_tensor(g_second, 2)
    g_owned = whole_columns(g_first, g_second)
    grad_mixed = dot(hidden_low, w_o, NT).astype(BF)
    small = total(jnp.concatenate([router_part, gain_two_part[None]], 0))

    g = to_lines(grad_mixed, q_cols)
    g_heads = g.reshape(lines, rows, group, HD).transpose(0, 2, 1, 3)
    g_wide = jnp.concatenate([nothing, g_heads], 3)
    dq_far, dkv = attend_back(meta, q_wide, g_wide, raw, logs, starts[:, None, :], kv, stride)

    dkv, x_second = after(dkv, x_second)
    x_owned = whole_columns(x_first, gather_tensor(x_second, 2))

    def reduce_back(x):
        for bit in bits_of(stride):
            view = x.reshape((x.shape[0] // 2, 2) + x.shape[1:])
            x = view[:, 0] + across(view[:, 1], "dp", bit)
        return x[0]

    mixed_true = jnp.concatenate(xor_blocks(columns_of(mixed, lines), line), 1)
    proj_out = scatter_rows(dot(hidden_low, mixed_true, TN)).T

    dkv = from_lines(reduce_back(dkv.reshape(stride, lines, rows, PAIR)))
    dq = from_lines(join_heads(dq_far[..., :HD]))
    dkv = jnp.concatenate(dkv, 1)
    dq = jnp.concatenate(dq, 1)
    grad_in_part = dot(dq, w_q, NT) + dot(dkv, w_kv, NT)
    grad_in_rows = scatter_tensor(grad_in_part)
    dqkv = jnp.concatenate(
        xor_blocks(columns_of(dkv, lines), line) + xor_blocks(columns_of(dq, lines), line), 1
    )
    dqkv, (x_owned, g_owned) = after(dqkv, (x_owned, g_owned))
    weight_grad = scatter_rows(dot(normed_in, dqkv, TN))
    kv_grad = weight_grad[:, : lines * PAIR].reshape(-1, lines, 2, HD)
    key_out = kv_grad[:, :, 0].reshape(-1, lines * HD)
    value_out = kv_grad[:, :, 1].reshape(-1, lines * HD)
    query_out = weight_grad[:, lines * PAIR :]

    factor_rows = lax.dynamic_slice_in_dim(factor_one, first, part, 0)
    unit_rows = lax.dynamic_slice_in_dim(in_float, first, part, 0) * factor_rows
    input_grad = grad_hidden + norm_back(unit_rows, factor_rows, norm1_gain, grad_in_rows)
    gain_one_grad = total(jnp.sum(grad_in_rows * unit_rows, axis=0)[None])[0]
    gain_two_grad = small[experts]
    router_grad = small[:experts].T

    held = experts // dp
    wg = lax.dynamic_slice_in_dim(w_gate, place * held, held, 0)
    wu = lax.dynamic_slice_in_dim(w_up, place * held, held, 0)
    wd = lax.dynamic_slice_in_dim(w_down, place * held, held, 0)
    grad_outs = []
    for e in range(held):
        x = x_owned.reshape(dp, held, CAP, width)[:, e].reshape(dp * CAP, width)
        gx = g_owned.reshape(dp, held, CAP, width)[:, e].reshape(dp * CAP, width)
        gate = gate_owned.reshape(dp, held, CAP)[:, e].reshape(dp * CAP, 1)
        gate_pre = dot(x, wg[e])
        up_pre = dot(x, wu[e])
        sigma = jax.nn.sigmoid(gate_pre)
        silu = gate_pre * sigma
        act = (silu * up_pre).astype(BF)
        grad_expert = (gate * gx.astype(F32)).astype(BF)
        grad_act = dot(grad_expert, wd[e], NT)
        grad_gate = (grad_act * up_pre * sigma * (1.0 + gate_pre * (1.0 - sigma))).astype(BF)
        grad_up = (grad_act * silu).astype(BF)
        grad_outs.append((dot(x, grad_gate, TN), dot(x, grad_up, TN), dot(act, grad_expert, TN)))
    gate_out, up_out, down_out = (jnp.stack(each) for each in zip(*grad_outs))
    return (
        layer_out,
        input_grad,
        gain_one_grad,
        query_out,
        key_out,
        value_out,
        proj_out,
        gain_two_grad,
        router_grad,
        gate_out,
        up_out,
        down_out,
    )


def solution(mesh):
    in_specs = (
        P("dp", None),
        P(),
        P(None, "tensor"),
        P(None, "tensor"),
        P(None, "tensor"),
        P("tensor", None),
        P(),
        P(),
        P(None, None, "tensor"),
        P(None, None, "tensor"),
        P(None, "tensor", None),
        P(),
        P("dp", None),
        P("dp", None),
    )
    out_specs = (
        P(("dp", "tensor"), None),
        P(("dp", "tensor"), None),
        P(),
        P("dp", "tensor"),
        P("dp", "tensor"),
        P("dp", "tensor"),
        P("tensor", "dp"),
        P(),
        P(),
        P("dp", None, "tensor"),
        P("dp", None, "tensor"),
        P("dp", "tensor", None),
    )
    return jax.shard_map(shards, mesh=mesh, in_specs=in_specs, out_specs=out_specs, check_vma=False)
```

```python
import functools

import jax
import jax.numpy as jnp
from jax import lax
from jax.experimental import pallas as pl
from jax.experimental.pallas import tpu as pltpu
from jax.sharding import PartitionSpec as P

HD = 64
PAIR = 2 * HD
CAP = 128
DOCS = 8
EPS = 1e-05
HIGH = lax.Precision.HIGHEST
NEG = -1000000000.0
BF = jnp.bfloat16
F32 = jnp.float32

NT = (((1,), (1,)), ((), ()))
TN = (((0,), (0,)), ((), ()))


def dot(a, b, dims=None):
    if dims is None:
        return jnp.dot(a, b, preferred_element_type=F32)
    return lax.dot_general(a, b, dims, preferred_element_type=F32)


def across(x, axis, mask):
    n = lax.axis_size(axis)
    return lax.ppermute(x, axis, [(i, i ^ mask) for i in range(n)])


def bits_of(n):
    return [1 << k for k in range(n.bit_length() - 1)]


def after(x, y):
    return lax.optimization_barrier((x, y))


def to_owner(x):
    return lax.all_to_all(x, "dp", 0, 0, tiled=True)


def norm_factor(value):
    return lax.rsqrt(jnp.mean(value * value, axis=-1, keepdims=True) + EPS)


def norm_back(unit, factor, gain, grad):
    inner = gain * grad
    return factor * (inner - unit * jnp.mean(unit * inner, axis=-1, keepdims=True))


def total(x):
    for axis in ("dp", "tensor"):
        for bit in bits_of(lax.axis_size(axis)):
            x = x + across(x, axis, bit)
    return x


def scatter_tensor(x):
    n = lax.axis_size("tensor")
    if n != 2:
        return lax.psum_scatter(x.astype(BF), "tensor", scatter_dimension=0, tiled=True).astype(F32)
    me = lax.axis_index("tensor")
    part = x.shape[0] // 2
    sent = lax.dynamic_slice_in_dim(x, (1 - me) * part, part, 0).astype(BF)
    own = lax.dynamic_slice_in_dim(x, me * part, part, 0)
    return own.astype(F32) + across(sent, "tensor", 1).astype(F32)


def swap_tensor(x, dim):
    if lax.axis_size("tensor") != 2:
        return (lax.all_gather(x, "tensor", axis=dim, tiled=True),)
    return x, across(x, "tensor", 1)


def assemble(parts, dim):
    if len(parts) == 1:
        return parts[0]
    own, other = parts
    low = lax.axis_index("tensor") == 0
    return jnp.concatenate([jnp.where(low, own, other), jnp.where(low, other, own)], dim)


def gather_tensor(x, dim):
    return assemble(swap_tensor(x, dim), dim)


def xor_blocks(blocks, index):
    for bit in bits_of(len(blocks)):
        crossed = (index & bit) != 0
        blocks = [jnp.where(crossed, blocks[s ^ bit], block) for s, block in enumerate(blocks)]
    return blocks


def columns_of(x, count):
    size = x.shape[1] // count
    return [x[:, s * size : (s + 1) * size] for s in range(count)]


def scatter_rows(x, later):
    n = lax.axis_size("dp")
    at = lax.axis_index("dp")
    bits = bits_of(n)
    x = x.astype(BF)
    x = halve_first(x, at, n)
    half = x.shape[1] // 2
    orders = (bits[1:], bits[2:] + bits[1:2])
    pieces = [
        halve_rest(piece, at, order[:1], bits[1:])
        for piece, order in zip((x[:, :half], x[:, half:]), orders)
    ]
    pieces, later = after(pieces, later)
    outs = [
        halve_rest(piece, at, order[1:], [b for b in bits[1:] if b != order[0]])
        for piece, order in zip(pieces, orders)
    ]
    return jnp.concatenate(outs, 1).astype(F32), later


def halve_first(x, at, n):
    size = x.shape[0] // n
    view = x.reshape(n // 2, 2, size, x.shape[1])
    mine = at & 1

    def pick(which):
        return lax.dynamic_index_in_dim(view, which, 1, keepdims=False)

    return (pick(mine) + across(pick(1 - mine), "dp", 1)).reshape(-1, x.shape[1])


def halve_rest(x, at, order, left):
    left = sorted(left)
    for bit in order:
        high = 1
        for other in left:
            if other > bit:
                high *= 2
        view = x.reshape(high, 2, -1, x.shape[1])
        mine = (at >> (bit.bit_length() - 1)) & 1
        kept = lax.dynamic_index_in_dim(view, mine, 1, keepdims=False)
        sent = lax.dynamic_index_in_dim(view, 1 - mine, 1, keepdims=False)
        x = (kept + across(sent, "dp", bit)).reshape(-1, x.shape[1])
        left.remove(bit)
    return x


def project_kernel(lines, q_cols, at, x_ref, gain_ref, wq_ref, wk_ref, wv_ref, normed_ref, *rest):
    kv_refs, q_refs = rest[:lines], rest[lines : 2 * lines]
    kv_s, q_s = rest[2 * lines :]
    x = x_ref[...].astype(F32)
    scale = lax.rsqrt(jnp.mean(x * x, axis=-1, keepdims=True) + EPS)
    normed = (x * scale * gain_ref[...]).astype(BF)
    normed_ref[...] = normed
    key = dot(normed, wk_ref[...])
    value = dot(normed, wv_ref[...])
    query = dot(normed, wq_ref[...])
    for c in range(lines):
        pair = [key[:, c * HD : (c + 1) * HD], value[:, c * HD : (c + 1) * HD]]
        kv_s[c] = jnp.concatenate(pair, 1).astype(BF)
        q_s[c] = query[:, c * q_cols : (c + 1) * q_cols].astype(BF) * jnp.asarray(0.125, BF)
    for s in range(lines):
        kv_refs[s][...] = kv_s[s ^ at[0]]
        q_refs[s][...] = q_s[s ^ at[0]]


def project(line, x, gain, w_query, w_key, w_value, lines):
    rows, width = x.shape
    q_cols = w_query.shape[1] // lines

    def whole(*shape):
        return pl.BlockSpec(shape, lambda i, m: (0,) * len(shape))

    out = [(rows, width)] + [(rows, PAIR)] * lines + [(rows, q_cols)] * lines
    outs = pl.pallas_call(
        functools.partial(project_kernel, lines, q_cols),
        grid_spec=pltpu.PrefetchScalarGridSpec(
            num_scalar_prefetch=1,
            grid=(1,),
            in_specs=[
                whole(rows, width),
                whole(1, width),
                whole(*w_query.shape),
                whole(*w_key.shape),
                whole(*w_value.shape),
            ],
            out_specs=[whole(*shape) for shape in out],
            scratch_shapes=[
                pltpu.VMEM((lines, rows, PAIR), BF),
                pltpu.VMEM((lines, rows, q_cols), BF),
            ],
        ),
        out_shape=[jax.ShapeDtypeStruct(shape, BF) for shape in out],
        compiler_params=pltpu.CompilerParams(vmem_limit_bytes=48 * 1024 * 1024),
        cost_estimate=pl.CostEstimate(
            flops=2 * rows * width * (w_query.shape[1] + 2 * w_key.shape[1]),
            bytes_accessed=8 << 20,
            transcendentals=0,
        ),
        name="project",
    )(line[None], x, gain[None], w_query, w_key, w_value)
    return outs[0], outs[1 : 1 + lines], outs[1 + lines :]


def spread_heads(refs, out, heads, high):
    for s, ref in enumerate(refs):
        x = ref[...]
        zero = jnp.zeros((x.shape[0], HD), BF)
        for h in range(heads):
            one = x[:, h * HD : (h + 1) * HD]
            out[s, h] = jnp.concatenate([zero, one] if high else [one, zero], 1)


def gather_blocks(refs, out, lines):
    for m, ref in enumerate(refs):
        out[m * lines : (m + 1) * lines] = ref[...]


def position(meta, lines):
    slot = pl.program_id(0)
    return slot, meta[0], meta[1 + slot], meta[1 + lines + slot], meta[1 + 2 * lines + slot]


def walk(low, clear, own, step):
    def body(blk, carry):
        full = (blk >= clear) & (blk < own)

        @pl.when(full)
        def _():
            step(blk, False)

        @pl.when(jnp.logical_not(full))
        def _():
            step(blk, True)

        return carry

    lax.fori_loop(low, own + 1, body, 0)


def visible(blk, own, rows, start):
    key_pos = lax.broadcasted_iota(jnp.int32, (rows, rows), 0) + blk * rows
    q_pos = lax.broadcasted_iota(jnp.int32, (rows, rows), 1) + own * rows
    return (key_pos >= start) & (key_pos <= q_pos)


def attend_kernel(heads, rows, lines, stride, meta, *refs):
    q_refs, kv_refs, start_ref = refs[:lines], refs[lines : lines + stride], refs[lines + stride]
    outs = refs[lines + stride + 1 :]
    mixed_refs, (raw_ref, log_ref, q_s, kv_s, m_s, l_s, acc_s) = outs[:lines], outs[lines:]
    slot, place, own, low, clear = position(meta, lines)

    @pl.when(slot == 0)
    def _():
        spread_heads(q_refs, q_s, heads, False)
        gather_blocks(kv_refs, kv_s, lines)

    m_s[...] = jnp.full_like(m_s, -3e38)
    l_s[...] = jnp.zeros_like(l_s)
    acc_s[...] = jnp.zeros_like(acc_s)

    def step(blk, masked):
        x = blk ^ place
        kv = kv_s[(x % stride) * lines + x // stride]
        if masked:
            seen = visible(blk, own, rows, start_ref[0])
        for h in range(heads):
            s = dot(kv, q_s[slot, h], NT)
            if masked:
                s = jnp.where(seen, s, NEG)
            m_old = m_s[h : h + 1, :]
            m_new = jnp.maximum(m_old, jnp.max(s, axis=0, keepdims=True))
            p = jnp.exp(s - m_new)
            alpha = jnp.exp(m_old - m_new)
            l_s[h : h + 1, :] = l_s[h : h + 1, :] * alpha + jnp.sum(p, axis=0, keepdims=True)
            acc_s[h] = acc_s[h] * alpha + dot(kv, p.astype(BF), TN)
            m_s[h : h + 1, :] = m_new

    walk(low, clear, own, step)
    parts = []
    for h in range(heads):
        out = (acc_s[h] / l_s[h : h + 1, :]).T
        raw_ref[0, h] = out
        parts.append(out[:, HD:])
    log_ref[0] = m_s[...] + jnp.log(l_s[...])
    mixed = jnp.concatenate(parts, 1).astype(BF)
    for s in range(lines):

        @pl.when(slot == s)
        def _(s=s):
            mixed_refs[s][...] = mixed


def whole_block(shape):
    return pl.BlockSpec(shape, lambda i, m: (0,) * len(shape))


def attend(meta, q, kv, start_row, heads):
    lines, stride = len(q), len(kv)
    rows, q_cols = q[0].shape
    narrow = whole_block((rows, q_cols))
    return pl.pallas_call(
        functools.partial(attend_kernel, heads, rows, lines, stride),
        grid_spec=pltpu.PrefetchScalarGridSpec(
            num_scalar_prefetch=1,
            grid=(lines,),
            in_specs=[narrow] * lines
            + [whole_block((lines, rows, PAIR))] * stride
            + [pl.BlockSpec((1, 1, rows), lambda i, m: (i, 0, 0))],
            out_specs=[narrow] * lines
            + [
                pl.BlockSpec((1, heads, rows, PAIR), lambda i, m: (i, 0, 0, 0)),
                pl.BlockSpec((1, 8, rows), lambda i, m: (i, 0, 0)),
            ],
            scratch_shapes=[
                pltpu.VMEM((lines, heads, rows, PAIR), BF),
                pltpu.VMEM((stride * lines, rows, PAIR), BF),
                pltpu.VMEM((8, rows), F32),
                pltpu.VMEM((8, rows), F32),
                pltpu.VMEM((heads, PAIR, rows), F32),
            ],
        ),
        out_shape=[jax.ShapeDtypeStruct((rows, q_cols), BF)] * lines
        + [
            jax.ShapeDtypeStruct((lines, heads, rows, PAIR), F32),
            jax.ShapeDtypeStruct((lines, 8, rows), F32),
        ],
        compiler_params=pltpu.CompilerParams(vmem_limit_bytes=48 * 1024 * 1024),
        cost_estimate=pl.CostEstimate(
            flops=36 * 4 * rows * rows * PAIR * 2, bytes_accessed=8 << 20, transcendentals=36 * rows * rows
        ),
        name="attend",
    )(meta, *q, *kv, start_row)


def attend_back_kernel(heads, rows, lines, stride, meta, *refs):
    q_refs, g_refs, kv_refs = refs[:lines], refs[lines : 2 * lines], refs[2 * lines : 2 * lines + stride]
    raw_ref, log_ref, start_ref = refs[2 * lines + stride : 2 * lines + stride + 3]
    outs = refs[2 * lines + stride + 3 :]
    dq_refs, (keep_ref, send_ref, q_s, g_s, kv_s, dq_s, dkv_s, delta_s) = outs[:lines], outs[lines:]
    slot, place, own, low, clear = position(meta, lines)

    @pl.when(slot == 0)
    def _():
        spread_heads(q_refs, q_s, heads, False)
        spread_heads(g_refs, g_s, heads, True)
        gather_blocks(kv_refs, kv_s, lines)
        dkv_s[...] = jnp.zeros_like(dkv_s)

    dq_s[...] = jnp.zeros_like(dq_s)
    for h in range(heads):
        prod = raw_ref[0, h] * g_s[slot, h].astype(F32)
        delta_s[h : h + 1, :] = jnp.sum(prod.T, axis=0, keepdims=True)

    def step(blk, masked):
        x = blk ^ place
        index = (x % stride) * lines + x // stride
        kv = kv_s[index]
        if masked:
            seen = visible(blk, own, rows, start_ref[0])
        for h in range(heads):
            q = q_s[slot, h]
            g = g_s[slot, h]
            s = dot(kv, q, NT)
            if masked:
                s = jnp.where(seen, s, NEG)
            p = jnp.exp(s - log_ref[0, h : h + 1, :])
            gp = dot(kv, g, NT)
            gs = (p * (gp - delta_s[h : h + 1, :])).astype(BF)
            part = dot(gs, q) + dot(p.astype(BF), g)
            dkv_s[index] += part
            dq_s[h] += dot(gs, kv, TN)

    walk(low, clear, own, step)
    dq = jnp.concatenate([dq_s[h][:, :HD] * 0.125 for h in range(heads)], 1).astype(BF)
    for s in range(lines):

        @pl.when(slot == s)
        def _(s=s):
            dq_refs[s][...] = dq

    @pl.when(slot == lines - 1)
    def _():
        for m in range(stride):
            half = m // 2
            out = send_ref if m % 2 else keep_ref
            out[half * lines : (half + 1) * lines] = dkv_s[m * lines : (m + 1) * lines].astype(BF)


def attend_back(meta, q, g, kv, raw, logs, start_row, heads):
    lines, stride = len(q), len(kv)
    rows, q_cols = q[0].shape
    blocks = lines * stride
    narrow = whole_block((rows, q_cols))
    half = whole_block((blocks // 2, rows, PAIR))
    return pl.pallas_call(
        functools.partial(attend_back_kernel, heads, rows, lines, stride),
        grid_spec=pltpu.PrefetchScalarGridSpec(
            num_scalar_prefetch=1,
            grid=(lines,),
            in_specs=[narrow] * (2 * lines)
            + [whole_block((lines, rows, PAIR))] * stride
            + [
                pl.BlockSpec((1, heads, rows, PAIR), lambda i, m: (i, 0, 0, 0)),
                pl.BlockSpec((1, 8, rows), lambda i, m: (i, 0, 0)),
                pl.BlockSpec((1, 1, rows), lambda i, m: (i, 0, 0)),
            ],
            out_specs=[narrow] * lines + [half] * 2,
            scratch_shapes=[
                pltpu.VMEM((lines, heads, rows, PAIR), BF),
                pltpu.VMEM((lines, heads, rows, PAIR), BF),
                pltpu.VMEM((blocks, rows, PAIR), BF),
                pltpu.VMEM((heads, rows, PAIR), F32),
                pltpu.VMEM((blocks, rows, PAIR), F32),
                pltpu.VMEM((8, rows), F32),
            ],
        ),
        out_shape=[jax.ShapeDtypeStruct((rows, q_cols), BF)] * lines
        + [jax.ShapeDtypeStruct((blocks // 2, rows, PAIR), BF)] * 2,
        compiler_params=pltpu.CompilerParams(vmem_limit_bytes=56 * 1024 * 1024),
        cost_estimate=pl.CostEstimate(
            flops=36 * 10 * rows * rows * PAIR * 2, bytes_accessed=10 << 20, transcendentals=36 * rows * rows
        ),
        name="attend_back",
    )(meta, *q, *g, *kv, raw, logs, start_row)


def experts_kernel(x_ref, g_ref, gate_ref, wg_ref, wu_ref, wd_ref, out_ref, back_ref, inner_ref):
    x = x_ref[0]
    g = g_ref[0]
    gate = gate_ref[0]
    gate_pre = dot(x, wg_ref[0])
    up_pre = dot(x, wu_ref[0])
    sigma = jax.nn.sigmoid(gate_pre)
    silu = gate_pre * sigma
    act = (silu * up_pre).astype(BF)
    out = dot(act, wd_ref[0])
    g_float = g.astype(F32)
    inner = jnp.sum(out * g_float, axis=-1, keepdims=True)
    inner_ref[0] = jnp.broadcast_to(inner, (x.shape[0], 128)).T[:8]
    out_ref[0] = (gate * out).astype(BF)
    grad_expert = (gate * g_float).astype(BF)
    grad_act = dot(grad_expert, wd_ref[0], NT)
    grad_gate = (grad_act * up_pre * sigma * (1.0 + gate_pre * (1.0 - sigma))).astype(BF)
    grad_up = (grad_act * silu).astype(BF)
    back_ref[0] = (dot(grad_gate, wg_ref[0], NT) + dot(grad_up, wu_ref[0], NT)).astype(BF)


def run_experts(x, g, gate, w_gate, w_up, w_down):
    experts, cap, width = x.shape
    hidden = w_gate.shape[2]

    def of(*shape):
        return pl.BlockSpec((1,) + shape, lambda e: (e, 0, 0))

    return pl.pallas_call(
        experts_kernel,
        grid=(experts,),
        in_specs=[
            of(cap, width),
            of(cap, width),
            of(cap, 1),
            of(width, hidden),
            of(width, hidden),
            of(hidden, width),
        ],
        out_specs=[of(cap, width), of(cap, width), of(8, cap)],
        out_shape=[
            jax.ShapeDtypeStruct((experts, cap, width), BF),
            jax.ShapeDtypeStruct((experts, cap, width), BF),
            jax.ShapeDtypeStruct((experts, 8, cap), F32),
        ],
        compiler_params=pltpu.CompilerParams(vmem_limit_bytes=48 * 1024 * 1024),
        cost_estimate=pl.CostEstimate(
            flops=experts * cap * width * hidden * 12,
            bytes_accessed=experts * width * (hidden * 6 + cap * 8),
            transcendentals=experts * cap * hidden,
        ),
        name="experts",
    )(x, g, gate, w_gate, w_up, w_down)


def owner_forward(e, held, place, x_owned, g_owned, gate_owned, w_gate, w_up, w_down):
    dp, _, cap, width = x_owned.shape[0], held, x_owned.shape[1], x_owned.shape[2]

    def mine(x):
        return x.reshape((dp, held, cap) + x.shape[2:])[:, e].reshape((dp * cap,) + x.shape[2:])

    def weight(w):
        return lax.dynamic_index_in_dim(w, place * held + e, 0, keepdims=False)

    x = mine(x_owned)
    gate_pre = dot(x, weight(w_gate))
    up_pre = dot(x, weight(w_up))
    sigma = jax.nn.sigmoid(gate_pre)
    silu = gate_pre * sigma
    act = (silu * up_pre).astype(BF)
    grad_expert = (mine(gate_owned)[:, None] * mine(g_owned).astype(F32)).astype(BF)
    grad_act = dot(grad_expert, weight(w_down), NT)
    grad_gate = (grad_act * up_pre * sigma * (1.0 + gate_pre * (1.0 - sigma))).astype(BF)
    grad_up = (grad_act * silu).astype(BF)
    return x, act, grad_expert, grad_gate, grad_up


def shards(
    layer_in,
    norm1_gain,
    w_query,
    w_key,
    w_value,
    w_out,
    norm2_gain,
    router,
    w_gate,
    w_up,
    w_down,
    segments,
    routes,
    out_grad,
):
    rows, width = layer_in.shape
    kv_heads = w_key.shape[1] // HD
    group = w_query.shape[1] // HD // kv_heads
    q_cols = group * HD
    experts = w_gate.shape[0]
    dp = lax.axis_size("dp")
    place = lax.axis_index("dp")
    tensor_size = lax.axis_size("tensor")
    tensor_at = lax.axis_index("tensor")
    lines = kv_heads
    stride = dp // lines
    line = place >> (stride.bit_length() - 1)
    part = rows // tensor_size
    first = tensor_at * part
    held = experts // dp
    cols = width // tensor_size

    names = jnp.arange(experts, dtype=jnp.int32)
    named = jnp.any(routes[:, :, None] == names[None, None, :], axis=1)
    earlier = jnp.tril(jnp.ones((rows, rows), BF), -1)
    slots = jnp.where(named, dot(earlier, named.astype(BF)).astype(jnp.int32), -1)
    in_slot = slots.T[:, None, :] == jnp.arange(CAP, dtype=jnp.int32)[None, :, None]
    to_slots = in_slot.astype(BF).reshape(experts * CAP, rows)
    from_slots = (
        (slots[:, :, None] == jnp.arange(CAP, dtype=jnp.int32)[None, None, :])
        .astype(BF)
        .reshape(rows, experts * CAP)
    )

    def halves(x):
        own = lax.dynamic_slice_in_dim(x, tensor_at * cols, cols, 2)
        return own[..., : cols // 2], own[..., cols // 2 :]

    q_blocks = place ^ (jnp.arange(lines, dtype=jnp.int32) * stride)
    seg_query = jnp.stack(
        [lax.dynamic_slice_in_dim(segments, q_blocks[s] * rows, rows, 0) for s in range(lines)]
    )
    documents = jnp.arange(DOCS, dtype=jnp.int32)
    lengths_before = jnp.sum(
        (segments[None, :] < documents[:, None]).astype(jnp.int32), axis=1
    )
    starts = jnp.sum(
        jnp.where(seg_query[None] == documents[:, None, None], lengths_before[:, None, None], 0),
        axis=0,
    )
    shift = rows.bit_length() - 1
    meta = jnp.concatenate(
        [place[None], q_blocks, starts[:, 0] >> shift, (starts[:, -1] + rows - 1) >> shift]
    ).astype(jnp.int32)

    normed_in, kv_mine, q_mine = project(line, layer_in, norm1_gain, w_query, w_key, w_value, lines)

    def to_lines(blocks):
        return [b if s == 0 else across(b, "dp", s * stride) for s, b in enumerate(blocks)]

    kv = [jnp.stack(to_lines(kv_mine))]
    q = to_lines(q_mine)
    for bit in reversed(bits_of(stride)):
        kv = [piece for one in kv for piece in (one, across(one, "dp", bit))]
    g_slots = dot(to_slots, out_grad).astype(BF).reshape(experts, CAP, width)
    g_sent, (kv, q, starts, meta) = after(halves(g_slots), (kv, q, starts, meta))
    g_first = to_owner(g_sent[0])
    *mixed_far, raw, logs = attend(meta, q, kv, starts[:, None, :], group)
    mixed_far, g_first = after(mixed_far, g_first)

    def from_lines(blocks):
        return xor_blocks(to_lines(blocks), line)

    mixed = jnp.concatenate(from_lines(mixed_far), 1)
    g_late, mixed = after(g_sent[1], mixed)
    g_second = to_owner(g_late)
    attn = scatter_tensor(dot(mixed, w_out))
    hidden = lax.dynamic_slice_in_dim(layer_in, first, part, 0).astype(F32) + attn
    factor_two = norm_factor(hidden)
    unit_two = hidden * factor_two
    normed_mid = gather_tensor((unit_two * norm2_gain).astype(BF), 0)

    logits = dot(normed_mid, router)
    peak = jnp.max(jnp.where(named, logits, -jnp.inf), axis=1, keepdims=True)
    expo = jnp.where(named, jnp.exp(jnp.where(named, logits - peak, 0.0)), 0.0)
    gates = expo / jnp.sum(expo, axis=1, keepdims=True)
    slot_gate = jnp.sum(jnp.where(in_slot, gates.T[:, None, :], 0.0), axis=-1)

    x_slots = dot(to_slots, normed_mid).astype(BF).reshape(experts, CAP, width)
    x_early, x_late = halves(x_slots)
    x_early, g_second = after(x_early, g_second)
    x_first = to_owner(x_early)
    gate_high = lax.reduce_precision(slot_gate, 8, 7)
    gate_mid = lax.reduce_precision(slot_gate - gate_high, 8, 7)
    gate_pieces = jnp.stack([gate_high, gate_mid, slot_gate - gate_high - gate_mid], 2)
    x_late = jnp.concatenate(
        [x_late, jnp.pad(gate_pieces.astype(BF), ((0, 0), (0, 0), (0, 125)))], 2
    )
    g_first, x_slots = after(g_first, x_slots)
    g_first = swap_tensor(g_first, 2)

    out_slots, back_slots, inner_slots = run_experts(
        x_slots, g_slots, slot_gate[:, :, None], w_gate, w_up, w_down
    )
    back_slots, (x_first, g_first) = after(back_slots, (x_first, g_first))
    x_late, back_slots = after(x_late, back_slots)
    x_second = to_owner(x_late)
    moe_part = dot(from_slots, out_slots.reshape(experts * CAP, width))
    grad_gates = jnp.sum(
        jnp.where(
            slots[:, :, None] == jnp.arange(CAP, dtype=jnp.int32)[None, None, :],
            inner_slots[None, :, 0, :],
            0.0,
        ),
        axis=-1,
    )
    grad_logits = gates * (grad_gates - jnp.sum(gates * grad_gates, axis=-1, keepdims=True))
    router_part = lax.dot_general(
        grad_logits, normed_mid.astype(F32), TN, precision=HIGH, preferred_element_type=F32
    )
    grad_mid_part = dot(from_slots, back_slots.reshape(experts * CAP, width)) + lax.dot_general(
        grad_logits, router.astype(F32), NT, precision=HIGH, preferred_element_type=F32
    )
    grad_mid = scatter_tensor(grad_mid_part)
    gain_two_part = jnp.sum(grad_mid * unit_two, axis=0)
    grad_rows = lax.dynamic_slice_in_dim(out_grad, first, part, 0).astype(F32)
    grad_hidden = grad_rows + norm_back(unit_two, factor_two, norm2_gain, grad_mid)
    hidden_low = gather_tensor(grad_hidden.astype(BF), 0)
    (x_first, x_second, g_second), hidden_low = after((x_first, x_second, g_second), hidden_low)
    g_second = swap_tensor(g_second, 2)
    gate_owned = jnp.sum(x_second[..., cols // 2 : cols // 2 + 3].astype(F32), axis=2)
    x_owned = swap_tensor(jnp.concatenate([x_first, x_second[..., : cols // 2]], 2), 2)
    grad_mixed = dot(hidden_low, w_out, NT).astype(BF)
    g = to_lines(xor_blocks(columns_of(grad_mixed, lines), line))
    *dq_far, keep, send = attend_back(meta, q, g, kv, raw, logs, starts[:, None, :], group)

    dkv = (keep + across(send, "dp", 1)).reshape(stride // 2, lines, rows, PAIR)
    dkv, dq_far = after(dkv, dq_far)
    for bit in bits_of(stride)[1:]:
        view = dkv.reshape((dkv.shape[0] // 2, 2) + dkv.shape[1:])
        dkv = view[:, 0] + across(view[:, 1], "dp", bit)
    dkv, moe_part, x_owned, g_second = lax.optimization_barrier(
        (dkv[0], moe_part, x_owned, g_second)
    )
    x_owned = assemble(x_owned, 2)
    size = cols // 2
    g_pieces = [assemble(g_first, 2), assemble(g_second, 2)]
    g_owned = jnp.concatenate(
        [g[..., t * size : (t + 1) * size] for t in range(tensor_size) for g in g_pieces], 2
    )
    dq = from_lines(dq_far)
    layer_out = (hidden + scatter_tensor(moe_part)).astype(BF)
    dkv = from_lines([dkv[s] for s in range(lines)])
    owned = [
        owner_forward(e, held, place, x_owned, g_owned, gate_owned, w_gate, w_up, w_down)
        for e in range(held)
    ]
    w_all = jnp.concatenate([w_query, w_key, w_value], 1)
    dqkv = jnp.concatenate(dq + [b[:, :HD] for b in dkv] + [b[:, HD:] for b in dkv], 1)
    weight_part = jnp.concatenate(
        [dot(normed_in, dqkv, TN).astype(BF), dot(hidden_low, mixed, TN).astype(BF)], 1
    )
    dqkv, weight_part, owned = lax.optimization_barrier((dqkv, weight_part, owned))
    grad_in_part = dot(dqkv, w_all, NT)
    in_float = layer_in.astype(F32)
    factor_one = norm_factor(in_float)
    small_in = jnp.concatenate(
        [router_part, gain_two_part[None], jnp.sum(grad_in_part * (in_float * factor_one), axis=0)[None]], 0
    )
    weight_grad, small_in = scatter_rows(weight_part, small_in)
    grad_in_rows = scatter_tensor(grad_in_part)
    ends = [0]
    for size in (lines * q_cols, lines * HD, lines * HD, lines * q_cols):
        ends.append(ends[-1] + size)
    query_out, key_out, value_out, proj_out = (
        weight_grad[:, a:b] for a, b in zip(ends[:-1], ends[1:])
    )
    proj_out = proj_out.T

    factor_rows = lax.dynamic_slice_in_dim(factor_one, first, part, 0)
    unit_rows = lax.dynamic_slice_in_dim(in_float, first, part, 0) * factor_rows
    input_grad = grad_hidden + norm_back(unit_rows, factor_rows, norm1_gain, grad_in_rows)
    small = total(small_in)
    gain_one_grad = small[experts + 1]
    gain_two_grad = small[experts]
    router_grad = small[:experts].T

    grad_outs = [
        (dot(x, grad_gate, TN), dot(x, grad_up, TN), dot(act, grad_expert, TN))
        for x, act, grad_expert, grad_gate, grad_up in owned
    ]
    gate_out, up_out, down_out = (jnp.stack(each) for each in zip(*grad_outs))
    return (
        layer_out,
        input_grad,
        gain_one_grad,
        query_out,
        key_out,
        value_out,
        proj_out,
        gain_two_grad,
        router_grad,
        gate_out,
        up_out,
        down_out,
    )


def solution(mesh):
    in_specs = (
        P("dp", None),
        P(),
        P(None, "tensor"),
        P(None, "tensor"),
        P(None, "tensor"),
        P("tensor", None),
        P(),
        P(),
        P(None, None, "tensor"),
        P(None, None, "tensor"),
        P(None, "tensor", None),
        P(),
        P("dp", None),
        P("dp", None),
    )
    out_specs = (
        P(("dp", "tensor"), None),
        P(("dp", "tensor"), None),
        P(),
        P("dp", "tensor"),
        P("dp", "tensor"),
        P("dp", "tensor"),
        P("tensor", "dp"),
        P(),
        P(),
        P("dp", None, "tensor"),
        P("dp", None, "tensor"),
        P("dp", "tensor", None),
    )
    return jax.shard_map(shards, mesh=mesh, in_specs=in_specs, out_specs=out_specs, check_vma=False)
```

```python
import functools

import jax
import jax.numpy as jnp
from jax import lax
from jax.experimental import pallas as pl
from jax.experimental.pallas import tpu as pltpu
from jax.sharding import PartitionSpec as P

HD = 64
PAIR = 2 * HD
CAP = 128
DOCS = 8
EPS = 1e-05
HIGH = lax.Precision.HIGHEST
NEG = -1000000000.0
BF = jnp.bfloat16
F32 = jnp.float32

NT = (((1,), (1,)), ((), ()))
TN = (((0,), (0,)), ((), ()))


def dot(a, b, dims=None):
    if dims is None:
        return jnp.dot(a, b, preferred_element_type=F32)
    return lax.dot_general(a, b, dims, preferred_element_type=F32)


def across(x, axis, mask):
    n = lax.axis_size(axis)
    return lax.ppermute(x, axis, [(i, i ^ mask) for i in range(n)])


def bits_of(n):
    return [1 << k for k in range(n.bit_length() - 1)]


def after(x, y):
    return lax.optimization_barrier((x, y))


def to_owner(x):
    return lax.all_to_all(x, "dp", 0, 0, tiled=True)


def norm_factor(value):
    return lax.rsqrt(jnp.mean(value * value, axis=-1, keepdims=True) + EPS)


def norm_back(unit, factor, gain, grad):
    inner = gain * grad
    return factor * (inner - unit * jnp.mean(unit * inner, axis=-1, keepdims=True))


def total(x):
    for axis in ("dp", "tensor"):
        bits = bits_of(lax.axis_size(axis))
        while bits:
            one, *bits = bits
            if bits:
                two, *bits = bits
                far, both = across(x, axis, two), across(x, axis, one | two)
                x = (x + across(x, axis, one)) + (far + both)
            else:
                x = x + across(x, axis, one)
    return x


def scatter_tensor(x):
    n = lax.axis_size("tensor")
    if n != 2:
        return lax.psum_scatter(x.astype(BF), "tensor", scatter_dimension=0, tiled=True).astype(F32)
    me = lax.axis_index("tensor")
    part = x.shape[0] // 2
    sent = lax.dynamic_slice_in_dim(x, (1 - me) * part, part, 0).astype(BF)
    own = lax.dynamic_slice_in_dim(x, me * part, part, 0)
    return own.astype(F32) + across(sent, "tensor", 1).astype(F32)


def swap_tensor(x, dim):
    if lax.axis_size("tensor") != 2:
        return (lax.all_gather(x, "tensor", axis=dim, tiled=True),)
    return x, across(x, "tensor", 1)


def assemble(parts, dim):
    if len(parts) == 1:
        return parts[0]
    own, other = parts
    low = lax.axis_index("tensor") == 0
    return jnp.concatenate([jnp.where(low, own, other), jnp.where(low, other, own)], dim)


def gather_tensor(x, dim):
    return assemble(swap_tensor(x, dim), dim)


def xor_blocks(blocks, index):
    for bit in bits_of(len(blocks)):
        crossed = (index & bit) != 0
        blocks = [jnp.where(crossed, blocks[s ^ bit], block) for s, block in enumerate(blocks)]
    return blocks


def columns_of(x, count):
    size = x.shape[1] // count
    return [x[:, s * size : (s + 1) * size] for s in range(count)]


def scatter_rows(keep, send, later):
    n = lax.axis_size("dp")
    x = keep + across(send, "dp", 1)
    x, later = after(x, later)
    groups = [list(range(first, n, 2)) for first in range(2)]
    x = lax.all_to_all(x, "dp", 0, 0, tiled=True, axis_index_groups=groups)
    return jnp.sum(x.astype(F32), axis=0), later


def project_kernel(lines, q_cols, at, x_ref, gain_ref, wq_ref, wk_ref, wv_ref, normed_ref, *rest):
    kv_refs, q_refs = rest[:lines], rest[lines : 2 * lines]
    kv_s, q_s = rest[2 * lines :]
    x = x_ref[...].astype(F32)
    scale = lax.rsqrt(jnp.mean(x * x, axis=-1, keepdims=True) + EPS)
    normed = (x * scale * gain_ref[...]).astype(BF)
    normed_ref[...] = normed
    key = dot(normed, wk_ref[...])
    value = dot(normed, wv_ref[...])
    query = dot(normed, wq_ref[...])
    for c in range(lines):
        pair = [key[:, c * HD : (c + 1) * HD], value[:, c * HD : (c + 1) * HD]]
        kv_s[c] = jnp.concatenate(pair, 1).astype(BF)
        q_s[c] = query[:, c * q_cols : (c + 1) * q_cols].astype(BF) * jnp.asarray(0.125, BF)
    for s in range(lines):
        kv_refs[s][...] = kv_s[s ^ at[0]]
        q_refs[s][...] = q_s[s ^ at[0]]


def project(line, x, gain, w_query, w_key, w_value, lines):
    rows, width = x.shape
    q_cols = w_query.shape[1] // lines

    def whole(*shape):
        return pl.BlockSpec(shape, lambda i, m: (0,) * len(shape))

    out = [(rows, width)] + [(rows, PAIR)] * lines + [(rows, q_cols)] * lines
    outs = pl.pallas_call(
        functools.partial(project_kernel, lines, q_cols),
        grid_spec=pltpu.PrefetchScalarGridSpec(
            num_scalar_prefetch=1,
            grid=(1,),
            in_specs=[
                whole(rows, width),
                whole(1, width),
                whole(*w_query.shape),
                whole(*w_key.shape),
                whole(*w_value.shape),
            ],
            out_specs=[whole(*shape) for shape in out],
            scratch_shapes=[
                pltpu.VMEM((lines, rows, PAIR), BF),
                pltpu.VMEM((lines, rows, q_cols), BF),
            ],
        ),
        out_shape=[jax.ShapeDtypeStruct(shape, BF) for shape in out],
        compiler_params=pltpu.CompilerParams(vmem_limit_bytes=48 * 1024 * 1024),
        cost_estimate=pl.CostEstimate(
            flops=2 * rows * width * (w_query.shape[1] + 2 * w_key.shape[1]),
            bytes_accessed=8 << 20,
            transcendentals=0,
        ),
        name="project",
    )(line[None], x, gain[None], w_query, w_key, w_value)
    return outs[0], outs[1 : 1 + lines], outs[1 + lines :]


def spread_heads(refs, out, heads, high):
    for s, ref in enumerate(refs):
        x = ref[...]
        zero = jnp.zeros((x.shape[0], HD), BF)
        for h in range(heads):
            one = x[:, h * HD : (h + 1) * HD]
            out[s, h] = jnp.concatenate([zero, one] if high else [one, zero], 1)


def gather_blocks(refs, out, lines):
    for m, ref in enumerate(refs):
        out[m * lines : (m + 1) * lines] = ref[...]


def position(meta, lines):
    slot = pl.program_id(0)
    return slot, meta[0], meta[1 + slot], meta[1 + lines + slot], meta[1 + 2 * lines + slot]


def walk(low, clear, own, step):
    def body(blk, carry):
        full = (blk >= clear) & (blk < own)

        @pl.when(full)
        def _():
            step(blk, False)

        @pl.when(jnp.logical_not(full))
        def _():
            step(blk, True)

        return carry

    lax.fori_loop(low, own + 1, body, 0)


def visible(blk, own, rows, start):
    key_pos = lax.broadcasted_iota(jnp.int32, (rows, rows), 0) + blk * rows
    q_pos = lax.broadcasted_iota(jnp.int32, (rows, rows), 1) + own * rows
    return (key_pos >= start) & (key_pos <= q_pos)


def attend_kernel(heads, rows, lines, stride, meta, *refs):
    q_refs, kv_refs, start_ref = refs[:lines], refs[lines : lines + stride], refs[lines + stride]
    outs = refs[lines + stride + 1 :]
    mixed_refs, (raw_ref, log_ref, q_s, kv_s, m_s, l_s, acc_s) = outs[:lines], outs[lines:]
    slot, place, own, low, clear = position(meta, lines)

    @pl.when(slot == 0)
    def _():
        spread_heads(q_refs, q_s, heads, False)
        gather_blocks(kv_refs, kv_s, lines)

    m_s[...] = jnp.full_like(m_s, -3e38)
    l_s[...] = jnp.zeros_like(l_s)
    acc_s[...] = jnp.zeros_like(acc_s)

    def step(blk, masked):
        x = blk ^ place
        kv = kv_s[(x % stride) * lines + x // stride]
        if masked:
            seen = visible(blk, own, rows, start_ref[0])
        for h in range(heads):
            s = dot(kv, q_s[slot, h], NT)
            if masked:
                s = jnp.where(seen, s, NEG)
            m_old = m_s[h : h + 1, :]
            m_new = jnp.maximum(m_old, jnp.max(s, axis=0, keepdims=True))
            p = jnp.exp(s - m_new)
            alpha = jnp.exp(m_old - m_new)
            l_s[h : h + 1, :] = l_s[h : h + 1, :] * alpha + jnp.sum(p, axis=0, keepdims=True)
            acc_s[h] = acc_s[h] * alpha + dot(kv, p.astype(BF), TN)
            m_s[h : h + 1, :] = m_new

    walk(low, clear, own, step)
    parts = []
    for h in range(heads):
        out = (acc_s[h] / l_s[h : h + 1, :]).T
        raw_ref[0, h] = out
        parts.append(out[:, HD:])
    log_ref[0] = m_s[...] + jnp.log(l_s[...])
    mixed = jnp.concatenate(parts, 1).astype(BF)
    for s in range(lines):

        @pl.when(slot == s)
        def _(s=s):
            mixed_refs[s][...] = mixed


def whole_block(shape):
    return pl.BlockSpec(shape, lambda i, m: (0,) * len(shape))


def attend(meta, q, kv, start_row, heads):
    lines, stride = len(q), len(kv)
    rows, q_cols = q[0].shape
    narrow = whole_block((rows, q_cols))
    return pl.pallas_call(
        functools.partial(attend_kernel, heads, rows, lines, stride),
        grid_spec=pltpu.PrefetchScalarGridSpec(
            num_scalar_prefetch=1,
            grid=(lines,),
            in_specs=[narrow] * lines
            + [whole_block((lines, rows, PAIR))] * stride
            + [pl.BlockSpec((1, 1, rows), lambda i, m: (i, 0, 0))],
            out_specs=[narrow] * lines
            + [
                pl.BlockSpec((1, heads, rows, PAIR), lambda i, m: (i, 0, 0, 0)),
                pl.BlockSpec((1, 8, rows), lambda i, m: (i, 0, 0)),
            ],
            scratch_shapes=[
                pltpu.VMEM((lines, heads, rows, PAIR), BF),
                pltpu.VMEM((stride * lines, rows, PAIR), BF),
                pltpu.VMEM((8, rows), F32),
                pltpu.VMEM((8, rows), F32),
                pltpu.VMEM((heads, PAIR, rows), F32),
            ],
        ),
        out_shape=[jax.ShapeDtypeStruct((rows, q_cols), BF)] * lines
        + [
            jax.ShapeDtypeStruct((lines, heads, rows, PAIR), F32),
            jax.ShapeDtypeStruct((lines, 8, rows), F32),
        ],
        compiler_params=pltpu.CompilerParams(vmem_limit_bytes=48 * 1024 * 1024),
        cost_estimate=pl.CostEstimate(
            flops=36 * 4 * rows * rows * PAIR * 2, bytes_accessed=8 << 20, transcendentals=36 * rows * rows
        ),
        name="attend",
    )(meta, *q, *kv, start_row)


def attend_back_kernel(heads, rows, lines, stride, meta, *refs):
    q_refs, g_refs, kv_refs = refs[:lines], refs[lines : 2 * lines], refs[2 * lines : 2 * lines + stride]
    raw_ref, log_ref, start_ref = refs[2 * lines + stride : 2 * lines + stride + 3]
    outs = refs[2 * lines + stride + 3 :]
    dq_refs, (keep_ref, send_ref, q_s, g_s, kv_s, dq_s, dkv_s, delta_s) = outs[:lines], outs[lines:]
    slot, place, own, low, clear = position(meta, lines)

    @pl.when(slot == 0)
    def _():
        spread_heads(q_refs, q_s, heads, False)
        spread_heads(g_refs, g_s, heads, True)
        gather_blocks(kv_refs, kv_s, lines)
        dkv_s[...] = jnp.zeros_like(dkv_s)

    dq_s[...] = jnp.zeros_like(dq_s)
    for h in range(heads):
        prod = raw_ref[0, h] * g_s[slot, h].astype(F32)
        delta_s[h : h + 1, :] = jnp.sum(prod.T, axis=0, keepdims=True)

    def step(blk, masked):
        x = blk ^ place
        index = (x % stride) * lines + x // stride
        kv = kv_s[index]
        if masked:
            seen = visible(blk, own, rows, start_ref[0])
        for h in range(heads):
            q = q_s[slot, h]
            g = g_s[slot, h]
            s = dot(kv, q, NT)
            if masked:
                s = jnp.where(seen, s, NEG)
            p = jnp.exp(s - log_ref[0, h : h + 1, :])
            gp = dot(kv, g, NT)
            gs = (p * (gp - delta_s[h : h + 1, :])).astype(BF)
            part = dot(gs, q) + dot(p.astype(BF), g)
            dkv_s[index] += part
            dq_s[h] += dot(gs, kv, TN)

    walk(low, clear, own, step)
    dq = jnp.concatenate([dq_s[h][:, :HD] * 0.125 for h in range(heads)], 1).astype(BF)
    for s in range(lines):

        @pl.when(slot == s)
        def _(s=s):
            dq_refs[s][...] = dq

    @pl.when(slot == lines - 1)
    def _():
        for m in range(stride):
            half = m // 2
            out = send_ref if m % 2 else keep_ref
            out[half * lines : (half + 1) * lines] = dkv_s[m * lines : (m + 1) * lines].astype(BF)


def attend_back(meta, q, g, kv, raw, logs, start_row, heads):
    lines, stride = len(q), len(kv)
    rows, q_cols = q[0].shape
    blocks = lines * stride
    narrow = whole_block((rows, q_cols))
    half = whole_block((blocks // 2, rows, PAIR))
    return pl.pallas_call(
        functools.partial(attend_back_kernel, heads, rows, lines, stride),
        grid_spec=pltpu.PrefetchScalarGridSpec(
            num_scalar_prefetch=1,
            grid=(lines,),
            in_specs=[narrow] * (2 * lines)
            + [whole_block((lines, rows, PAIR))] * stride
            + [
                pl.BlockSpec((1, heads, rows, PAIR), lambda i, m: (i, 0, 0, 0)),
                pl.BlockSpec((1, 8, rows), lambda i, m: (i, 0, 0)),
                pl.BlockSpec((1, 1, rows), lambda i, m: (i, 0, 0)),
            ],
            out_specs=[narrow] * lines + [half] * 2,
            scratch_shapes=[
                pltpu.VMEM((lines, heads, rows, PAIR), BF),
                pltpu.VMEM((lines, heads, rows, PAIR), BF),
                pltpu.VMEM((blocks, rows, PAIR), BF),
                pltpu.VMEM((heads, rows, PAIR), F32),
                pltpu.VMEM((blocks, rows, PAIR), F32),
                pltpu.VMEM((8, rows), F32),
            ],
        ),
        out_shape=[jax.ShapeDtypeStruct((rows, q_cols), BF)] * lines
        + [jax.ShapeDtypeStruct((blocks // 2, rows, PAIR), BF)] * 2,
        compiler_params=pltpu.CompilerParams(vmem_limit_bytes=56 * 1024 * 1024),
        cost_estimate=pl.CostEstimate(
            flops=36 * 10 * rows * rows * PAIR * 2, bytes_accessed=10 << 20, transcendentals=36 * rows * rows
        ),
        name="attend_back",
    )(meta, *q, *g, *kv, raw, logs, start_row)


def experts_kernel(x_ref, g_ref, gate_ref, wg_ref, wu_ref, wd_ref, out_ref, back_ref, inner_ref):
    each = range(x_ref.shape[0])
    cap = x_ref.shape[1]
    gate_pre = [dot(x_ref[i], wg_ref[i]) for i in each]
    grad_expert = [(gate_ref[i] * g_ref[i].astype(F32)).astype(BF) for i in each]
    grad_act = [dot(grad_expert[i], wd_ref[i], NT) for i in each]
    up_pre = [dot(x_ref[i], wu_ref[i]) for i in each]
    sigma = [jax.nn.sigmoid(gate_pre[i]) for i in each]
    silu = [gate_pre[i] * sigma[i] for i in each]
    act = [(silu[i] * up_pre[i]).astype(BF) for i in each]
    grad_gate = [
        (grad_act[i] * up_pre[i] * sigma[i] * (1.0 + gate_pre[i] * (1.0 - sigma[i]))).astype(BF)
        for i in each
    ]
    grad_up = [(grad_act[i] * silu[i]).astype(BF) for i in each]
    for i in each:
        out = dot(act[i], wd_ref[i])
        inner = jnp.sum(out * g_ref[i].astype(F32), axis=-1, keepdims=True)
        inner_ref[i] = jnp.broadcast_to(inner, (cap, 128)).T[:8]
        out_ref[i] = (gate_ref[i] * out).astype(BF)
        back_ref[i] = (dot(grad_gate[i], wg_ref[i], NT) + dot(grad_up[i], wu_ref[i], NT)).astype(BF)


def run_experts(x, g, gate, w_gate, w_up, w_down):
    experts, cap, width = x.shape
    hidden = w_gate.shape[2]
    at_once = 2 if experts % 2 == 0 else 1

    def of(*shape):
        return pl.BlockSpec((at_once,) + shape, lambda e: (e, 0, 0))

    return pl.pallas_call(
        experts_kernel,
        grid=(experts // at_once,),
        in_specs=[
            of(cap, width),
            of(cap, width),
            of(cap, 1),
            of(width, hidden),
            of(width, hidden),
            of(hidden, width),
        ],
        out_specs=[of(cap, width), of(cap, width), of(8, cap)],
        out_shape=[
            jax.ShapeDtypeStruct((experts, cap, width), BF),
            jax.ShapeDtypeStruct((experts, cap, width), BF),
            jax.ShapeDtypeStruct((experts, 8, cap), F32),
        ],
        compiler_params=pltpu.CompilerParams(vmem_limit_bytes=56 * 1024 * 1024),
        cost_estimate=pl.CostEstimate(
            flops=experts * cap * width * hidden * 12,
            bytes_accessed=experts * width * (hidden * 6 + cap * 8),
            transcendentals=experts * cap * hidden,
        ),
        name="experts",
    )(x, g, gate, w_gate, w_up, w_down)


def weights_kernel(dp, at, a_ref, b_ref, c_ref, d_ref, keep_ref, send_ref):
    size = a_ref.shape[1] // dp
    chunk = 4
    split = b_ref.shape[1]
    odd = at[0] != 0
    for part in range(dp // chunk):
        span = slice(part * chunk * size, (part + 1) * chunk * size)
        for left, right, lanes in (
            (a_ref, b_ref, slice(0, split)),
            (c_ref, d_ref, slice(split, split + d_ref.shape[1])),
        ):
            block = dot(left[:, span], right[...], TN).astype(BF)
            for pair in range(chunk // 2):
                one = block[2 * pair * size : (2 * pair + 1) * size]
                two = block[(2 * pair + 1) * size : (2 * pair + 2) * size]
                at_pair = part * (chunk // 2) + pair
                keep_ref[at_pair, :, lanes] = jnp.where(odd, two, one)
                send_ref[at_pair, :, lanes] = jnp.where(odd, one, two)


def weight_parts(bit, a, b, c, d, dp):
    rows, width = a.shape
    columns = b.shape[1] + d.shape[1]
    out = (dp // 2, width // dp, columns)
    return pl.pallas_call(
        functools.partial(weights_kernel, dp),
        grid_spec=pltpu.PrefetchScalarGridSpec(
            num_scalar_prefetch=1,
            grid=(1,),
            in_specs=[whole_block(x.shape) for x in (a, b, c, d)],
            out_specs=[whole_block(out)] * 2,
        ),
        out_shape=[jax.ShapeDtypeStruct(out, BF)] * 2,
        compiler_params=pltpu.CompilerParams(vmem_limit_bytes=48 * 1024 * 1024),
        cost_estimate=pl.CostEstimate(
            flops=2 * rows * width * columns, bytes_accessed=12 << 20, transcendentals=0
        ),
        name="weights",
    )(bit[None], a, b, c, d)


def flat(x):
    return x.reshape(x.shape[0] * x.shape[1], x.shape[2])


def owner_forward_kernel(n_x, n_g, at, gate_ref, wg_ref, wu_ref, wd_ref, *refs):
    x_refs, g_refs, outs = refs[:n_x], refs[n_x : n_x + n_g], refs[n_x + n_g :]
    act_ref, grad_gate_ref, grad_up_ref = outs

    def span(i, ref):
        return pl.ds(pl.multiple_of(at[1 + i], ref.shape[2]), ref.shape[2])

    gate_pre = sum(dot(flat(x[...]), wg_ref[0, span(i, x), :]) for i, x in enumerate(x_refs))
    up_pre = sum(dot(flat(x[...]), wu_ref[0, span(i, x), :]) for i, x in enumerate(x_refs))
    grad_act = sum(
        dot(
            (gate_ref[...] * flat(g[...]).astype(F32)).astype(BF),
            wd_ref[0, :, span(n_x + i, g)],
            NT,
        )
        for i, g in enumerate(g_refs)
    )
    sigma = jax.nn.sigmoid(gate_pre)
    silu = gate_pre * sigma
    act_ref[...] = (silu * up_pre).astype(BF)
    grad_gate_ref[...] = (
        grad_act * up_pre * sigma * (1.0 + gate_pre * (1.0 - sigma))
    ).astype(BF)
    grad_up_ref[...] = (grad_act * silu).astype(BF)


def owner_grads_kernel(n_x, n_g, at, gate_ref, act_ref, grad_gate_ref, grad_up_ref, *refs):
    x_refs, g_refs, outs = refs[:n_x], refs[n_x : n_x + n_g], refs[n_x + n_g :]
    gate_out, up_out, down_out = outs

    def span(i, ref):
        return pl.ds(pl.multiple_of(at[1 + i], ref.shape[2]), ref.shape[2])

    @pl.when(pl.program_id(0) == 0)
    def _():
        for out in outs:
            out[...] = jnp.zeros_like(out)

    for i, ref in enumerate(x_refs):
        x = flat(ref[...])
        gate_out[0, span(i, ref), :] += dot(x, grad_gate_ref[...], TN)
        up_out[0, span(i, ref), :] += dot(x, grad_up_ref[...], TN)
    for i, ref in enumerate(g_refs):
        grad_expert = (gate_ref[...] * flat(ref[...]).astype(F32)).astype(BF)
        down_out[0, :, span(n_x + i, ref)] += dot(act_ref[...], grad_expert, TN)


def owner_call(kernel, name, at, gate, given, x, g, weights, outs, steps):
    dp, cap, _ = x[0].shape
    rows = dp * cap // steps

    def rowwise(a):
        return pl.BlockSpec((rows, a.shape[1]), lambda i, m: (i, 0))

    def piece(a):
        return pl.BlockSpec((dp // steps, cap, a.shape[2]), lambda i, m: (i, 0, 0))

    def weight(a):
        return pl.BlockSpec((1,) + a.shape[1:], lambda i, m: (m[0], 0, 0))

    out_specs = [rowwise(o) if len(o.shape) == 2 else whole_block(o.shape) for o in outs]
    return pl.pallas_call(
        functools.partial(kernel, len(x), len(g)),
        grid_spec=pltpu.PrefetchScalarGridSpec(
            num_scalar_prefetch=1,
            grid=(steps,),
            in_specs=[rowwise(gate)]
            + [rowwise(a) for a in given]
            + [weight(w) for w in weights]
            + [piece(a) for a in list(x) + list(g)],
            out_specs=out_specs,
        ),
        out_shape=outs,
        compiler_params=pltpu.CompilerParams(vmem_limit_bytes=58 * 1024 * 1024),
        cost_estimate=pl.CostEstimate(flops=10 << 30, bytes_accessed=24 << 20, transcendentals=1 << 20),
        name=name,
    )(at, gate, *given, *weights, *x, *g)


def shards(
    layer_in,
    norm1_gain,
    w_query,
    w_key,
    w_value,
    w_out,
    norm2_gain,
    router,
    w_gate,
    w_up,
    w_down,
    segments,
    routes,
    out_grad,
):
    rows, width = layer_in.shape
    kv_heads = w_key.shape[1] // HD
    group = w_query.shape[1] // HD // kv_heads
    q_cols = group * HD
    experts = w_gate.shape[0]
    dp = lax.axis_size("dp")
    place = lax.axis_index("dp")
    tensor_size = lax.axis_size("tensor")
    tensor_at = lax.axis_index("tensor")
    lines = kv_heads
    stride = dp // lines
    line = place >> (stride.bit_length() - 1)
    part = rows // tensor_size
    first = tensor_at * part
    held = experts // dp
    cols = width // tensor_size
    first_col = tensor_at * cols

    names = jnp.arange(experts, dtype=jnp.int32)
    named = jnp.any(routes[:, :, None] == names[None, None, :], axis=1)
    earlier = jnp.tril(jnp.ones((rows, rows), BF), -1)
    slots = jnp.where(named, dot(earlier, named.astype(BF)).astype(jnp.int32), -1)
    in_slot = slots.T[:, None, :] == jnp.arange(CAP, dtype=jnp.int32)[None, :, None]
    to_slots = in_slot.astype(BF).reshape(experts * CAP, rows)
    from_slots = (
        (slots[:, :, None] == jnp.arange(CAP, dtype=jnp.int32)[None, None, :])
        .astype(BF)
        .reshape(rows, experts * CAP)
    )

    def to_experts(x):
        return dot(to_slots, x).astype(BF).reshape(experts, CAP, -1)

    def half(x, i):
        size = cols // 2
        return to_experts(lax.dynamic_slice_in_dim(x, tensor_at * cols + i * size, size, 1))

    q_blocks = place ^ (jnp.arange(lines, dtype=jnp.int32) * stride)
    seg_query = jnp.stack(
        [lax.dynamic_slice_in_dim(segments, q_blocks[s] * rows, rows, 0) for s in range(lines)]
    )
    documents = jnp.arange(DOCS, dtype=jnp.int32)
    lengths_before = jnp.sum(
        (segments[None, :] < documents[:, None]).astype(jnp.int32), axis=1
    )
    starts = jnp.sum(
        jnp.where(seg_query[None] == documents[:, None, None], lengths_before[:, None, None], 0),
        axis=0,
    )
    shift = rows.bit_length() - 1
    meta = jnp.concatenate(
        [place[None], q_blocks, starts[:, 0] >> shift, (starts[:, -1] + rows - 1) >> shift]
    ).astype(jnp.int32)

    normed_in, kv_mine, q_mine = project(line, layer_in, norm1_gain, w_query, w_key, w_value, lines)

    def to_lines(blocks):
        return [b if s == 0 else across(b, "dp", s * stride) for s, b in enumerate(blocks)]

    kv = [jnp.stack(to_lines(kv_mine))]
    q = to_lines(q_mine)
    for bit in reversed(bits_of(stride)):
        kv = [piece for one in kv for piece in (one, across(one, "dp", bit))]
    g_sent, (kv, q, starts, meta) = after([half(out_grad, i) for i in range(2)], (kv, q, starts, meta))
    g_first = to_owner(g_sent[0])
    *mixed_far, raw, logs = attend(meta, q, kv, starts[:, None, :], group)
    mixed_far, g_first = after(mixed_far, g_first)

    def from_lines(blocks):
        return xor_blocks(to_lines(blocks), line)

    mixed = jnp.concatenate(from_lines(mixed_far), 1)
    g_late, (mixed, g_slots) = after(g_sent[1], (mixed, to_experts(out_grad)))
    g_second = to_owner(g_late)
    attn = scatter_tensor(dot(mixed, w_out))
    hidden = lax.dynamic_slice_in_dim(layer_in, first, part, 0).astype(F32) + attn
    factor_two = norm_factor(hidden)
    unit_two = hidden * factor_two
    normed_mid = gather_tensor((unit_two * norm2_gain).astype(BF), 0)

    logits = dot(normed_mid, router)
    peak = jnp.max(jnp.where(named, logits, -jnp.inf), axis=1, keepdims=True)
    expo = jnp.where(named, jnp.exp(jnp.where(named, logits - peak, 0.0)), 0.0)
    gates = expo / jnp.sum(expo, axis=1, keepdims=True)
    slot_gate = jnp.sum(jnp.where(in_slot, gates.T[:, None, :], 0.0), axis=-1)

    x_slots = to_experts(normed_mid)
    x_mine = lax.dynamic_slice_in_dim(x_slots, first_col, cols, 2)
    x_early, x_late = x_mine[..., : cols // 2], x_mine[..., cols // 2 :]
    x_early, g_second = after(x_early, g_second)
    x_first = to_owner(x_early)
    gate_high = lax.reduce_precision(slot_gate, 8, 7)
    gate_mid = lax.reduce_precision(slot_gate - gate_high, 8, 7)
    gate_pieces = jnp.stack([gate_high, gate_mid, slot_gate - gate_high - gate_mid], 2)
    g_first, x_slots = after(g_first, x_slots)
    g_first = swap_tensor(g_first, 2)

    out_slots, back_slots, inner_slots = run_experts(
        x_slots, g_slots, slot_gate[:, :, None], w_gate, w_up, w_down
    )
    back_slots, (x_first, g_first) = after(back_slots, (x_first, g_first))
    moe_part = dot(from_slots, out_slots.reshape(experts * CAP, width))
    grad_gates = jnp.sum(
        jnp.where(
            slots[:, :, None] == jnp.arange(CAP, dtype=jnp.int32)[None, None, :],
            inner_slots[None, :, 0, :],
            0.0,
        ),
        axis=-1,
    )
    grad_logits = gates * (grad_gates - jnp.sum(gates * grad_gates, axis=-1, keepdims=True))
    grad_mid_part = dot(from_slots, back_slots.reshape(experts * CAP, width)) + lax.dot_general(
        grad_logits, router.astype(F32), NT, precision=HIGH, preferred_element_type=F32
    )
    (x_late, gate_pieces, router_part), grad_mid_part = after(
        (x_late, gate_pieces, (grad_logits, normed_mid)), grad_mid_part
    )
    router_part = lax.dot_general(
        router_part[0], router_part[1].astype(F32), TN, precision=HIGH, preferred_element_type=F32
    )
    x_late = jnp.concatenate(
        [x_late, jnp.pad(gate_pieces.astype(BF), ((0, 0), (0, 0), (0, 125)))], 2
    )
    x_second = to_owner(x_late)
    grad_mid, moe_part = after(scatter_tensor(grad_mid_part), moe_part)
    gain_two_part = jnp.sum(grad_mid * unit_two, axis=0)
    grad_rows = lax.dynamic_slice_in_dim(out_grad, first, part, 0).astype(F32)
    grad_hidden = grad_rows + norm_back(unit_two, factor_two, norm2_gain, grad_mid)
    hidden_low = gather_tensor(grad_hidden.astype(BF), 0)
    (x_first, x_second, g_second), hidden_low = after((x_first, x_second, g_second), hidden_low)
    g_second = swap_tensor(g_second, 2)
    gate_owned = jnp.sum(x_second[..., cols // 2 : cols // 2 + 3].astype(F32), axis=2)
    x_owned = swap_tensor(jnp.concatenate([x_first, x_second[..., : cols // 2]], 2), 2)
    grad_mixed = dot(hidden_low, w_out, NT).astype(BF)
    g = to_lines(xor_blocks(columns_of(grad_mixed, lines), line))
    *dq_far, keep, send = attend_back(meta, q, g, kv, raw, logs, starts[:, None, :], group)

    dkv = (keep + across(send, "dp", 1)).reshape(stride // 2, lines, rows, PAIR)
    dkv, dq_far = after(dkv, dq_far)
    for bit in bits_of(stride)[1:]:
        view = dkv.reshape((dkv.shape[0] // 2, 2) + dkv.shape[1:])
        dkv = view[:, 0] + across(view[:, 1], "dp", bit)
    dkv, (moe_part, x_owned) = after(dkv[0], (moe_part, x_owned))
    dq = from_lines(dq_far)
    moe_rows = scatter_tensor(moe_part)
    dkv = from_lines([dkv[s] for s in range(lines)])
    w_all = jnp.concatenate([w_query, w_key, w_value], 1)
    dqkv = jnp.concatenate(dq + [b[:, :HD] for b in dkv] + [b[:, HD:] for b in dkv], 1)
    dqkv, x_owned, g_second = lax.optimization_barrier((dqkv, x_owned, g_second))
    weight_keep, weight_send = weight_parts(place & 1, normed_in, dqkv, hidden_low, mixed, dp)
    dqkv, weight_keep, weight_send = lax.optimization_barrier((dqkv, weight_keep, weight_send))
    def mine(x, e):
        return x.reshape((dp, held, CAP) + x.shape[2:])[:, e]

    def pieces_of(parts, offset):
        return [(parts[0], first_col + offset), (parts[1], cols - first_col + offset)]

    def owner_work(given):
        x_parts, g_parts = given
        size = cols // 2
        if tensor_size == 2:
            x = pieces_of(x_parts, 0)
            g = pieces_of(g_first, 0) + pieces_of(g_parts, size)
        else:
            x = [(assemble(x_parts, 2), 0)]
            both = [assemble(g_first, 2), assemble(g_parts, 2)]
            order = [each[..., t * size : (t + 1) * size] for t in range(tensor_size) for each in both]
            g = [(jnp.concatenate(order, 2), 0)]
        results = []
        for e in range(held):
            at = jnp.stack([jnp.int32(place * held + e)] + [jnp.int32(o) for _, o in x + g])
            tokens = [mine(a, e) for a, _ in x], [mine(a, e) for a, _ in g]
            gate = mine(gate_owned, e).reshape(dp * CAP, 1)
            hidden_shape = jax.ShapeDtypeStruct((dp * CAP, w_gate.shape[2]), BF)
            given_back = owner_call(
                owner_forward_kernel,
                "owner_forward",
                at,
                gate,
                [],
                *tokens,
                [w_gate, w_up, w_down],
                [hidden_shape] * 3,
                4,
            )
            results.append((at, gate, given_back, *tokens))
        return results

    def owner_grads(owned):
        shapes = [
            jax.ShapeDtypeStruct((1,) + w.shape[1:], F32) for w in (w_gate, w_up, w_down)
        ]
        grad_outs = [
            owner_call(owner_grads_kernel, "owner_grads", at, gate, given, x, g, [], shapes, 2)
            for at, gate, given, x, g in owned
        ]
        return [jnp.concatenate(each, 0) for each in zip(*grad_outs)]

    weight_grad, (owner_given, dqkv, small) = scatter_rows(
        weight_keep, weight_send, ((x_owned, g_second), dqkv, (router_part, gain_two_part))
    )
    grad_in_part = dot(dqkv, w_all, NT)
    in_float = layer_in.astype(F32)
    factor_one = norm_factor(in_float)
    gain_one_part = jnp.sum(grad_in_part * (in_float * factor_one), axis=0)
    small = total(jnp.concatenate([small[0], small[1][None], gain_one_part[None]], 0))
    gate_out, up_out, down_out = owner_grads(owner_work(owner_given))
    grad_in_rows = scatter_tensor(grad_in_part)
    layer_out = (hidden + moe_rows).astype(BF)
    ends = [0]
    for size in (lines * q_cols, lines * HD, lines * HD, lines * q_cols):
        ends.append(ends[-1] + size)
    query_out, key_out, value_out, proj_out = (
        weight_grad[:, a:b] for a, b in zip(ends[:-1], ends[1:])
    )
    proj_out = proj_out.T

    factor_rows = lax.dynamic_slice_in_dim(factor_one, first, part, 0)
    unit_rows = lax.dynamic_slice_in_dim(in_float, first, part, 0) * factor_rows
    input_grad = grad_hidden + norm_back(unit_rows, factor_rows, norm1_gain, grad_in_rows)
    gain_one_grad = small[experts + 1]
    gain_two_grad = small[experts]
    router_grad = small[:experts].T

    return (
        layer_out,
        input_grad,
        gain_one_grad,
        query_out,
        key_out,
        value_out,
        proj_out,
        gain_two_grad,
        router_grad,
        gate_out,
        up_out,
        down_out,
    )


def solution(mesh):
    in_specs = (
        P("dp", None),
        P(),
        P(None, "tensor"),
        P(None, "tensor"),
        P(None, "tensor"),
        P("tensor", None),
        P(),
        P(),
        P(None, None, "tensor"),
        P(None, None, "tensor"),
        P(None, "tensor", None),
        P(),
        P("dp", None),
        P("dp", None),
    )
    out_specs = (
        P(("dp", "tensor"), None),
        P(("dp", "tensor"), None),
        P(),
        P("dp", "tensor"),
        P("dp", "tensor"),
        P("dp", "tensor"),
        P("tensor", "dp"),
        P(),
        P(),
        P("dp", None, "tensor"),
        P("dp", None, "tensor"),
        P("dp", "tensor", None),
    )
    return jax.shard_map(shards, mesh=mesh, in_specs=in_specs, out_specs=out_specs, check_vma=False)
```

```python
import functools

import jax
import jax.numpy as jnp
from jax import lax
from jax.experimental import pallas as pl
from jax.experimental.pallas import tpu as pltpu
from jax.sharding import PartitionSpec as P

HD = 64
PAIR = 2 * HD
CAP = 128
DOCS = 8
EPS = 1e-05
HIGH = lax.Precision.HIGHEST
NEG = -1000000000.0
BF = jnp.bfloat16
F32 = jnp.float32

NT = (((1,), (1,)), ((), ()))
TN = (((0,), (0,)), ((), ()))


def dot(a, b, dims=None):
    if dims is None:
        return jnp.dot(a, b, preferred_element_type=F32)
    return lax.dot_general(a, b, dims, preferred_element_type=F32)


def across(x, axis, mask):
    n = lax.axis_size(axis)
    return lax.ppermute(x, axis, [(i, i ^ mask) for i in range(n)])


def bits_of(n):
    return [1 << k for k in range(n.bit_length() - 1)]


def after(x, y):
    return lax.optimization_barrier((x, y))


def to_owner(x):
    return lax.all_to_all(x, "dp", 0, 0, tiled=True)


def norm_factor(value):
    return lax.rsqrt(jnp.mean(value * value, axis=-1, keepdims=True) + EPS)


def norm_back(unit, factor, gain, grad):
    inner = gain * grad
    return factor * (inner - unit * jnp.mean(unit * inner, axis=-1, keepdims=True))


def total(x, axis):
    bits = bits_of(lax.axis_size(axis))

    def met(low, bit):
        return across(low, axis, bit).astype(F32)

    while bits:
        one, *bits = bits
        low = x.astype(BF)
        if bits:
            two, *bits = bits
            far, both = met(low, two), met(low, one | two)
            x = (low.astype(F32) + met(low, one)) + (far + both)
        else:
            x = low.astype(F32) + met(low, one)
    return x


def scatter_tensor(x):
    n = lax.axis_size("tensor")
    if n != 2:
        return lax.psum_scatter(x.astype(BF), "tensor", scatter_dimension=0, tiled=True).astype(F32)
    me = lax.axis_index("tensor")
    part = x.shape[0] // 2
    sent = lax.dynamic_slice_in_dim(x, (1 - me) * part, part, 0).astype(BF)
    own = lax.dynamic_slice_in_dim(x, me * part, part, 0)
    return own.astype(F32) + across(sent, "tensor", 1).astype(F32)


def swap_tensor(x, dim):
    if lax.axis_size("tensor") != 2:
        return (lax.all_gather(x, "tensor", axis=dim, tiled=True),)
    return x, across(x, "tensor", 1)


def assemble(parts, dim):
    if len(parts) == 1:
        return parts[0]
    own, other = parts
    low = lax.axis_index("tensor") == 0
    return jnp.concatenate([jnp.where(low, own, other), jnp.where(low, other, own)], dim)


def gather_tensor(x, dim):
    return assemble(swap_tensor(x, dim), dim)


def xor_blocks(blocks, index):
    for bit in bits_of(len(blocks)):
        crossed = (index & bit) != 0
        blocks = [jnp.where(crossed, blocks[s ^ bit], block) for s, block in enumerate(blocks)]
    return blocks


def columns_of(x, count):
    size = x.shape[1] // count
    return [x[:, s * size : (s + 1) * size] for s in range(count)]


def pair_sum(keep, send):
    return keep + across(send, "dp", 1)


def send_rows(x):
    n = lax.axis_size("dp")
    groups = [list(range(first, n, 2)) for first in range(2)]
    return lax.all_to_all(x, "dp", 0, 0, tiled=True, axis_index_groups=groups)


def project_kernel(lines, q_cols, at, x_ref, gain_ref, wq_ref, wk_ref, wv_ref, normed_ref, *rest):
    kv_refs, q_refs = rest[:lines], rest[lines : 2 * lines]
    kv_s, q_s = rest[2 * lines :]
    x = x_ref[...].astype(F32)
    scale = lax.rsqrt(jnp.mean(x * x, axis=-1, keepdims=True) + EPS)
    normed = (x * scale * gain_ref[...]).astype(BF)
    normed_ref[...] = normed
    key = dot(normed, wk_ref[...])
    value = dot(normed, wv_ref[...])
    query = dot(normed, wq_ref[...])
    for c in range(lines):
        pair = [key[:, c * HD : (c + 1) * HD], value[:, c * HD : (c + 1) * HD]]
        kv_s[c] = jnp.concatenate(pair, 1).astype(BF)
        q_s[c] = query[:, c * q_cols : (c + 1) * q_cols].astype(BF) * jnp.asarray(0.125, BF)
    for s in range(lines):
        kv_refs[s][...] = kv_s[s ^ at[0]]
        q_refs[s][...] = q_s[s ^ at[0]]


def project(line, x, gain, w_query, w_key, w_value, lines):
    rows, width = x.shape
    q_cols = w_query.shape[1] // lines

    def whole(*shape):
        return pl.BlockSpec(shape, lambda i, m: (0,) * len(shape))

    out = [(rows, width)] + [(rows, PAIR)] * lines + [(rows, q_cols)] * lines
    outs = pl.pallas_call(
        functools.partial(project_kernel, lines, q_cols),
        grid_spec=pltpu.PrefetchScalarGridSpec(
            num_scalar_prefetch=1,
            grid=(1,),
            in_specs=[
                whole(rows, width),
                whole(1, width),
                whole(*w_query.shape),
                whole(*w_key.shape),
                whole(*w_value.shape),
            ],
            out_specs=[whole(*shape) for shape in out],
            scratch_shapes=[
                pltpu.VMEM((lines, rows, PAIR), BF),
                pltpu.VMEM((lines, rows, q_cols), BF),
            ],
        ),
        out_shape=[jax.ShapeDtypeStruct(shape, BF) for shape in out],
        compiler_params=pltpu.CompilerParams(vmem_limit_bytes=48 * 1024 * 1024),
        cost_estimate=pl.CostEstimate(
            flops=2 * rows * width * (w_query.shape[1] + 2 * w_key.shape[1]),
            bytes_accessed=8 << 20,
            transcendentals=0,
        ),
        name="project",
    )(line[None], x, gain[None], w_query, w_key, w_value)
    return outs[0], outs[1 : 1 + lines], outs[1 + lines :]


def spread_heads(refs, out, heads, high):
    for s, ref in enumerate(refs):
        x = ref[...]
        zero = jnp.zeros((x.shape[0], HD), BF)
        for h in range(heads):
            one = x[:, h * HD : (h + 1) * HD]
            out[s, h] = jnp.concatenate([zero, one] if high else [one, zero], 1)


def gather_blocks(refs, out, lines):
    for m, ref in enumerate(refs):
        out[m * lines : (m + 1) * lines] = ref[...]


def position(meta, lines):
    slot = pl.program_id(0)
    return slot, meta[0], meta[1 + slot], meta[1 + lines + slot], meta[1 + 2 * lines + slot]


def walk(low, clear, own, step):
    def body(blk, carry):
        full = (blk >= clear) & (blk < own)

        @pl.when(full)
        def _():
            step(blk, False)

        @pl.when(jnp.logical_not(full))
        def _():
            step(blk, True)

        return carry

    lax.fori_loop(low, own + 1, body, 0)


def visible(blk, own, rows, start):
    key_pos = lax.broadcasted_iota(jnp.int32, (rows, rows), 0) + blk * rows
    q_pos = lax.broadcasted_iota(jnp.int32, (rows, rows), 1) + own * rows
    return (key_pos >= start) & (key_pos <= q_pos)


def attend_kernel(heads, rows, lines, stride, meta, *refs):
    q_refs, kv_refs, start_ref = refs[:lines], refs[lines : lines + stride], refs[lines + stride]
    outs = refs[lines + stride + 1 :]
    mixed_refs, (raw_ref, log_ref, q_s, kv_s, m_s, l_s, acc_s) = outs[:lines], outs[lines:]
    slot, place, own, low, clear = position(meta, lines)

    @pl.when(slot == 0)
    def _():
        spread_heads(q_refs, q_s, heads, False)
        gather_blocks(kv_refs, kv_s, lines)

    m_s[...] = jnp.full_like(m_s, -3e38)
    l_s[...] = jnp.zeros_like(l_s)
    acc_s[...] = jnp.zeros_like(acc_s)

    def step(blk, masked):
        x = blk ^ place
        kv = kv_s[(x % stride) * lines + x // stride]
        if masked:
            seen = visible(blk, own, rows, start_ref[0])
        for h in range(heads):
            s = dot(kv, q_s[slot, h], NT)
            if masked:
                s = jnp.where(seen, s, NEG)
            m_old = m_s[h : h + 1, :]
            m_new = jnp.maximum(m_old, jnp.max(s, axis=0, keepdims=True))
            p = jnp.exp(s - m_new)
            alpha = jnp.exp(m_old - m_new)
            l_s[h : h + 1, :] = l_s[h : h + 1, :] * alpha + jnp.sum(p, axis=0, keepdims=True)
            acc_s[h] = acc_s[h] * alpha + dot(kv, p.astype(BF), TN)
            m_s[h : h + 1, :] = m_new

    walk(low, clear, own, step)
    parts = []
    for h in range(heads):
        out = (acc_s[h] / l_s[h : h + 1, :]).T
        raw_ref[0, h] = out
        parts.append(out[:, HD:])
    log_ref[0] = m_s[...] + jnp.log(l_s[...])
    mixed = jnp.concatenate(parts, 1).astype(BF)
    for s in range(lines):

        @pl.when(slot == s)
        def _(s=s):
            mixed_refs[s][...] = mixed


def whole_block(shape):
    return pl.BlockSpec(shape, lambda i, m: (0,) * len(shape))


def attend(meta, q, kv, start_row, heads):
    lines, stride = len(q), len(kv)
    rows, q_cols = q[0].shape
    narrow = whole_block((rows, q_cols))
    return pl.pallas_call(
        functools.partial(attend_kernel, heads, rows, lines, stride),
        grid_spec=pltpu.PrefetchScalarGridSpec(
            num_scalar_prefetch=1,
            grid=(lines,),
            in_specs=[narrow] * lines
            + [whole_block((lines, rows, PAIR))] * stride
            + [pl.BlockSpec((1, 1, rows), lambda i, m: (i, 0, 0))],
            out_specs=[narrow] * lines
            + [
                pl.BlockSpec((1, heads, rows, PAIR), lambda i, m: (i, 0, 0, 0)),
                pl.BlockSpec((1, 8, rows), lambda i, m: (i, 0, 0)),
            ],
            scratch_shapes=[
                pltpu.VMEM((lines, heads, rows, PAIR), BF),
                pltpu.VMEM((stride * lines, rows, PAIR), BF),
                pltpu.VMEM((8, rows), F32),
                pltpu.VMEM((8, rows), F32),
                pltpu.VMEM((heads, PAIR, rows), F32),
            ],
        ),
        out_shape=[jax.ShapeDtypeStruct((rows, q_cols), BF)] * lines
        + [
            jax.ShapeDtypeStruct((lines, heads, rows, PAIR), F32),
            jax.ShapeDtypeStruct((lines, 8, rows), F32),
        ],
        compiler_params=pltpu.CompilerParams(vmem_limit_bytes=48 * 1024 * 1024),
        cost_estimate=pl.CostEstimate(
            flops=36 * 4 * rows * rows * PAIR * 2, bytes_accessed=8 << 20, transcendentals=36 * rows * rows
        ),
        name="attend",
    )(meta, *q, *kv, start_row)


def attend_back_kernel(heads, rows, lines, stride, meta, *refs):
    q_refs, g_ref, kv_refs = refs[:lines], refs[lines], refs[lines + 1 : lines + 1 + stride]
    raw_ref, log_ref, start_ref = refs[lines + 1 + stride : lines + stride + 4]
    outs = refs[lines + stride + 4 :]
    dq_refs, (keep_ref, send_ref, q_s, g_s, kv_s, dq_s, dkv_s, delta_s) = outs[:lines], outs[lines:]
    slot, place, own, low, clear = position(meta, lines)

    @pl.when(slot == 0)
    def _():
        spread_heads(q_refs, q_s, heads, False)
        spread_heads([g_ref.at[s ^ (place // stride)] for s in range(lines)], g_s, heads, True)
        gather_blocks(kv_refs, kv_s, lines)
        dkv_s[...] = jnp.zeros_like(dkv_s)

    dq_s[...] = jnp.zeros_like(dq_s)
    for h in range(heads):
        prod = raw_ref[0, h] * g_s[slot, h].astype(F32)
        delta_s[h : h + 1, :] = jnp.sum(prod.T, axis=0, keepdims=True)

    def step(blk, masked):
        x = blk ^ place
        index = (x % stride) * lines + x // stride
        kv = kv_s[index]
        if masked:
            seen = visible(blk, own, rows, start_ref[0])
        for h in range(heads):
            q = q_s[slot, h]
            g = g_s[slot, h]
            s = dot(kv, q, NT)
            if masked:
                s = jnp.where(seen, s, NEG)
            p = jnp.exp(s - log_ref[0, h : h + 1, :])
            gp = dot(kv, g, NT)
            gs = (p * (gp - delta_s[h : h + 1, :])).astype(BF)
            part = dot(gs, q) + dot(p.astype(BF), g)
            dkv_s[index] += part
            dq_s[h] += dot(gs, kv, TN)

    walk(low, clear, own, step)
    dq = jnp.concatenate([dq_s[h][:, :HD] * 0.125 for h in range(heads)], 1).astype(BF)
    for s in range(lines):

        @pl.when(slot == s)
        def _(s=s):
            dq_refs[s][...] = dq

    @pl.when(slot == lines - 1)
    def _():
        for m in range(stride):
            half = m // 2
            out = send_ref if m % 2 else keep_ref
            out[half * lines : (half + 1) * lines] = dkv_s[m * lines : (m + 1) * lines].astype(BF)


def attend_back(meta, q, g, kv, raw, logs, start_row, heads):
    lines, stride = len(q), len(kv)
    rows, q_cols = q[0].shape
    blocks = lines * stride
    narrow = whole_block((rows, q_cols))
    half = whole_block((blocks // 2, rows, PAIR))
    return pl.pallas_call(
        functools.partial(attend_back_kernel, heads, rows, lines, stride),
        grid_spec=pltpu.PrefetchScalarGridSpec(
            num_scalar_prefetch=1,
            grid=(lines,),
            in_specs=[narrow] * lines
            + [whole_block((lines, rows, q_cols))]
            + [whole_block((lines, rows, PAIR))] * stride
            + [
                pl.BlockSpec((1, heads, rows, PAIR), lambda i, m: (i, 0, 0, 0)),
                pl.BlockSpec((1, 8, rows), lambda i, m: (i, 0, 0)),
                pl.BlockSpec((1, 1, rows), lambda i, m: (i, 0, 0)),
            ],
            out_specs=[narrow] * lines + [half] * 2,
            scratch_shapes=[
                pltpu.VMEM((lines, heads, rows, PAIR), BF),
                pltpu.VMEM((lines, heads, rows, PAIR), BF),
                pltpu.VMEM((blocks, rows, PAIR), BF),
                pltpu.VMEM((heads, rows, PAIR), F32),
                pltpu.VMEM((blocks, rows, PAIR), F32),
                pltpu.VMEM((8, rows), F32),
            ],
        ),
        out_shape=[jax.ShapeDtypeStruct((rows, q_cols), BF)] * lines
        + [jax.ShapeDtypeStruct((blocks // 2, rows, PAIR), BF)] * 2,
        compiler_params=pltpu.CompilerParams(vmem_limit_bytes=56 * 1024 * 1024),
        cost_estimate=pl.CostEstimate(
            flops=36 * 10 * rows * rows * PAIR * 2, bytes_accessed=10 << 20, transcendentals=36 * rows * rows
        ),
        name="attend_back",
    )(meta, *q, g, *kv, raw, logs, start_row)


def experts_kernel(x_ref, g_ref, gate_ref, wg_ref, wu_ref, wd_ref, out_ref, back_ref, inner_ref):
    each = range(x_ref.shape[0])
    cap = x_ref.shape[1]
    gate_pre = [dot(x_ref[i], wg_ref[i]) for i in each]
    grad_expert = [(gate_ref[i] * g_ref[i].astype(F32)).astype(BF) for i in each]
    grad_act = [dot(grad_expert[i], wd_ref[i], NT) for i in each]
    up_pre = [dot(x_ref[i], wu_ref[i]) for i in each]
    sigma = [jax.nn.sigmoid(gate_pre[i]) for i in each]
    silu = [gate_pre[i] * sigma[i] for i in each]
    act = [(silu[i] * up_pre[i]).astype(BF) for i in each]
    grad_gate = [
        (grad_act[i] * up_pre[i] * sigma[i] * (1.0 + gate_pre[i] * (1.0 - sigma[i]))).astype(BF)
        for i in each
    ]
    grad_up = [(grad_act[i] * silu[i]).astype(BF) for i in each]
    for i in each:
        out = dot(act[i], wd_ref[i])
        inner = jnp.sum(out * g_ref[i].astype(F32), axis=-1, keepdims=True)
        inner_ref[i] = jnp.broadcast_to(inner, (cap, 128)).T[:8]
        out_ref[i] = (gate_ref[i] * out).astype(BF)
        back_ref[i] = (dot(grad_gate[i], wg_ref[i], NT) + dot(grad_up[i], wu_ref[i], NT)).astype(BF)


def run_experts(x, g, gate, w_gate, w_up, w_down):
    experts, cap, width = x.shape
    hidden = w_gate.shape[2]
    at_once = 2 if experts % 2 == 0 else 1

    def of(*shape):
        return pl.BlockSpec((at_once,) + shape, lambda e: (e, 0, 0))

    return pl.pallas_call(
        experts_kernel,
        grid=(experts // at_once,),
        in_specs=[
            of(cap, width),
            of(cap, width),
            of(cap, 1),
            of(width, hidden),
            of(width, hidden),
            of(hidden, width),
        ],
        out_specs=[of(cap, width), of(cap, width), of(8, cap)],
        out_shape=[
            jax.ShapeDtypeStruct((experts, cap, width), BF),
            jax.ShapeDtypeStruct((experts, cap, width), BF),
            jax.ShapeDtypeStruct((experts, 8, cap), F32),
        ],
        compiler_params=pltpu.CompilerParams(vmem_limit_bytes=56 * 1024 * 1024),
        cost_estimate=pl.CostEstimate(
            flops=experts * cap * width * hidden * 12,
            bytes_accessed=experts * width * (hidden * 6 + cap * 8),
            transcendentals=experts * cap * hidden,
        ),
        name="experts",
    )(x, g, gate, w_gate, w_up, w_down)


def weights_kernel(dp, at, a_ref, b_ref, keep_ref, send_ref):
    size = a_ref.shape[1] // dp
    chunk = 4
    odd = at[0] != 0
    for part in range(dp // chunk):
        span = slice(part * chunk * size, (part + 1) * chunk * size)
        block = dot(a_ref[:, span], b_ref[...], TN).astype(BF)
        for pair in range(chunk // 2):
            one = block[2 * pair * size : (2 * pair + 1) * size]
            two = block[(2 * pair + 1) * size : (2 * pair + 2) * size]
            at_pair = part * (chunk // 2) + pair
            keep_ref[at_pair] = jnp.where(odd, two, one)
            send_ref[at_pair] = jnp.where(odd, one, two)


def weight_parts(bit, a, b, dp):
    rows, width = a.shape
    columns = b.shape[1]
    out = (dp // 2, width // dp, columns)
    return pl.pallas_call(
        functools.partial(weights_kernel, dp),
        grid_spec=pltpu.PrefetchScalarGridSpec(
            num_scalar_prefetch=1,
            grid=(1,),
            in_specs=[whole_block(x.shape) for x in (a, b)],
            out_specs=[whole_block(out)] * 2,
        ),
        out_shape=[jax.ShapeDtypeStruct(out, BF)] * 2,
        compiler_params=pltpu.CompilerParams(vmem_limit_bytes=48 * 1024 * 1024),
        cost_estimate=pl.CostEstimate(
            flops=2 * rows * width * columns, bytes_accessed=8 << 20, transcendentals=0
        ),
        name="weights",
    )(bit[None], a, b)


def flat(x):
    return x.reshape(x.shape[0] * x.shape[1], x.shape[2])


def owner_forward_kernel(n_x, n_g, at, gate_ref, wg_ref, wu_ref, wd_ref, *refs):
    x_refs, g_refs, outs = refs[:n_x], refs[n_x : n_x + n_g], refs[n_x + n_g :]
    act_ref, grad_gate_ref, grad_up_ref = outs

    def span(i, ref):
        return pl.ds(pl.multiple_of(at[1 + i], ref.shape[2]), ref.shape[2])

    gate_pre = sum(dot(flat(x[...]), wg_ref[0, span(i, x), :]) for i, x in enumerate(x_refs))
    up_pre = sum(dot(flat(x[...]), wu_ref[0, span(i, x), :]) for i, x in enumerate(x_refs))
    grad_act = sum(
        dot(
            (gate_ref[...] * flat(g[...]).astype(F32)).astype(BF),
            wd_ref[0, :, span(n_x + i, g)],
            NT,
        )
        for i, g in enumerate(g_refs)
    )
    sigma = jax.nn.sigmoid(gate_pre)
    silu = gate_pre * sigma
    act_ref[...] = (silu * up_pre).astype(BF)
    grad_gate_ref[...] = (
        grad_act * up_pre * sigma * (1.0 + gate_pre * (1.0 - sigma))
    ).astype(BF)
    grad_up_ref[...] = (grad_act * silu).astype(BF)


def owner_grads_kernel(n_x, n_g, at, gate_ref, act_ref, grad_gate_ref, grad_up_ref, *refs):
    x_refs, g_refs, outs = refs[:n_x], refs[n_x : n_x + n_g], refs[n_x + n_g :]
    gate_out, up_out, down_out = outs

    def span(i, ref):
        return pl.ds(pl.multiple_of(at[1 + i], ref.shape[2]), ref.shape[2])

    @pl.when(pl.program_id(0) == 0)
    def _():
        for out in outs:
            out[...] = jnp.zeros_like(out)

    for i, ref in enumerate(x_refs):
        x = flat(ref[...])
        gate_out[0, span(i, ref), :] += dot(x, grad_gate_ref[...], TN)
        up_out[0, span(i, ref), :] += dot(x, grad_up_ref[...], TN)
    for i, ref in enumerate(g_refs):
        grad_expert = (gate_ref[...] * flat(ref[...]).astype(F32)).astype(BF)
        down_out[0, :, span(n_x + i, ref)] += dot(act_ref[...], grad_expert, TN)


def owner_call(kernel, name, at, gate, given, x, g, weights, outs, steps):
    dp, cap, _ = x[0].shape
    rows = dp * cap // steps

    def rowwise(a):
        return pl.BlockSpec((rows, a.shape[1]), lambda i, m: (i, 0))

    def piece(a):
        return pl.BlockSpec((dp // steps, cap, a.shape[2]), lambda i, m: (i, 0, 0))

    def weight(a):
        return pl.BlockSpec((1,) + a.shape[1:], lambda i, m: (m[0], 0, 0))

    out_specs = [rowwise(o) if len(o.shape) == 2 else whole_block(o.shape) for o in outs]
    return pl.pallas_call(
        functools.partial(kernel, len(x), len(g)),
        grid_spec=pltpu.PrefetchScalarGridSpec(
            num_scalar_prefetch=1,
            grid=(steps,),
            in_specs=[rowwise(gate)]
            + [rowwise(a) for a in given]
            + [weight(w) for w in weights]
            + [piece(a) for a in list(x) + list(g)],
            out_specs=out_specs,
        ),
        out_shape=outs,
        compiler_params=pltpu.CompilerParams(vmem_limit_bytes=58 * 1024 * 1024),
        cost_estimate=pl.CostEstimate(flops=10 << 30, bytes_accessed=24 << 20, transcendentals=1 << 20),
        name=name,
    )(at, gate, *given, *weights, *x, *g)


def shards(
    layer_in,
    norm1_gain,
    w_query,
    w_key,
    w_value,
    w_out,
    norm2_gain,
    router,
    w_gate,
    w_up,
    w_down,
    segments,
    routes,
    out_grad,
):
    rows, width = layer_in.shape
    kv_heads = w_key.shape[1] // HD
    group = w_query.shape[1] // HD // kv_heads
    q_cols = group * HD
    experts = w_gate.shape[0]
    dp = lax.axis_size("dp")
    place = lax.axis_index("dp")
    tensor_size = lax.axis_size("tensor")
    tensor_at = lax.axis_index("tensor")
    lines = kv_heads
    stride = dp // lines
    line = place >> (stride.bit_length() - 1)
    part = rows // tensor_size
    first = tensor_at * part
    held = experts // dp
    cols = width // tensor_size
    first_col = tensor_at * cols

    names = jnp.arange(experts, dtype=jnp.int32)
    named = jnp.any(routes[:, :, None] == names[None, None, :], axis=1)
    earlier = jnp.tril(jnp.ones((rows, rows), BF), -1)
    slots = jnp.where(named, dot(earlier, named.astype(BF)).astype(jnp.int32), -1)
    in_slot = slots.T[:, None, :] == jnp.arange(CAP, dtype=jnp.int32)[None, :, None]
    to_slots = in_slot.astype(BF).reshape(experts * CAP, rows)
    from_slots = (
        (slots[:, :, None] == jnp.arange(CAP, dtype=jnp.int32)[None, None, :])
        .astype(BF)
        .reshape(rows, experts * CAP)
    )

    def to_experts(x):
        return dot(to_slots, x).astype(BF).reshape(experts, CAP, -1)

    def half(x, i):
        size = cols // 2
        return to_experts(lax.dynamic_slice_in_dim(x, tensor_at * cols + i * size, size, 1))

    q_blocks = place ^ (jnp.arange(lines, dtype=jnp.int32) * stride)
    seg_query = jnp.stack(
        [lax.dynamic_slice_in_dim(segments, q_blocks[s] * rows, rows, 0) for s in range(lines)]
    )
    documents = jnp.arange(DOCS, dtype=jnp.int32)
    lengths_before = jnp.sum(
        (segments[None, :] < documents[:, None]).astype(jnp.int32), axis=1
    )
    starts = jnp.sum(
        jnp.where(seg_query[None] == documents[:, None, None], lengths_before[:, None, None], 0),
        axis=0,
    )
    shift = rows.bit_length() - 1
    meta = jnp.concatenate(
        [place[None], q_blocks, starts[:, 0] >> shift, (starts[:, -1] + rows - 1) >> shift]
    ).astype(jnp.int32)

    normed_in, kv_mine, q_mine = project(line, layer_in, norm1_gain, w_query, w_key, w_value, lines)

    def to_lines(blocks):
        return [b if s == 0 else across(b, "dp", s * stride) for s, b in enumerate(blocks)]

    kv = [jnp.stack(to_lines(kv_mine))]
    q = to_lines(q_mine)
    for bit in reversed(bits_of(stride)):
        kv = [piece for one in kv for piece in (one, across(one, "dp", bit))]
    g_sent, (kv, q, starts, meta) = after([half(out_grad, i) for i in range(2)], (kv, q, starts, meta))
    g_first = to_owner(g_sent[0])
    *mixed_far, raw, logs = attend(meta, q, kv, starts[:, None, :], group)
    mixed_far, g_first = after(mixed_far, g_first)

    def from_lines(blocks):
        return xor_blocks(to_lines(blocks), line)

    mixed = jnp.concatenate(from_lines(mixed_far), 1)
    g_late, (mixed, g_slots) = after(g_sent[1], (mixed, to_experts(out_grad)))
    g_second = to_owner(g_late)
    attn = scatter_tensor(dot(mixed, w_out))
    hidden = lax.dynamic_slice_in_dim(layer_in, first, part, 0).astype(F32) + attn
    factor_two = norm_factor(hidden)
    unit_two = hidden * factor_two
    normed_mid = gather_tensor((unit_two * norm2_gain).astype(BF), 0)
    normed_mid, g_second = after(normed_mid, g_second)

    logits = dot(normed_mid, router)
    peak = jnp.max(jnp.where(named, logits, -jnp.inf), axis=1, keepdims=True)
    expo = jnp.where(named, jnp.exp(jnp.where(named, logits - peak, 0.0)), 0.0)
    gates = expo / jnp.sum(expo, axis=1, keepdims=True)
    slot_gate = jnp.sum(jnp.where(in_slot, gates.T[:, None, :], 0.0), axis=-1)

    x_slots = to_experts(normed_mid)
    gate_high = lax.reduce_precision(slot_gate, 8, 7)
    gate_mid = lax.reduce_precision(slot_gate - gate_high, 8, 7)
    gate_pieces = jnp.stack([gate_high, gate_mid, slot_gate - gate_high - gate_mid], 2)
    x_mine = lax.dynamic_slice_in_dim(x_slots, first_col, cols, 2)
    early = cols // 2
    x_late = x_mine[..., early:]
    x_first = to_owner(x_mine[..., :early])
    g_owned = swap_tensor(jnp.concatenate([g_first, g_second], 2), 2)

    out_slots, back_slots, inner_slots = run_experts(
        x_slots, g_slots, slot_gate[:, :, None], w_gate, w_up, w_down
    )
    back_slots, (x_first, g_owned) = after(back_slots, (x_first, g_owned))
    moe_part = dot(from_slots, out_slots.reshape(experts * CAP, width))
    grad_gates = jnp.sum(
        jnp.where(
            slots[:, :, None] == jnp.arange(CAP, dtype=jnp.int32)[None, None, :],
            inner_slots[None, :, 0, :],
            0.0,
        ),
        axis=-1,
    )
    grad_logits = gates * (grad_gates - jnp.sum(gates * grad_gates, axis=-1, keepdims=True))
    grad_mid_part = dot(from_slots, back_slots.reshape(experts * CAP, width)) + lax.dot_general(
        grad_logits, router.astype(F32), NT, precision=HIGH, preferred_element_type=F32
    )
    (x_late, gate_pieces, router_part), grad_mid_part = after(
        (x_late, gate_pieces, (grad_logits, normed_mid)), grad_mid_part
    )
    x_second = to_owner(
        jnp.concatenate([x_late, jnp.pad(gate_pieces.astype(BF), ((0, 0), (0, 0), (0, 125)))], 2)
    )
    router_part = lax.dot_general(
        router_part[0], router_part[1].astype(F32), TN, precision=HIGH, preferred_element_type=F32
    )
    grad_mid, moe_part = after(scatter_tensor(grad_mid_part), moe_part)
    gain_two_part = jnp.sum(grad_mid * unit_two, axis=0)
    grad_rows = lax.dynamic_slice_in_dim(out_grad, first, part, 0).astype(F32)
    grad_hidden = grad_rows + norm_back(unit_two, factor_two, norm2_gain, grad_mid)
    hidden_low = gather_tensor(grad_hidden.astype(BF), 0)
    grad_mixed = dot(hidden_low, w_out, NT).astype(BF)
    g = jnp.stack(columns_of(grad_mixed, lines))
    g, (x_first, x_second, hidden_late) = after(g, (x_first, x_second, hidden_low))
    if lines > 1:
        groups = [[first_of + j * stride for j in range(lines)] for first_of in range(stride)]
        g = lax.all_to_all(g, "dp", 0, 0, tiled=True, axis_index_groups=groups)
    gate_owned = jnp.sum(x_second[..., cols - early : cols - early + 3].astype(F32), axis=2)
    x_owned = swap_tensor(jnp.concatenate([x_first, x_second[..., : cols - early]], 2), 2)
    proj_part = dot(hidden_late, mixed, TN).astype(BF).reshape(dp // 2, 2, width // dp, -1)
    proj_keep, proj_send = (
        lax.dynamic_index_in_dim(proj_part, (place & 1) ^ other, 1, keepdims=False)
        for other in (0, 1)
    )
    proj_got = send_rows(pair_sum(proj_keep, proj_send))
    *dq_far, keep, send = attend_back(meta, q, g, kv, raw, logs, starts[:, None, :], group)

    dkv = (keep + across(send, "dp", 1)).reshape(stride // 2, lines, rows, PAIR)
    dkv, dq_far, proj_got = lax.optimization_barrier((dkv, dq_far, proj_got))
    proj_out = jnp.sum(proj_got.astype(F32), axis=0).T
    for bit in bits_of(stride)[1:]:
        view = dkv.reshape((dkv.shape[0] // 2, 2) + dkv.shape[1:])
        dkv = view[:, 0] + across(view[:, 1], "dp", bit)
    dkv, (moe_part, x_owned, g_owned) = after(dkv[0], (moe_part, x_owned, g_owned))
    dq = from_lines(dq_far)
    dkv = from_lines([dkv[s] for s in range(lines)])
    def mine(x, e):
        return x.reshape((dp, held, CAP) + x.shape[2:])[:, e]

    def pieces_of(parts):
        return [(parts[0], first_col), (parts[1], cols - first_col)]

    def owner_work(x_parts, g_parts):
        if tensor_size == 2:
            x, g = pieces_of(x_parts), pieces_of(g_parts)
        else:
            x, g = [(assemble(x_parts, 2), 0)], [(assemble(g_parts, 2), 0)]
        results = []
        for e in range(held):
            at = jnp.stack([jnp.int32(place * held + e)] + [jnp.int32(o) for _, o in x + g])
            tokens = [mine(a, e) for a, _ in x], [mine(a, e) for a, _ in g]
            gate = mine(gate_owned, e).reshape(dp * CAP, 1)
            hidden_shape = jax.ShapeDtypeStruct((dp * CAP, w_gate.shape[2]), BF)
            given_back = owner_call(
                owner_forward_kernel,
                "owner_forward",
                at,
                gate,
                [],
                *tokens,
                [w_gate, w_up, w_down],
                [hidden_shape] * 3,
                4,
            )
            results.append((at, gate, given_back, *tokens))
        return results

    def owner_grads(owned):
        shapes = [
            jax.ShapeDtypeStruct((1,) + w.shape[1:], F32) for w in (w_gate, w_up, w_down)
        ]
        grad_outs = [
            owner_call(owner_grads_kernel, "owner_grads", at, gate, given, x, g, [], shapes, 2)
            for at, gate, given, x, g in owned
        ]
        return [jnp.concatenate(each, 0) for each in zip(*grad_outs)]

    owned = owner_work(x_owned, g_owned)
    w_all = jnp.concatenate([w_query, w_key, w_value], 1)
    dqkv = jnp.concatenate(dq + [b[:, :HD] for b in dkv] + [b[:, HD:] for b in dkv], 1)
    in_float = layer_in.astype(F32)
    factor_one = norm_factor(in_float)
    unit_one = in_float * factor_one
    dqkv, (owned, moe_rows, unit_one) = after(dqkv, (owned, scatter_tensor(moe_part), unit_one))
    grad_in_part = dot(dqkv, w_all, NT)
    gain_one_part = jnp.sum(grad_in_part * unit_one, axis=0)
    small = jnp.concatenate([router_part, gain_two_part[None], gain_one_part[None]], 0)
    small = total(small.reshape(-1, 128), "dp")
    weight_keep, weight_send = weight_parts(place & 1, normed_in, dqkv, dp)
    weight_pair, (owned, small, grad_in_part) = after(
        pair_sum(weight_keep, weight_send), (owned, small, grad_in_part)
    )
    small = total(small, "tensor")
    (gate_out, up_out, down_out), small, weight_got, grad_in_rows = lax.optimization_barrier(
        (owner_grads(owned), small, send_rows(weight_pair), scatter_tensor(grad_in_part))
    )
    weight_grad = jnp.sum(weight_got.astype(F32), axis=0)
    layer_out = (hidden + moe_rows).astype(BF)
    ends = [0]
    for size in (lines * q_cols, lines * HD, lines * HD):
        ends.append(ends[-1] + size)
    query_out, key_out, value_out = (weight_grad[:, a:b] for a, b in zip(ends[:-1], ends[1:]))

    factor_rows = lax.dynamic_slice_in_dim(factor_one, first, part, 0)
    unit_rows = lax.dynamic_slice_in_dim(in_float, first, part, 0) * factor_rows
    input_grad = grad_hidden + norm_back(unit_rows, factor_rows, norm1_gain, grad_in_rows)
    small = small.reshape(-1, width)
    gain_one_grad = small[experts + 1]
    gain_two_grad = small[experts]
    router_grad = small[:experts].T

    return (
        layer_out,
        input_grad,
        gain_one_grad,
        query_out,
        key_out,
        value_out,
        proj_out,
        gain_two_grad,
        router_grad,
        gate_out,
        up_out,
        down_out,
    )


def solution(mesh):
    in_specs = (
        P("dp", None),
        P(),
        P(None, "tensor"),
        P(None, "tensor"),
        P(None, "tensor"),
        P("tensor", None),
        P(),
        P(),
        P(None, None, "tensor"),
        P(None, None, "tensor"),
        P(None, "tensor", None),
        P(),
        P("dp", None),
        P("dp", None),
    )
    out_specs = (
        P(("dp", "tensor"), None),
        P(("dp", "tensor"), None),
        P(),
        P("dp", "tensor"),
        P("dp", "tensor"),
        P("dp", "tensor"),
        P("tensor", "dp"),
        P(),
        P(),
        P("dp", None, "tensor"),
        P("dp", None, "tensor"),
        P("dp", "tensor", None),
    )
    return jax.shard_map(shards, mesh=mesh, in_specs=in_specs, out_specs=out_specs, check_vma=False)
```

```python
import functools

import jax
import jax.numpy as jnp
from jax import lax
from jax.experimental import pallas as pl
from jax.experimental.pallas import tpu as pltpu
from jax.sharding import PartitionSpec as P

HD = 64
PAIR = 2 * HD
CAP = 128
DOCS = 8
EPS = 1e-05
HIGH = lax.Precision.HIGHEST
NEG = -1000000000.0
BF = jnp.bfloat16
F32 = jnp.float32

NT = (((1,), (1,)), ((), ()))
TN = (((0,), (0,)), ((), ()))


def dot(a, b, dims=None):
    if dims is None:
        return jnp.dot(a, b, preferred_element_type=F32)
    return lax.dot_general(a, b, dims, preferred_element_type=F32)


def across(x, axis, mask):
    n = lax.axis_size(axis)
    return lax.ppermute(x, axis, [(i, i ^ mask) for i in range(n)])


def bits_of(n):
    return [1 << k for k in range(n.bit_length() - 1)]


def after(x, y):
    return lax.optimization_barrier((x, y))


def to_owner(x):
    return lax.all_to_all(x, "dp", 0, 0, tiled=True)


def norm_factor(value):
    return lax.rsqrt(jnp.mean(value * value, axis=-1, keepdims=True) + EPS)


def norm_back(unit, factor, gain, grad):
    inner = gain * grad
    return factor * (inner - unit * jnp.mean(unit * inner, axis=-1, keepdims=True))


def total(x, axis):
    bits = bits_of(lax.axis_size(axis))

    def met(low, bit):
        return across(low, axis, bit).astype(F32)

    while bits:
        one, *bits = bits
        low = x.astype(BF)
        if bits:
            two, *bits = bits
            far, both = met(low, two), met(low, one | two)
            x = (low.astype(F32) + met(low, one)) + (far + both)
        else:
            x = low.astype(F32) + met(low, one)
    return x


def scatter_tensor(x):
    n = lax.axis_size("tensor")
    if n != 2:
        return lax.psum_scatter(x.astype(BF), "tensor", scatter_dimension=0, tiled=True).astype(F32)
    me = lax.axis_index("tensor")
    part = x.shape[0] // 2
    sent = lax.dynamic_slice_in_dim(x, (1 - me) * part, part, 0).astype(BF)
    own = lax.dynamic_slice_in_dim(x, me * part, part, 0)
    return own.astype(F32) + across(sent, "tensor", 1).astype(F32)


def swap_tensor(x, dim):
    if lax.axis_size("tensor") != 2:
        return (lax.all_gather(x, "tensor", axis=dim, tiled=True),)
    return x, across(x, "tensor", 1)


def assemble(parts, dim):
    if len(parts) == 1:
        return parts[0]
    own, other = parts
    low = lax.axis_index("tensor") == 0
    return jnp.concatenate([jnp.where(low, own, other), jnp.where(low, other, own)], dim)


def gather_tensor(x, dim):
    return assemble(swap_tensor(x, dim), dim)


def xor_blocks(blocks, index):
    for bit in bits_of(len(blocks)):
        crossed = (index & bit) != 0
        blocks = [jnp.where(crossed, blocks[s ^ bit], block) for s, block in enumerate(blocks)]
    return blocks


def columns_of(x, count):
    size = x.shape[1] // count
    return [x[:, s * size : (s + 1) * size] for s in range(count)]


def pair_sum(keep, send):
    return keep + across(send, "dp", 1)


def send_rows(x):
    n = lax.axis_size("dp")
    groups = [list(range(first, n, 2)) for first in range(2)]
    return lax.all_to_all(x, "dp", 0, 0, tiled=True, axis_index_groups=groups)


def project_kernel(lines, q_cols, at, x_ref, gain_ref, wq_ref, wk_ref, wv_ref, normed_ref, *rest):
    kv_refs, q_refs = rest[:lines], rest[lines : 2 * lines]
    kv_s, q_s = rest[2 * lines :]
    x = x_ref[...].astype(F32)
    scale = lax.rsqrt(jnp.mean(x * x, axis=-1, keepdims=True) + EPS)
    normed = (x * scale * gain_ref[...]).astype(BF)
    normed_ref[...] = normed
    key = dot(normed, wk_ref[...])
    value = dot(normed, wv_ref[...])
    query = dot(normed, wq_ref[...])
    for c in range(lines):
        pair = [key[:, c * HD : (c + 1) * HD], value[:, c * HD : (c + 1) * HD]]
        kv_s[c] = jnp.concatenate(pair, 1).astype(BF)
        q_s[c] = query[:, c * q_cols : (c + 1) * q_cols].astype(BF) * jnp.asarray(0.125, BF)
    for s in range(lines):
        kv_refs[s][...] = kv_s[s ^ at[0]]
        q_refs[s][...] = q_s[s ^ at[0]]


def project(line, x, gain, w_query, w_key, w_value, lines):
    rows, width = x.shape
    q_cols = w_query.shape[1] // lines

    def whole(*shape):
        return pl.BlockSpec(shape, lambda i, m: (0,) * len(shape))

    out = [(rows, width)] + [(rows, PAIR)] * lines + [(rows, q_cols)] * lines
    outs = pl.pallas_call(
        functools.partial(project_kernel, lines, q_cols),
        grid_spec=pltpu.PrefetchScalarGridSpec(
            num_scalar_prefetch=1,
            grid=(1,),
            in_specs=[
                whole(rows, width),
                whole(1, width),
                whole(*w_query.shape),
                whole(*w_key.shape),
                whole(*w_value.shape),
            ],
            out_specs=[whole(*shape) for shape in out],
            scratch_shapes=[
                pltpu.VMEM((lines, rows, PAIR), BF),
                pltpu.VMEM((lines, rows, q_cols), BF),
            ],
        ),
        out_shape=[jax.ShapeDtypeStruct(shape, BF) for shape in out],
        compiler_params=pltpu.CompilerParams(vmem_limit_bytes=48 * 1024 * 1024),
        cost_estimate=pl.CostEstimate(
            flops=2 * rows * width * (w_query.shape[1] + 2 * w_key.shape[1]),
            bytes_accessed=8 << 20,
            transcendentals=0,
        ),
        name="project",
    )(line[None], x, gain[None], w_query, w_key, w_value)
    return outs[0], outs[1 : 1 + lines], outs[1 + lines :]


def spread_heads(refs, out, heads, high):
    for s, ref in enumerate(refs):
        x = ref[...]
        zero = jnp.zeros((x.shape[0], HD), BF)
        for h in range(heads):
            one = x[:, h * HD : (h + 1) * HD]
            out[s, h] = jnp.concatenate([zero, one] if high else [one, zero], 1)


def gather_blocks(refs, out, lines):
    for m, ref in enumerate(refs):
        out[m * lines : (m + 1) * lines] = ref[...]


def position(meta, lines):
    slot = pl.program_id(0)
    return slot, meta[0], meta[1 + slot], meta[1 + lines + slot], meta[1 + 2 * lines + slot]


def walk(low, clear, own, step):
    def body(blk, carry):
        full = (blk >= clear) & (blk < own)

        @pl.when(full)
        def _():
            step(blk, False)

        @pl.when(jnp.logical_not(full))
        def _():
            step(blk, True)

        return carry

    lax.fori_loop(low, own + 1, body, 0)


def visible(blk, own, rows, start):
    key_pos = lax.broadcasted_iota(jnp.int32, (rows, rows), 0) + blk * rows
    q_pos = lax.broadcasted_iota(jnp.int32, (rows, rows), 1) + own * rows
    return (key_pos >= start) & (key_pos <= q_pos)


def attend_kernel(heads, rows, lines, stride, meta, *refs):
    q_refs, kv_refs, start_ref = refs[:lines], refs[lines : lines + stride], refs[lines + stride]
    outs = refs[lines + stride + 1 :]
    mixed_refs, (raw_ref, log_ref, q_s, kv_s, m_s, l_s, acc_s) = outs[:lines], outs[lines:]
    slot, place, own, low, clear = position(meta, lines)

    @pl.when(slot == 0)
    def _():
        spread_heads(q_refs, q_s, heads, False)
        gather_blocks(kv_refs, kv_s, lines)

    m_s[...] = jnp.full_like(m_s, -3e38)
    l_s[...] = jnp.zeros_like(l_s)
    acc_s[...] = jnp.zeros_like(acc_s)

    def step(blk, masked):
        x = blk ^ place
        index = (x % stride) * lines + x // stride
        kv = kv_s[index]
        if masked:
            seen = visible(blk, own, rows, start_ref[0])
        each = range(heads)
        scores = [dot(kv, q_s[slot, h], NT) for h in each]
        if masked:
            scores = [jnp.where(seen, s, NEG) for s in scores]
        m_old = [m_s[h : h + 1, :] for h in each]
        m_new = [jnp.maximum(m_old[h], jnp.max(scores[h], axis=0, keepdims=True)) for h in each]
        p = [jnp.exp(scores[h] - m_new[h]) for h in each]
        alpha = [jnp.exp(m_old[h] - m_new[h]) for h in each]
        added = [dot(kv, p[h].astype(BF), TN) for h in each]
        for h in each:
            l_s[h : h + 1, :] = l_s[h : h + 1, :] * alpha[h] + jnp.sum(p[h], axis=0, keepdims=True)
            acc_s[h] = acc_s[h] * alpha[h] + added[h]
            m_s[h : h + 1, :] = m_new[h]

    walk(low, clear, own, step)
    parts = []
    for h in range(heads):
        out = (acc_s[h] / l_s[h : h + 1, :]).T
        raw_ref[0, h] = out
        parts.append(out[:, HD:])
    log_ref[0] = m_s[...] + jnp.log(l_s[...])
    mixed = jnp.concatenate(parts, 1).astype(BF)
    for s in range(lines):

        @pl.when(slot == s)
        def _(s=s):
            mixed_refs[s][...] = mixed


def whole_block(shape):
    return pl.BlockSpec(shape, lambda i, m: (0,) * len(shape))


def attend(meta, q, kv, start_row, heads):
    lines, stride = len(q), len(kv)
    rows, q_cols = q[0].shape
    narrow = whole_block((rows, q_cols))
    return pl.pallas_call(
        functools.partial(attend_kernel, heads, rows, lines, stride),
        grid_spec=pltpu.PrefetchScalarGridSpec(
            num_scalar_prefetch=1,
            grid=(lines,),
            in_specs=[narrow] * lines
            + [whole_block((lines, rows, PAIR))] * stride
            + [pl.BlockSpec((1, 1, rows), lambda i, m: (i, 0, 0))],
            out_specs=[narrow] * lines
            + [
                pl.BlockSpec((1, heads, rows, PAIR), lambda i, m: (i, 0, 0, 0)),
                pl.BlockSpec((1, 8, rows), lambda i, m: (i, 0, 0)),
            ],
            scratch_shapes=[
                pltpu.VMEM((lines, heads, rows, PAIR), BF),
                pltpu.VMEM((stride * lines, rows, PAIR), BF),
                pltpu.VMEM((8, rows), F32),
                pltpu.VMEM((8, rows), F32),
                pltpu.VMEM((heads, PAIR, rows), F32),
            ],
        ),
        out_shape=[jax.ShapeDtypeStruct((rows, q_cols), BF)] * lines
        + [
            jax.ShapeDtypeStruct((lines, heads, rows, PAIR), F32),
            jax.ShapeDtypeStruct((lines, 8, rows), F32),
        ],
        compiler_params=pltpu.CompilerParams(vmem_limit_bytes=48 * 1024 * 1024),
        cost_estimate=pl.CostEstimate(
            flops=36 * 4 * rows * rows * PAIR * 2, bytes_accessed=8 << 20, transcendentals=36 * rows * rows
        ),
        name="attend",
    )(meta, *q, *kv, start_row)


def attend_back_kernel(heads, rows, lines, stride, meta, *refs):
    q_refs, g_ref, kv_refs = refs[:lines], refs[lines], refs[lines + 1 : lines + 1 + stride]
    raw_ref, log_ref, start_ref = refs[lines + 1 + stride : lines + stride + 4]
    outs = refs[lines + stride + 4 :]
    dq_refs, (keep_ref, send_ref, q_s, g_s, kv_s, dq_s, dkv_s, delta_s) = outs[:lines], outs[lines:]
    slot, place, own, low, clear = position(meta, lines)

    @pl.when(slot == 0)
    def _():
        spread_heads(q_refs, q_s, heads, False)
        spread_heads([g_ref.at[s ^ (place // stride)] for s in range(lines)], g_s, heads, True)
        gather_blocks(kv_refs, kv_s, lines)
        dkv_s[...] = jnp.zeros_like(dkv_s)

    dq_s[...] = jnp.zeros_like(dq_s)
    for h in range(heads):
        prod = raw_ref[0, h] * g_s[slot, h].astype(F32)
        delta_s[h : h + 1, :] = jnp.sum(prod.T, axis=0, keepdims=True)

    def step(blk, masked):
        x = blk ^ place
        index = (x % stride) * lines + x // stride
        kv = kv_s[index]
        if masked:
            seen = visible(blk, own, rows, start_ref[0])
        each = range(heads)
        scores = [dot(kv, q_s[slot, h], NT) for h in each]
        grad_probs = [dot(kv, g_s[slot, h], NT) for h in each]
        if masked:
            scores = [jnp.where(seen, s, NEG) for s in scores]
        p = [jnp.exp(scores[h] - log_ref[0, h : h + 1, :]) for h in each]
        grad_scores = [(p[h] * (grad_probs[h] - delta_s[h : h + 1, :])).astype(BF) for h in each]
        parts = [dot(grad_scores[h], q_s[slot, h]) + dot(p[h].astype(BF), g_s[slot, h]) for h in each]
        dkv_s[index] += sum(parts[1:], parts[0])
        for h in each:
            dq_s[h] += dot(grad_scores[h], kv, TN)

    walk(low, clear, own, step)
    dq = jnp.concatenate([dq_s[h][:, :HD] * 0.125 for h in range(heads)], 1).astype(BF)
    for s in range(lines):

        @pl.when(slot == s)
        def _(s=s):
            dq_refs[s][...] = dq

    @pl.when(slot == lines - 1)
    def _():
        for m in range(stride):
            half = m // 2
            out = send_ref if m % 2 else keep_ref
            out[half * lines : (half + 1) * lines] = dkv_s[m * lines : (m + 1) * lines].astype(BF)


def attend_back(meta, q, g, kv, raw, logs, start_row, heads):
    lines, stride = len(q), len(kv)
    rows, q_cols = q[0].shape
    blocks = lines * stride
    narrow = whole_block((rows, q_cols))
    half = whole_block((blocks // 2, rows, PAIR))
    return pl.pallas_call(
        functools.partial(attend_back_kernel, heads, rows, lines, stride),
        grid_spec=pltpu.PrefetchScalarGridSpec(
            num_scalar_prefetch=1,
            grid=(lines,),
            in_specs=[narrow] * lines
            + [whole_block((lines, rows, q_cols))]
            + [whole_block((lines, rows, PAIR))] * stride
            + [
                pl.BlockSpec((1, heads, rows, PAIR), lambda i, m: (i, 0, 0, 0)),
                pl.BlockSpec((1, 8, rows), lambda i, m: (i, 0, 0)),
                pl.BlockSpec((1, 1, rows), lambda i, m: (i, 0, 0)),
            ],
            out_specs=[narrow] * lines + [half] * 2,
            scratch_shapes=[
                pltpu.VMEM((lines, heads, rows, PAIR), BF),
                pltpu.VMEM((lines, heads, rows, PAIR), BF),
                pltpu.VMEM((blocks, rows, PAIR), BF),
                pltpu.VMEM((heads, rows, PAIR), F32),
                pltpu.VMEM((blocks, rows, PAIR), F32),
                pltpu.VMEM((8, rows), F32),
            ],
        ),
        out_shape=[jax.ShapeDtypeStruct((rows, q_cols), BF)] * lines
        + [jax.ShapeDtypeStruct((blocks // 2, rows, PAIR), BF)] * 2,
        compiler_params=pltpu.CompilerParams(vmem_limit_bytes=56 * 1024 * 1024),
        cost_estimate=pl.CostEstimate(
            flops=36 * 10 * rows * rows * PAIR * 2, bytes_accessed=10 << 20, transcendentals=36 * rows * rows
        ),
        name="attend_back",
    )(meta, *q, g, *kv, raw, logs, start_row)


def experts_kernel(x_ref, g_ref, gate_ref, wg_ref, wu_ref, wd_ref, out_ref, back_ref, inner_ref):
    each = range(x_ref.shape[0])
    cap = x_ref.shape[1]
    gate_pre = [dot(x_ref[i], wg_ref[i]) for i in each]
    grad_expert = [(gate_ref[i] * g_ref[i].astype(F32)).astype(BF) for i in each]
    grad_act = [dot(grad_expert[i], wd_ref[i], NT) for i in each]
    up_pre = [dot(x_ref[i], wu_ref[i]) for i in each]
    sigma = [jax.nn.sigmoid(gate_pre[i]) for i in each]
    silu = [gate_pre[i] * sigma[i] for i in each]
    act = [(silu[i] * up_pre[i]).astype(BF) for i in each]
    grad_gate = [
        (grad_act[i] * up_pre[i] * sigma[i] * (1.0 + gate_pre[i] * (1.0 - sigma[i]))).astype(BF)
        for i in each
    ]
    grad_up = [(grad_act[i] * silu[i]).astype(BF) for i in each]
    for i in each:
        out = dot(act[i], wd_ref[i])
        inner = jnp.sum(out * g_ref[i].astype(F32), axis=-1, keepdims=True)
        inner_ref[i] = jnp.broadcast_to(inner, (cap, 128)).T[:8]
        out_ref[i] = (gate_ref[i] * out).astype(BF)
        back_ref[i] = (dot(grad_gate[i], wg_ref[i], NT) + dot(grad_up[i], wu_ref[i], NT)).astype(BF)


def run_experts(x, g, gate, w_gate, w_up, w_down):
    experts, cap, width = x.shape
    hidden = w_gate.shape[2]
    at_once = 2 if experts % 2 == 0 else 1

    def of(*shape):
        return pl.BlockSpec((at_once,) + shape, lambda e: (e, 0, 0))

    return pl.pallas_call(
        experts_kernel,
        grid=(experts // at_once,),
        in_specs=[
            of(cap, width),
            of(cap, width),
            of(cap, 1),
            of(width, hidden),
            of(width, hidden),
            of(hidden, width),
        ],
        out_specs=[of(cap, width), of(cap, width), of(8, cap)],
        out_shape=[
            jax.ShapeDtypeStruct((experts, cap, width), BF),
            jax.ShapeDtypeStruct((experts, cap, width), BF),
            jax.ShapeDtypeStruct((experts, 8, cap), F32),
        ],
        compiler_params=pltpu.CompilerParams(vmem_limit_bytes=56 * 1024 * 1024),
        cost_estimate=pl.CostEstimate(
            flops=experts * cap * width * hidden * 12,
            bytes_accessed=experts * width * (hidden * 6 + cap * 8),
            transcendentals=experts * cap * hidden,
        ),
        name="experts",
    )(x, g, gate, w_gate, w_up, w_down)


def weights_kernel(dp, at, a_ref, b_ref, keep_ref, send_ref):
    size = a_ref.shape[1] // dp
    chunk = 4
    odd = at[0] != 0
    for part in range(dp // chunk):
        span = slice(part * chunk * size, (part + 1) * chunk * size)
        block = dot(a_ref[:, span], b_ref[...], TN).astype(BF)
        for pair in range(chunk // 2):
            one = block[2 * pair * size : (2 * pair + 1) * size]
            two = block[(2 * pair + 1) * size : (2 * pair + 2) * size]
            at_pair = part * (chunk // 2) + pair
            keep_ref[at_pair] = jnp.where(odd, two, one)
            send_ref[at_pair] = jnp.where(odd, one, two)


def weight_parts(bit, a, b, dp):
    rows, width = a.shape
    columns = b.shape[1]
    out = (dp // 2, width // dp, columns)
    return pl.pallas_call(
        functools.partial(weights_kernel, dp),
        grid_spec=pltpu.PrefetchScalarGridSpec(
            num_scalar_prefetch=1,
            grid=(1,),
            in_specs=[whole_block(x.shape) for x in (a, b)],
            out_specs=[whole_block(out)] * 2,
        ),
        out_shape=[jax.ShapeDtypeStruct(out, BF)] * 2,
        compiler_params=pltpu.CompilerParams(vmem_limit_bytes=48 * 1024 * 1024),
        cost_estimate=pl.CostEstimate(
            flops=2 * rows * width * columns, bytes_accessed=8 << 20, transcendentals=0
        ),
        name="weights",
    )(bit[None], a, b)


def flat(x):
    return x.reshape(x.shape[0] * x.shape[1], x.shape[2])


def owner_forward_kernel(n_x, n_g, at, gate_ref, wg_ref, wu_ref, wd_ref, *refs):
    x_refs, g_refs, outs = refs[:n_x], refs[n_x : n_x + n_g], refs[n_x + n_g :]
    act_ref, grad_gate_ref, grad_up_ref = outs

    def span(i, ref):
        return pl.ds(pl.multiple_of(at[1 + i], ref.shape[2]), ref.shape[2])

    gate_pre = sum(dot(flat(x[...]), wg_ref[0, span(i, x), :]) for i, x in enumerate(x_refs))
    up_pre = sum(dot(flat(x[...]), wu_ref[0, span(i, x), :]) for i, x in enumerate(x_refs))
    grad_act = sum(
        dot(
            (gate_ref[...] * flat(g[...]).astype(F32)).astype(BF),
            wd_ref[0, :, span(n_x + i, g)],
            NT,
        )
        for i, g in enumerate(g_refs)
    )
    sigma = jax.nn.sigmoid(gate_pre)
    silu = gate_pre * sigma
    act_ref[...] = (silu * up_pre).astype(BF)
    grad_gate_ref[...] = (
        grad_act * up_pre * sigma * (1.0 + gate_pre * (1.0 - sigma))
    ).astype(BF)
    grad_up_ref[...] = (grad_act * silu).astype(BF)


def owner_grads_kernel(n_x, n_g, at, gate_ref, act_ref, grad_gate_ref, grad_up_ref, *refs):
    x_refs, g_refs, outs = refs[:n_x], refs[n_x : n_x + n_g], refs[n_x + n_g :]
    gate_out, up_out, down_out = outs

    def span(i, ref):
        return pl.ds(pl.multiple_of(at[1 + i], ref.shape[2]), ref.shape[2])

    @pl.when(pl.program_id(0) == 0)
    def _():
        for out in outs:
            out[...] = jnp.zeros_like(out)

    for i, ref in enumerate(x_refs):
        x = flat(ref[...])
        gate_out[0, span(i, ref), :] += dot(x, grad_gate_ref[...], TN)
        up_out[0, span(i, ref), :] += dot(x, grad_up_ref[...], TN)
    for i, ref in enumerate(g_refs):
        grad_expert = (gate_ref[...] * flat(ref[...]).astype(F32)).astype(BF)
        down_out[0, :, span(n_x + i, ref)] += dot(act_ref[...], grad_expert, TN)


def owner_call(kernel, name, at, gate, given, x, g, weights, outs, steps):
    dp, cap, _ = x[0].shape
    rows = dp * cap // steps

    def rowwise(a):
        return pl.BlockSpec((rows, a.shape[1]), lambda i, m: (i, 0))

    def piece(a):
        return pl.BlockSpec((dp // steps, cap, a.shape[2]), lambda i, m: (i, 0, 0))

    def weight(a):
        return pl.BlockSpec((1,) + a.shape[1:], lambda i, m: (m[0], 0, 0))

    out_specs = [rowwise(o) if len(o.shape) == 2 else whole_block(o.shape) for o in outs]
    return pl.pallas_call(
        functools.partial(kernel, len(x), len(g)),
        grid_spec=pltpu.PrefetchScalarGridSpec(
            num_scalar_prefetch=1,
            grid=(steps,),
            in_specs=[rowwise(gate)]
            + [rowwise(a) for a in given]
            + [weight(w) for w in weights]
            + [piece(a) for a in list(x) + list(g)],
            out_specs=out_specs,
        ),
        out_shape=outs,
        compiler_params=pltpu.CompilerParams(vmem_limit_bytes=58 * 1024 * 1024),
        cost_estimate=pl.CostEstimate(flops=10 << 30, bytes_accessed=24 << 20, transcendentals=1 << 20),
        name=name,
    )(at, gate, *given, *weights, *x, *g)


def shards(
    layer_in,
    norm1_gain,
    w_query,
    w_key,
    w_value,
    w_out,
    norm2_gain,
    router,
    w_gate,
    w_up,
    w_down,
    segments,
    routes,
    out_grad,
):
    rows, width = layer_in.shape
    kv_heads = w_key.shape[1] // HD
    group = w_query.shape[1] // HD // kv_heads
    q_cols = group * HD
    experts = w_gate.shape[0]
    dp = lax.axis_size("dp")
    place = lax.axis_index("dp")
    tensor_size = lax.axis_size("tensor")
    tensor_at = lax.axis_index("tensor")
    lines = kv_heads
    stride = dp // lines
    line = place >> (stride.bit_length() - 1)
    part = rows // tensor_size
    first = tensor_at * part
    held = experts // dp
    cols = width // tensor_size
    first_col = tensor_at * cols

    names = jnp.arange(experts, dtype=jnp.int32)
    named = jnp.any(routes[:, :, None] == names[None, None, :], axis=1)
    earlier = jnp.tril(jnp.ones((rows, rows), BF), -1)
    slots = jnp.where(named, dot(earlier, named.astype(BF)).astype(jnp.int32), -1)
    in_slot = slots.T[:, None, :] == jnp.arange(CAP, dtype=jnp.int32)[None, :, None]
    to_slots = in_slot.astype(BF).reshape(experts * CAP, rows)
    from_slots = (
        (slots[:, :, None] == jnp.arange(CAP, dtype=jnp.int32)[None, None, :])
        .astype(BF)
        .reshape(rows, experts * CAP)
    )

    def to_experts(x):
        return dot(to_slots, x).astype(BF).reshape(experts, CAP, -1)

    def half(x, i):
        size = cols // 2
        return to_experts(lax.dynamic_slice_in_dim(x, tensor_at * cols + i * size, size, 1))

    q_blocks = place ^ (jnp.arange(lines, dtype=jnp.int32) * stride)
    seg_query = jnp.stack(
        [lax.dynamic_slice_in_dim(segments, q_blocks[s] * rows, rows, 0) for s in range(lines)]
    )
    documents = jnp.arange(DOCS, dtype=jnp.int32)
    lengths_before = jnp.sum(
        (segments[None, :] < documents[:, None]).astype(jnp.int32), axis=1
    )
    starts = jnp.sum(
        jnp.where(seg_query[None] == documents[:, None, None], lengths_before[:, None, None], 0),
        axis=0,
    )
    shift = rows.bit_length() - 1
    meta = jnp.concatenate(
        [place[None], q_blocks, starts[:, 0] >> shift, (starts[:, -1] + rows - 1) >> shift]
    ).astype(jnp.int32)

    normed_in, kv_mine, q_mine = project(line, layer_in, norm1_gain, w_query, w_key, w_value, lines)

    def to_lines(blocks):
        return [b if s == 0 else across(b, "dp", s * stride) for s, b in enumerate(blocks)]

    kv = [jnp.stack(to_lines(kv_mine))]
    q = to_lines(q_mine)
    g_sent = [half(out_grad, i) for i in range(2)]
    for turn, bit in enumerate(reversed(bits_of(stride))):
        kv = [piece for one in kv for piece in (one, across(one, "dp", bit))]
        if turn == 0:
            kv[1], g_sent = after(kv[1], g_sent)
    g_sent, (kv, q, starts, meta) = after(g_sent, (kv, q, starts, meta))
    g_first = to_owner(g_sent[0])
    *mixed_far, raw, logs = attend(meta, q, kv, starts[:, None, :], group)
    mixed_far, g_first = after(mixed_far, g_first)

    def from_lines(blocks):
        return xor_blocks(to_lines(blocks), line)

    mixed = jnp.concatenate(from_lines(mixed_far), 1)
    g_late, (mixed, g_slots) = after(g_sent[1], (mixed, to_experts(out_grad)))
    g_second = to_owner(g_late)
    attn = scatter_tensor(dot(mixed, w_out))
    hidden = lax.dynamic_slice_in_dim(layer_in, first, part, 0).astype(F32) + attn
    factor_two = norm_factor(hidden)
    unit_two = hidden * factor_two
    normed_mid = gather_tensor((unit_two * norm2_gain).astype(BF), 0)
    normed_mid, g_second = after(normed_mid, g_second)

    logits = dot(normed_mid, router)
    peak = jnp.max(jnp.where(named, logits, -jnp.inf), axis=1, keepdims=True)
    expo = jnp.where(named, jnp.exp(jnp.where(named, logits - peak, 0.0)), 0.0)
    gates = expo / jnp.sum(expo, axis=1, keepdims=True)
    slot_gate = jnp.sum(jnp.where(in_slot, gates.T[:, None, :], 0.0), axis=-1)

    x_slots = to_experts(normed_mid)
    gate_high = lax.reduce_precision(slot_gate, 8, 7)
    gate_mid = lax.reduce_precision(slot_gate - gate_high, 8, 7)
    gate_pieces = jnp.stack([gate_high, gate_mid, slot_gate - gate_high - gate_mid], 2)
    x_mine = lax.dynamic_slice_in_dim(x_slots, first_col, cols, 2)
    early = cols // 2
    x_late = x_mine[..., early:]
    x_first = to_owner(x_mine[..., :early])
    g_owned = swap_tensor(jnp.concatenate([g_first, g_second], 2), 2)

    out_slots, back_slots, inner_slots = run_experts(
        x_slots, g_slots, slot_gate[:, :, None], w_gate, w_up, w_down
    )
    back_slots, (x_first, g_owned) = after(back_slots, (x_first, g_owned))
    moe_part = dot(from_slots, out_slots.reshape(experts * CAP, width))
    grad_gates = jnp.sum(
        jnp.where(
            slots[:, :, None] == jnp.arange(CAP, dtype=jnp.int32)[None, None, :],
            inner_slots[None, :, 0, :],
            0.0,
        ),
        axis=-1,
    )
    grad_logits = gates * (grad_gates - jnp.sum(gates * grad_gates, axis=-1, keepdims=True))
    grad_mid_part = dot(from_slots, back_slots.reshape(experts * CAP, width)) + lax.dot_general(
        grad_logits, router.astype(F32), NT, precision=HIGH, preferred_element_type=F32
    )
    (x_late, gate_pieces, router_part), grad_mid_part = after(
        (x_late, gate_pieces, (grad_logits, normed_mid)), grad_mid_part
    )
    x_second = to_owner(
        jnp.concatenate([x_late, jnp.pad(gate_pieces.astype(BF), ((0, 0), (0, 0), (0, 125)))], 2)
    )
    router_part = lax.dot_general(
        router_part[0], router_part[1].astype(F32), TN, precision=HIGH, preferred_element_type=F32
    )
    grad_mid, moe_part = after(scatter_tensor(grad_mid_part), moe_part)
    gain_two_part = jnp.sum(grad_mid * unit_two, axis=0)
    grad_rows = lax.dynamic_slice_in_dim(out_grad, first, part, 0).astype(F32)
    grad_hidden = grad_rows + norm_back(unit_two, factor_two, norm2_gain, grad_mid)
    hidden_low = gather_tensor(grad_hidden.astype(BF), 0)
    grad_mixed = dot(hidden_low, w_out, NT).astype(BF)
    g = jnp.stack(columns_of(grad_mixed, lines))
    g, (x_first, x_second, hidden_late) = after(g, (x_first, x_second, hidden_low))
    if lines > 1:
        groups = [[first_of + j * stride for j in range(lines)] for first_of in range(stride)]
        g = lax.all_to_all(g, "dp", 0, 0, tiled=True, axis_index_groups=groups)
    gate_owned = jnp.sum(x_second[..., cols - early : cols - early + 3].astype(F32), axis=2)
    x_owned = swap_tensor(jnp.concatenate([x_first, x_second[..., : cols - early]], 2), 2)
    proj_part = dot(hidden_late, mixed, TN).astype(BF).reshape(dp // 2, 2, width // dp, -1)
    proj_keep, proj_send = (
        lax.dynamic_index_in_dim(proj_part, (place & 1) ^ other, 1, keepdims=False)
        for other in (0, 1)
    )
    proj_got = send_rows(pair_sum(proj_keep, proj_send))
    *dq_far, keep, send = attend_back(meta, q, g, kv, raw, logs, starts[:, None, :], group)

    dkv = (keep + across(send, "dp", 1)).reshape(stride // 2, lines, rows, PAIR)
    dkv, dq_far, proj_got = lax.optimization_barrier((dkv, dq_far, proj_got))
    proj_out = jnp.sum(proj_got.astype(F32), axis=0).T
    for bit in bits_of(stride)[1:]:
        view = dkv.reshape((dkv.shape[0] // 2, 2) + dkv.shape[1:])
        dkv = view[:, 0] + across(view[:, 1], "dp", bit)
    dkv, (moe_part, x_owned, g_owned) = after(dkv[0], (moe_part, x_owned, g_owned))
    dq = from_lines(dq_far)
    dkv = from_lines([dkv[s] for s in range(lines)])
    def mine(x, e):
        return x.reshape((dp, held, CAP) + x.shape[2:])[:, e]

    def pieces_of(parts):
        return [(parts[0], first_col), (parts[1], cols - first_col)]

    def owner_work(x_parts, g_parts):
        if tensor_size == 2:
            x, g = pieces_of(x_parts), pieces_of(g_parts)
        else:
            x, g = [(assemble(x_parts, 2), 0)], [(assemble(g_parts, 2), 0)]
        results = []
        for e in range(held):
            at = jnp.stack([jnp.int32(place * held + e)] + [jnp.int32(o) for _, o in x + g])
            tokens = [mine(a, e) for a, _ in x], [mine(a, e) for a, _ in g]
            gate = mine(gate_owned, e).reshape(dp * CAP, 1)
            hidden_shape = jax.ShapeDtypeStruct((dp * CAP, w_gate.shape[2]), BF)
            given_back = owner_call(
                owner_forward_kernel,
                "owner_forward",
                at,
                gate,
                [],
                *tokens,
                [w_gate, w_up, w_down],
                [hidden_shape] * 3,
                4,
            )
            results.append((at, gate, given_back, *tokens))
        return results

    def owner_grads(owned):
        shapes = [
            jax.ShapeDtypeStruct((1,) + w.shape[1:], F32) for w in (w_gate, w_up, w_down)
        ]
        grad_outs = [
            owner_call(owner_grads_kernel, "owner_grads", at, gate, given, x, g, [], shapes, 2)
            for at, gate, given, x, g in owned
        ]
        return [jnp.concatenate(each, 0) for each in zip(*grad_outs)]

    owned = owner_work(x_owned, g_owned)
    w_all = jnp.concatenate([w_query, w_key, w_value], 1)
    dqkv = jnp.concatenate(dq + [b[:, :HD] for b in dkv] + [b[:, HD:] for b in dkv], 1)
    in_float = layer_in.astype(F32)
    factor_one = norm_factor(in_float)
    unit_one = in_float * factor_one
    dqkv, (owned, moe_rows, unit_one) = after(dqkv, (owned, scatter_tensor(moe_part), unit_one))
    grad_in_part = dot(dqkv, w_all, NT)
    gain_one_part = jnp.sum(grad_in_part * unit_one, axis=0)
    small = jnp.concatenate([router_part, gain_two_part[None], gain_one_part[None]], 0)
    small = total(small.reshape(-1, 128), "dp")
    weight_keep, weight_send = weight_parts(place & 1, normed_in, dqkv, dp)
    weight_pair, (owned, small, grad_in_part) = after(
        pair_sum(weight_keep, weight_send), (owned, small, grad_in_part)
    )
    small = total(small, "tensor")
    owner_outs, small, grad_in_rows = lax.optimization_barrier(
        (owner_grads(owned), small, scatter_tensor(grad_in_part))
    )
    (gate_out, up_out, down_out), weight_got = after(owner_outs, send_rows(weight_pair))
    weight_grad = jnp.sum(weight_got.astype(F32), axis=0)
    layer_out = (hidden + moe_rows).astype(BF)
    ends = [0]
    for size in (lines * q_cols, lines * HD, lines * HD):
        ends.append(ends[-1] + size)
    query_out, key_out, value_out = (weight_grad[:, a:b] for a, b in zip(ends[:-1], ends[1:]))

    factor_rows = lax.dynamic_slice_in_dim(factor_one, first, part, 0)
    unit_rows = lax.dynamic_slice_in_dim(in_float, first, part, 0) * factor_rows
    input_grad = grad_hidden + norm_back(unit_rows, factor_rows, norm1_gain, grad_in_rows)
    small = small.reshape(-1, width)
    gain_one_grad = small[experts + 1]
    gain_two_grad = small[experts]
    router_grad = small[:experts].T

    return (
        layer_out,
        input_grad,
        gain_one_grad,
        query_out,
        key_out,
        value_out,
        proj_out,
        gain_two_grad,
        router_grad,
        gate_out,
        up_out,
        down_out,
    )


def solution(mesh):
    in_specs = (
        P("dp", None),
        P(),
        P(None, "tensor"),
        P(None, "tensor"),
        P(None, "tensor"),
        P("tensor", None),
        P(),
        P(),
        P(None, None, "tensor"),
        P(None, None, "tensor"),
        P(None, "tensor", None),
        P(),
        P("dp", None),
        P("dp", None),
    )
    out_specs = (
        P(("dp", "tensor"), None),
        P(("dp", "tensor"), None),
        P(),
        P("dp", "tensor"),
        P("dp", "tensor"),
        P("dp", "tensor"),
        P("tensor", "dp"),
        P(),
        P(),
        P("dp", None, "tensor"),
        P("dp", None, "tensor"),
        P("dp", "tensor", None),
    )
    return jax.shard_map(shards, mesh=mesh, in_specs=in_specs, out_specs=out_specs, check_vma=False)
```

```python
import functools

import jax
import jax.numpy as jnp
from jax import lax
from jax.experimental import pallas as pl
from jax.experimental.pallas import tpu as pltpu
from jax.sharding import PartitionSpec as P

HD = 64
PAIR = 2 * HD
CAP = 128
DOCS = 8
EPS = 1e-05
HIGH = lax.Precision.HIGHEST
NEG = -1000000000.0
BF = jnp.bfloat16
F32 = jnp.float32

NT = (((1,), (1,)), ((), ()))
TN = (((0,), (0,)), ((), ()))


def dot(a, b, dims=None):
    if dims is None:
        return jnp.dot(a, b, preferred_element_type=F32)
    return lax.dot_general(a, b, dims, preferred_element_type=F32)


def across(x, axis, mask):
    n = lax.axis_size(axis)
    return lax.ppermute(x, axis, [(i, i ^ mask) for i in range(n)])


def bits_of(n):
    return [1 << k for k in range(n.bit_length() - 1)]


def after(x, y):
    return lax.optimization_barrier((x, y))


def to_owner(x):
    return lax.all_to_all(x, "dp", 0, 0, tiled=True)


def norm_factor(value):
    return lax.rsqrt(jnp.mean(value * value, axis=-1, keepdims=True) + EPS)


def norm_back(unit, factor, gain, grad):
    inner = gain * grad
    return factor * (inner - unit * jnp.mean(unit * inner, axis=-1, keepdims=True))


def total(x, axis):
    bits = bits_of(lax.axis_size(axis))

    def met(low, bit):
        return across(low, axis, bit).astype(F32)

    while bits:
        one, *bits = bits
        low = x.astype(BF)
        if bits:
            two, *bits = bits
            far, both = met(low, two), met(low, one | two)
            x = (low.astype(F32) + met(low, one)) + (far + both)
        else:
            x = low.astype(F32) + met(low, one)
    return x


def scatter_tensor(x):
    n = lax.axis_size("tensor")
    if n != 2:
        return lax.psum_scatter(x.astype(BF), "tensor", scatter_dimension=0, tiled=True).astype(F32)
    me = lax.axis_index("tensor")
    part = x.shape[0] // 2
    sent = lax.dynamic_slice_in_dim(x, (1 - me) * part, part, 0).astype(BF)
    own = lax.dynamic_slice_in_dim(x, me * part, part, 0)
    return own.astype(F32) + across(sent, "tensor", 1).astype(F32)


def swap_tensor(x, dim):
    if lax.axis_size("tensor") != 2:
        return (lax.all_gather(x, "tensor", axis=dim, tiled=True),)
    return x, across(x, "tensor", 1)


def assemble(parts, dim):
    if len(parts) == 1:
        return parts[0]
    own, other = parts
    low = lax.axis_index("tensor") == 0
    return jnp.concatenate([jnp.where(low, own, other), jnp.where(low, other, own)], dim)


def gather_tensor(x, dim):
    return assemble(swap_tensor(x, dim), dim)


def xor_blocks(blocks, index):
    for bit in bits_of(len(blocks)):
        crossed = (index & bit) != 0
        blocks = [jnp.where(crossed, blocks[s ^ bit], block) for s, block in enumerate(blocks)]
    return blocks


def columns_of(x, count):
    size = x.shape[1] // count
    return [x[:, s * size : (s + 1) * size] for s in range(count)]


def pair_sum(keep, send):
    return keep + across(send, "dp", 1)


def send_rows(x):
    n = lax.axis_size("dp")
    groups = [list(range(first, n, 2)) for first in range(2)]
    return lax.all_to_all(x, "dp", 0, 0, tiled=True, axis_index_groups=groups)


def project_kernel(lines, q_cols, at, x_ref, gain_ref, wq_ref, wk_ref, wv_ref, normed_ref, *rest):
    kv_refs, q_refs = rest[:lines], rest[lines : 2 * lines]
    kv_s, q_s = rest[2 * lines :]
    x = x_ref[...].astype(F32)
    scale = lax.rsqrt(jnp.mean(x * x, axis=-1, keepdims=True) + EPS)
    normed = (x * scale * gain_ref[...]).astype(BF)
    normed_ref[...] = normed
    key = dot(normed, wk_ref[...])
    value = dot(normed, wv_ref[...])
    query = dot(normed, wq_ref[...])
    for c in range(lines):
        pair = [key[:, c * HD : (c + 1) * HD], value[:, c * HD : (c + 1) * HD]]
        kv_s[c] = jnp.concatenate(pair, 1).astype(BF)
        q_s[c] = query[:, c * q_cols : (c + 1) * q_cols].astype(BF) * jnp.asarray(0.125, BF)
    for s in range(lines):
        kv_refs[s][...] = kv_s[s ^ at[0]]
        q_refs[s][...] = q_s[s ^ at[0]]


def project(line, x, gain, w_query, w_key, w_value, lines):
    rows, width = x.shape
    q_cols = w_query.shape[1] // lines

    def whole(*shape):
        return pl.BlockSpec(shape, lambda i, m: (0,) * len(shape))

    out = [(rows, width)] + [(rows, PAIR)] * lines + [(rows, q_cols)] * lines
    outs = pl.pallas_call(
        functools.partial(project_kernel, lines, q_cols),
        grid_spec=pltpu.PrefetchScalarGridSpec(
            num_scalar_prefetch=1,
            grid=(1,),
            in_specs=[
                whole(rows, width),
                whole(1, width),
                whole(*w_query.shape),
                whole(*w_key.shape),
                whole(*w_value.shape),
            ],
            out_specs=[whole(*shape) for shape in out],
            scratch_shapes=[
                pltpu.VMEM((lines, rows, PAIR), BF),
                pltpu.VMEM((lines, rows, q_cols), BF),
            ],
        ),
        out_shape=[jax.ShapeDtypeStruct(shape, BF) for shape in out],
        compiler_params=pltpu.CompilerParams(vmem_limit_bytes=48 * 1024 * 1024),
        cost_estimate=pl.CostEstimate(
            flops=2 * rows * width * (w_query.shape[1] + 2 * w_key.shape[1]),
            bytes_accessed=8 << 20,
            transcendentals=0,
        ),
        name="project",
    )(line[None], x, gain[None], w_query, w_key, w_value)
    return outs[0], outs[1 : 1 + lines], outs[1 + lines :]


def spread_heads(refs, out, heads, high):
    for s, ref in enumerate(refs):
        x = ref[...]
        zero = jnp.zeros((x.shape[0], HD), BF)
        for h in range(heads):
            one = x[:, h * HD : (h + 1) * HD]
            out[s, h] = jnp.concatenate([zero, one] if high else [one, zero], 1)


def gather_blocks(refs, out, lines):
    for m, ref in enumerate(refs):
        out[m * lines : (m + 1) * lines] = ref[...]


def position(meta, lines):
    slot = pl.program_id(0)
    return slot, meta[0], meta[1 + slot], meta[1 + lines + slot], meta[1 + 2 * lines + slot]


def walk(low, clear, own, step):
    def body(blk, carry):
        full = (blk >= clear) & (blk < own)

        @pl.when(full)
        def _():
            step(blk, False)

        @pl.when(jnp.logical_not(full))
        def _():
            step(blk, True)

        return carry

    lax.fori_loop(low, own + 1, body, 0)


def visible(blk, own, rows, start):
    key_pos = lax.broadcasted_iota(jnp.int32, (rows, rows), 0) + blk * rows
    q_pos = lax.broadcasted_iota(jnp.int32, (rows, rows), 1) + own * rows
    return (key_pos >= start) & (key_pos <= q_pos)


def attend_kernel(heads, rows, lines, stride, meta, *refs):
    q_refs, kv_refs, start_ref = refs[:lines], refs[lines : lines + stride], refs[lines + stride]
    outs = refs[lines + stride + 1 :]
    mixed_refs, (raw_ref, log_ref, q_s, kv_s, m_s, l_s, acc_s) = outs[:lines], outs[lines:]
    slot, place, own, low, clear = position(meta, lines)

    @pl.when(slot == 0)
    def _():
        spread_heads(q_refs, q_s, heads, False)
        gather_blocks(kv_refs, kv_s, lines)

    m_s[...] = jnp.full_like(m_s, -3e38)
    l_s[...] = jnp.zeros_like(l_s)
    acc_s[...] = jnp.zeros_like(acc_s)

    def step(blk, masked):
        x = blk ^ place
        index = (x % stride) * lines + x // stride
        kv = kv_s[index]
        if masked:
            seen = visible(blk, own, rows, start_ref[0])
        each = range(heads)
        scores = [dot(kv, q_s[slot, h], NT) for h in each]
        if masked:
            scores = [jnp.where(seen, s, NEG) for s in scores]
        m_old = [m_s[h : h + 1, :] for h in each]
        m_new = [jnp.maximum(m_old[h], jnp.max(scores[h], axis=0, keepdims=True)) for h in each]
        p = [jnp.exp(scores[h] - m_new[h]) for h in each]
        alpha = [jnp.exp(m_old[h] - m_new[h]) for h in each]
        added = [dot(kv, p[h].astype(BF), TN) for h in each]
        for h in each:
            l_s[h : h + 1, :] = l_s[h : h + 1, :] * alpha[h] + jnp.sum(p[h], axis=0, keepdims=True)
            acc_s[h] = acc_s[h] * alpha[h] + added[h]
            m_s[h : h + 1, :] = m_new[h]

    walk(low, clear, own, step)
    parts = []
    for h in range(heads):
        out = (acc_s[h] / l_s[h : h + 1, :]).T
        raw_ref[0, h] = out
        parts.append(out[:, HD:])
    log_ref[0] = m_s[...] + jnp.log(l_s[...])
    mixed = jnp.concatenate(parts, 1).astype(BF)
    for s in range(lines):

        @pl.when(slot == s)
        def _(s=s):
            mixed_refs[s][...] = mixed


def whole_block(shape):
    return pl.BlockSpec(shape, lambda i, m: (0,) * len(shape))


def attend(meta, q, kv, start_row, heads):
    lines, stride = len(q), len(kv)
    rows, q_cols = q[0].shape
    narrow = whole_block((rows, q_cols))
    return pl.pallas_call(
        functools.partial(attend_kernel, heads, rows, lines, stride),
        grid_spec=pltpu.PrefetchScalarGridSpec(
            num_scalar_prefetch=1,
            grid=(lines,),
            in_specs=[narrow] * lines
            + [whole_block((lines, rows, PAIR))] * stride
            + [pl.BlockSpec((1, 1, rows), lambda i, m: (i, 0, 0))],
            out_specs=[narrow] * lines
            + [
                pl.BlockSpec((1, heads, rows, PAIR), lambda i, m: (i, 0, 0, 0)),
                pl.BlockSpec((1, 8, rows), lambda i, m: (i, 0, 0)),
            ],
            scratch_shapes=[
                pltpu.VMEM((lines, heads, rows, PAIR), BF),
                pltpu.VMEM((stride * lines, rows, PAIR), BF),
                pltpu.VMEM((8, rows), F32),
                pltpu.VMEM((8, rows), F32),
                pltpu.VMEM((heads, PAIR, rows), F32),
            ],
        ),
        out_shape=[jax.ShapeDtypeStruct((rows, q_cols), BF)] * lines
        + [
            jax.ShapeDtypeStruct((lines, heads, rows, PAIR), F32),
            jax.ShapeDtypeStruct((lines, 8, rows), F32),
        ],
        compiler_params=pltpu.CompilerParams(vmem_limit_bytes=48 * 1024 * 1024),
        cost_estimate=pl.CostEstimate(
            flops=36 * 4 * rows * rows * PAIR * 2, bytes_accessed=8 << 20, transcendentals=36 * rows * rows
        ),
        name="attend",
    )(meta, *q, *kv, start_row)


def attend_back_kernel(heads, rows, lines, stride, meta, *refs):
    q_refs, g_ref, kv_refs = refs[:lines], refs[lines], refs[lines + 1 : lines + 1 + stride]
    raw_ref, log_ref, start_ref = refs[lines + 1 + stride : lines + stride + 4]
    outs = refs[lines + stride + 4 :]
    dq_refs, (keep_ref, send_ref, q_s, g_s, kv_s, dq_s, dkv_s, delta_s) = outs[:lines], outs[lines:]
    slot, place, own, low, clear = position(meta, lines)

    @pl.when(slot == 0)
    def _():
        spread_heads(q_refs, q_s, heads, False)
        spread_heads([g_ref.at[s ^ (place // stride)] for s in range(lines)], g_s, heads, True)
        gather_blocks(kv_refs, kv_s, lines)
        dkv_s[...] = jnp.zeros_like(dkv_s)

    dq_s[...] = jnp.zeros_like(dq_s)
    for h in range(heads):
        prod = raw_ref[0, h] * g_s[slot, h].astype(F32)
        delta_s[h : h + 1, :] = jnp.sum(prod.T, axis=0, keepdims=True)

    def step(blk, masked):
        x = blk ^ place
        index = (x % stride) * lines + x // stride
        kv = kv_s[index]
        if masked:
            seen = visible(blk, own, rows, start_ref[0])
        for h in range(heads):
            q = q_s[slot, h]
            g = g_s[slot, h]
            s = dot(kv, q, NT)
            if masked:
                s = jnp.where(seen, s, NEG)
            p = jnp.exp(s - log_ref[0, h : h + 1, :])
            gp = dot(kv, g, NT)
            gs = (p * (gp - delta_s[h : h + 1, :])).astype(BF)
            part = dot(gs, q) + dot(p.astype(BF), g)
            dkv_s[index] += part
            dq_s[h] += dot(gs, kv, TN)

    walk(low, clear, own, step)
    dq = jnp.concatenate([dq_s[h][:, :HD] * 0.125 for h in range(heads)], 1).astype(BF)
    for s in range(lines):

        @pl.when(slot == s)
        def _(s=s):
            dq_refs[s][...] = dq

    @pl.when(slot == lines - 1)
    def _():
        for m in range(stride):
            half = m // 2
            out = send_ref if m % 2 else keep_ref
            out[half * lines : (half + 1) * lines] = dkv_s[m * lines : (m + 1) * lines].astype(BF)


def attend_back(meta, q, g, kv, raw, logs, start_row, heads):
    lines, stride = len(q), len(kv)
    rows, q_cols = q[0].shape
    blocks = lines * stride
    narrow = whole_block((rows, q_cols))
    half = whole_block((blocks // 2, rows, PAIR))
    return pl.pallas_call(
        functools.partial(attend_back_kernel, heads, rows, lines, stride),
        grid_spec=pltpu.PrefetchScalarGridSpec(
            num_scalar_prefetch=1,
            grid=(lines,),
            in_specs=[narrow] * lines
            + [whole_block((lines, rows, q_cols))]
            + [whole_block((lines, rows, PAIR))] * stride
            + [
                pl.BlockSpec((1, heads, rows, PAIR), lambda i, m: (i, 0, 0, 0)),
                pl.BlockSpec((1, 8, rows), lambda i, m: (i, 0, 0)),
                pl.BlockSpec((1, 1, rows), lambda i, m: (i, 0, 0)),
            ],
            out_specs=[narrow] * lines + [half] * 2,
            scratch_shapes=[
                pltpu.VMEM((lines, heads, rows, PAIR), BF),
                pltpu.VMEM((lines, heads, rows, PAIR), BF),
                pltpu.VMEM((blocks, rows, PAIR), BF),
                pltpu.VMEM((heads, rows, PAIR), F32),
                pltpu.VMEM((blocks, rows, PAIR), F32),
                pltpu.VMEM((8, rows), F32),
            ],
        ),
        out_shape=[jax.ShapeDtypeStruct((rows, q_cols), BF)] * lines
        + [jax.ShapeDtypeStruct((blocks // 2, rows, PAIR), BF)] * 2,
        compiler_params=pltpu.CompilerParams(vmem_limit_bytes=56 * 1024 * 1024),
        cost_estimate=pl.CostEstimate(
            flops=36 * 10 * rows * rows * PAIR * 2, bytes_accessed=10 << 20, transcendentals=36 * rows * rows
        ),
        name="attend_back",
    )(meta, *q, g, *kv, raw, logs, start_row)


def experts_kernel(x_ref, g_ref, gate_ref, wg_ref, wu_ref, wd_ref, out_ref, back_ref, inner_ref):
    each = range(x_ref.shape[0])
    cap = x_ref.shape[1]
    gate_pre = [dot(x_ref[i], wg_ref[i]) for i in each]
    grad_expert = [(gate_ref[i] * g_ref[i].astype(F32)).astype(BF) for i in each]
    grad_act = [dot(grad_expert[i], wd_ref[i], NT) for i in each]
    up_pre = [dot(x_ref[i], wu_ref[i]) for i in each]
    sigma = [jax.nn.sigmoid(gate_pre[i]) for i in each]
    silu = [gate_pre[i] * sigma[i] for i in each]
    act = [(silu[i] * up_pre[i]).astype(BF) for i in each]
    grad_gate = [
        (grad_act[i] * up_pre[i] * sigma[i] * (1.0 + gate_pre[i] * (1.0 - sigma[i]))).astype(BF)
        for i in each
    ]
    grad_up = [(grad_act[i] * silu[i]).astype(BF) for i in each]
    for i in each:
        out = dot(act[i], wd_ref[i])
        inner = jnp.sum(out * g_ref[i].astype(F32), axis=-1, keepdims=True)
        inner_ref[i] = jnp.broadcast_to(inner, (cap, 128)).T[:8]
        out_ref[i] = (gate_ref[i] * out).astype(BF)
        back_ref[i] = (dot(grad_gate[i], wg_ref[i], NT) + dot(grad_up[i], wu_ref[i], NT)).astype(BF)


def run_experts(x, g, gate, w_gate, w_up, w_down):
    experts, cap, width = x.shape
    hidden = w_gate.shape[2]
    at_once = 2 if experts % 2 == 0 else 1

    def of(*shape):
        return pl.BlockSpec((at_once,) + shape, lambda e: (e, 0, 0))

    return pl.pallas_call(
        experts_kernel,
        grid=(experts // at_once,),
        in_specs=[
            of(cap, width),
            of(cap, width),
            of(cap, 1),
            of(width, hidden),
            of(width, hidden),
            of(hidden, width),
        ],
        out_specs=[of(cap, width), of(cap, width), of(8, cap)],
        out_shape=[
            jax.ShapeDtypeStruct((experts, cap, width), BF),
            jax.ShapeDtypeStruct((experts, cap, width), BF),
            jax.ShapeDtypeStruct((experts, 8, cap), F32),
        ],
        compiler_params=pltpu.CompilerParams(vmem_limit_bytes=56 * 1024 * 1024),
        cost_estimate=pl.CostEstimate(
            flops=experts * cap * width * hidden * 12,
            bytes_accessed=experts * width * (hidden * 6 + cap * 8),
            transcendentals=experts * cap * hidden,
        ),
        name="experts",
    )(x, g, gate, w_gate, w_up, w_down)


def weights_kernel(dp, at, a_ref, b_ref, keep_ref, send_ref):
    size = a_ref.shape[1] // dp
    chunk = 4
    odd = at[0] != 0
    for part in range(dp // chunk):
        span = slice(part * chunk * size, (part + 1) * chunk * size)
        block = dot(a_ref[:, span], b_ref[...], TN).astype(BF)
        for pair in range(chunk // 2):
            one = block[2 * pair * size : (2 * pair + 1) * size]
            two = block[(2 * pair + 1) * size : (2 * pair + 2) * size]
            at_pair = part * (chunk // 2) + pair
            keep_ref[at_pair] = jnp.where(odd, two, one)
            send_ref[at_pair] = jnp.where(odd, one, two)


def weight_parts(bit, a, b, dp):
    rows, width = a.shape
    columns = b.shape[1]
    out = (dp // 2, width // dp, columns)
    return pl.pallas_call(
        functools.partial(weights_kernel, dp),
        grid_spec=pltpu.PrefetchScalarGridSpec(
            num_scalar_prefetch=1,
            grid=(1,),
            in_specs=[whole_block(x.shape) for x in (a, b)],
            out_specs=[whole_block(out)] * 2,
        ),
        out_shape=[jax.ShapeDtypeStruct(out, BF)] * 2,
        compiler_params=pltpu.CompilerParams(vmem_limit_bytes=48 * 1024 * 1024),
        cost_estimate=pl.CostEstimate(
            flops=2 * rows * width * columns, bytes_accessed=8 << 20, transcendentals=0
        ),
        name="weights",
    )(bit[None], a, b)


def flat(x):
    return x.reshape(x.shape[0] * x.shape[1], x.shape[2])


def owner_forward_kernel(n_x, n_g, at, gate_ref, wg_ref, wu_ref, wd_ref, *refs):
    x_refs, g_refs, outs = refs[:n_x], refs[n_x : n_x + n_g], refs[n_x + n_g :]
    act_ref, grad_gate_ref, grad_up_ref = outs

    def span(i, ref):
        return pl.ds(pl.multiple_of(at[1 + i], ref.shape[2]), ref.shape[2])

    gate_pre = sum(dot(flat(x[...]), wg_ref[0, span(i, x), :]) for i, x in enumerate(x_refs))
    up_pre = sum(dot(flat(x[...]), wu_ref[0, span(i, x), :]) for i, x in enumerate(x_refs))
    grad_act = sum(
        dot(
            (gate_ref[...] * flat(g[...]).astype(F32)).astype(BF),
            wd_ref[0, :, span(n_x + i, g)],
            NT,
        )
        for i, g in enumerate(g_refs)
    )
    sigma = jax.nn.sigmoid(gate_pre)
    silu = gate_pre * sigma
    act_ref[...] = (silu * up_pre).astype(BF)
    grad_gate_ref[...] = (
        grad_act * up_pre * sigma * (1.0 + gate_pre * (1.0 - sigma))
    ).astype(BF)
    grad_up_ref[...] = (grad_act * silu).astype(BF)


def owner_grads_kernel(n_x, n_g, at, gate_ref, act_ref, grad_gate_ref, grad_up_ref, *refs):
    x_refs, g_refs, outs = refs[:n_x], refs[n_x : n_x + n_g], refs[n_x + n_g :]
    gate_out, up_out, down_out = outs

    def span(i, ref):
        return pl.ds(pl.multiple_of(at[1 + i], ref.shape[2]), ref.shape[2])

    @pl.when(pl.program_id(0) == 0)
    def _():
        for out in outs:
            out[...] = jnp.zeros_like(out)

    for i, ref in enumerate(x_refs):
        x = flat(ref[...])
        gate_out[0, span(i, ref), :] += dot(x, grad_gate_ref[...], TN)
        up_out[0, span(i, ref), :] += dot(x, grad_up_ref[...], TN)
    for i, ref in enumerate(g_refs):
        grad_expert = (gate_ref[...] * flat(ref[...]).astype(F32)).astype(BF)
        down_out[0, :, span(n_x + i, ref)] += dot(act_ref[...], grad_expert, TN)


def owner_call(kernel, name, at, gate, given, x, g, weights, outs, steps):
    dp, cap, _ = x[0].shape
    rows = dp * cap // steps

    def rowwise(a):
        return pl.BlockSpec((rows, a.shape[1]), lambda i, m: (i, 0))

    def piece(a):
        return pl.BlockSpec((dp // steps, cap, a.shape[2]), lambda i, m: (i, 0, 0))

    def weight(a):
        return pl.BlockSpec((1,) + a.shape[1:], lambda i, m: (m[0], 0, 0))

    out_specs = [rowwise(o) if len(o.shape) == 2 else whole_block(o.shape) for o in outs]
    return pl.pallas_call(
        functools.partial(kernel, len(x), len(g)),
        grid_spec=pltpu.PrefetchScalarGridSpec(
            num_scalar_prefetch=1,
            grid=(steps,),
            in_specs=[rowwise(gate)]
            + [rowwise(a) for a in given]
            + [weight(w) for w in weights]
            + [piece(a) for a in list(x) + list(g)],
            out_specs=out_specs,
        ),
        out_shape=outs,
        compiler_params=pltpu.CompilerParams(vmem_limit_bytes=58 * 1024 * 1024),
        cost_estimate=pl.CostEstimate(flops=10 << 30, bytes_accessed=24 << 20, transcendentals=1 << 20),
        name=name,
    )(at, gate, *given, *weights, *x, *g)


def shards(
    layer_in,
    norm1_gain,
    w_query,
    w_key,
    w_value,
    w_out,
    norm2_gain,
    router,
    w_gate,
    w_up,
    w_down,
    segments,
    routes,
    out_grad,
):
    rows, width = layer_in.shape
    kv_heads = w_key.shape[1] // HD
    group = w_query.shape[1] // HD // kv_heads
    q_cols = group * HD
    experts = w_gate.shape[0]
    dp = lax.axis_size("dp")
    place = lax.axis_index("dp")
    tensor_size = lax.axis_size("tensor")
    tensor_at = lax.axis_index("tensor")
    lines = kv_heads
    stride = dp // lines
    line = place >> (stride.bit_length() - 1)
    part = rows // tensor_size
    first = tensor_at * part
    held = experts // dp
    cols = width // tensor_size
    first_col = tensor_at * cols

    names = jnp.arange(experts, dtype=jnp.int32)
    named = jnp.any(routes[:, :, None] == names[None, None, :], axis=1)
    earlier = jnp.tril(jnp.ones((rows, rows), BF), -1)
    slots = jnp.where(named, dot(earlier, named.astype(BF)).astype(jnp.int32), -1)
    in_slot = slots.T[:, None, :] == jnp.arange(CAP, dtype=jnp.int32)[None, :, None]
    to_slots = in_slot.astype(BF).reshape(experts * CAP, rows)
    from_slots = (
        (slots[:, :, None] == jnp.arange(CAP, dtype=jnp.int32)[None, None, :])
        .astype(BF)
        .reshape(rows, experts * CAP)
    )

    def to_experts(x):
        return dot(to_slots, x).astype(BF).reshape(experts, CAP, -1)

    def half(x, i):
        size = cols // 2
        return to_experts(lax.dynamic_slice_in_dim(x, tensor_at * cols + i * size, size, 1))

    q_blocks = place ^ (jnp.arange(lines, dtype=jnp.int32) * stride)
    seg_query = jnp.stack(
        [lax.dynamic_slice_in_dim(segments, q_blocks[s] * rows, rows, 0) for s in range(lines)]
    )
    documents = jnp.arange(DOCS, dtype=jnp.int32)
    lengths_before = jnp.sum(
        (segments[None, :] < documents[:, None]).astype(jnp.int32), axis=1
    )
    starts = jnp.sum(
        jnp.where(seg_query[None] == documents[:, None, None], lengths_before[:, None, None], 0),
        axis=0,
    )
    shift = rows.bit_length() - 1
    meta = jnp.concatenate(
        [place[None], q_blocks, starts[:, 0] >> shift, (starts[:, -1] + rows - 1) >> shift]
    ).astype(jnp.int32)

    normed_in, kv_mine, q_mine = project(line, layer_in, norm1_gain, w_query, w_key, w_value, lines)

    def to_lines(blocks):
        return [b if s == 0 else across(b, "dp", s * stride) for s, b in enumerate(blocks)]

    kv = [jnp.stack(to_lines(kv_mine))]
    q = to_lines(q_mine)
    for bit in reversed(bits_of(stride)):
        kv = [piece for one in kv for piece in (one, across(one, "dp", bit))]
    g_sent, (kv, q, starts, meta) = after([half(out_grad, i) for i in range(2)], (kv, q, starts, meta))
    g_first = to_owner(g_sent[0])
    *mixed_far, raw, logs = attend(meta, q, kv, starts[:, None, :], group)
    mixed_far, g_first = after(mixed_far, g_first)

    def from_lines(blocks):
        return xor_blocks(to_lines(blocks), line)

    mixed = jnp.concatenate(from_lines(mixed_far), 1)
    g_late, (mixed, g_slots) = after(g_sent[1], (mixed, to_experts(out_grad)))
    g_second = to_owner(g_late)
    attn = scatter_tensor(dot(mixed, w_out))
    hidden = lax.dynamic_slice_in_dim(layer_in, first, part, 0).astype(F32) + attn
    factor_two = norm_factor(hidden)
    unit_two = hidden * factor_two
    normed_mid = gather_tensor((unit_two * norm2_gain).astype(BF), 0)
    normed_mid, g_second = after(normed_mid, g_second)

    logits = dot(normed_mid, router)
    peak = jnp.max(jnp.where(named, logits, -jnp.inf), axis=1, keepdims=True)
    expo = jnp.where(named, jnp.exp(jnp.where(named, logits - peak, 0.0)), 0.0)
    gates = expo / jnp.sum(expo, axis=1, keepdims=True)
    slot_gate = jnp.sum(jnp.where(in_slot, gates.T[:, None, :], 0.0), axis=-1)

    x_slots = to_experts(normed_mid)
    gate_high = lax.reduce_precision(slot_gate, 8, 7)
    gate_mid = lax.reduce_precision(slot_gate - gate_high, 8, 7)
    gate_pieces = jnp.stack([gate_high, gate_mid, slot_gate - gate_high - gate_mid], 2)
    x_mine = lax.dynamic_slice_in_dim(x_slots, first_col, cols, 2)
    early = cols // 2
    x_late = x_mine[..., early:]
    x_first = to_owner(x_mine[..., :early])
    g_owned = swap_tensor(jnp.concatenate([g_first, g_second], 2), 2)

    out_slots, back_slots, inner_slots = run_experts(
        x_slots, g_slots, slot_gate[:, :, None], w_gate, w_up, w_down
    )
    back_slots, (x_first, g_owned) = after(back_slots, (x_first, g_owned))
    moe_part = dot(from_slots, out_slots.reshape(experts * CAP, width))
    grad_gates = jnp.sum(
        jnp.where(
            slots[:, :, None] == jnp.arange(CAP, dtype=jnp.int32)[None, None, :],
            inner_slots[None, :, 0, :],
            0.0,
        ),
        axis=-1,
    )
    grad_logits = gates * (grad_gates - jnp.sum(gates * grad_gates, axis=-1, keepdims=True))
    grad_mid_part = dot(from_slots, back_slots.reshape(experts * CAP, width)) + lax.dot_general(
        grad_logits, router.astype(F32), NT, precision=HIGH, preferred_element_type=F32
    )
    (x_late, gate_pieces, router_part), grad_mid_part = after(
        (x_late, gate_pieces, (grad_logits, normed_mid)), grad_mid_part
    )
    x_second = to_owner(
        jnp.concatenate([x_late, jnp.pad(gate_pieces.astype(BF), ((0, 0), (0, 0), (0, 125)))], 2)
    )
    router_part = lax.dot_general(
        router_part[0], router_part[1].astype(F32), TN, precision=HIGH, preferred_element_type=F32
    )
    grad_mid, moe_part = after(scatter_tensor(grad_mid_part), moe_part)
    gain_two_part = jnp.sum(grad_mid * unit_two, axis=0)
    grad_rows = lax.dynamic_slice_in_dim(out_grad, first, part, 0).astype(F32)
    grad_hidden = grad_rows + norm_back(unit_two, factor_two, norm2_gain, grad_mid)
    hidden_low = gather_tensor(grad_hidden.astype(BF), 0)
    grad_mixed = dot(hidden_low, w_out, NT).astype(BF)
    g = jnp.stack(columns_of(grad_mixed, lines))
    g, (x_first, x_second, hidden_late) = after(g, (x_first, x_second, hidden_low))
    if lines > 1:
        groups = [[first_of + j * stride for j in range(lines)] for first_of in range(stride)]
        g = lax.all_to_all(g, "dp", 0, 0, tiled=True, axis_index_groups=groups)
    gate_owned = jnp.sum(x_second[..., cols - early : cols - early + 3].astype(F32), axis=2)
    x_owned = swap_tensor(jnp.concatenate([x_first, x_second[..., : cols - early]], 2), 2)
    proj_part = dot(hidden_late, mixed, TN).astype(BF).reshape(dp // 2, 2, width // dp, -1)
    proj_keep, proj_send = (
        lax.dynamic_index_in_dim(proj_part, (place & 1) ^ other, 1, keepdims=False)
        for other in (0, 1)
    )
    proj_got = send_rows(pair_sum(proj_keep, proj_send))
    *dq_far, keep, send = attend_back(meta, q, g, kv, raw, logs, starts[:, None, :], group)

    dkv = (keep + across(send, "dp", 1)).reshape(stride // 2, lines, rows, PAIR)
    dkv, dq_far, proj_got = lax.optimization_barrier((dkv, dq_far, proj_got))
    proj_out = jnp.sum(proj_got.astype(F32), axis=0).T
    for bit in bits_of(stride)[1:]:
        view = dkv.reshape((dkv.shape[0] // 2, 2) + dkv.shape[1:])
        dkv = view[:, 0] + across(view[:, 1], "dp", bit)
    dkv, (moe_part, x_owned, g_owned) = after(dkv[0], (moe_part, x_owned, g_owned))
    dq = from_lines(dq_far)
    dkv = from_lines([dkv[s] for s in range(lines)])
    def mine(x, e):
        return x.reshape((dp, held, CAP) + x.shape[2:])[:, e]

    def pieces_of(parts):
        return [(parts[0], first_col), (parts[1], cols - first_col)]

    def owner_work(x_parts, g_parts):
        if tensor_size == 2:
            x, g = pieces_of(x_parts), pieces_of(g_parts)
        else:
            x, g = [(assemble(x_parts, 2), 0)], [(assemble(g_parts, 2), 0)]
        results = []
        for e in range(held):
            at = jnp.stack([jnp.int32(place * held + e)] + [jnp.int32(o) for _, o in x + g])
            tokens = [mine(a, e) for a, _ in x], [mine(a, e) for a, _ in g]
            gate = mine(gate_owned, e).reshape(dp * CAP, 1)
            hidden_shape = jax.ShapeDtypeStruct((dp * CAP, w_gate.shape[2]), BF)
            given_back = owner_call(
                owner_forward_kernel,
                "owner_forward",
                at,
                gate,
                [],
                *tokens,
                [w_gate, w_up, w_down],
                [hidden_shape] * 3,
                4,
            )
            results.append((at, gate, given_back, *tokens))
        return results

    def owner_grads(owned):
        shapes = [
            jax.ShapeDtypeStruct((1,) + w.shape[1:], F32) for w in (w_gate, w_up, w_down)
        ]
        grad_outs = [
            owner_call(owner_grads_kernel, "owner_grads", at, gate, given, x, g, [], shapes, 2)
            for at, gate, given, x, g in owned
        ]
        return [jnp.concatenate(each, 0) for each in zip(*grad_outs)]

    owned = owner_work(x_owned, g_owned)
    w_all = jnp.concatenate([w_query, w_key, w_value], 1)
    dqkv = jnp.concatenate(dq + [b[:, :HD] for b in dkv] + [b[:, HD:] for b in dkv], 1)
    in_float = layer_in.astype(F32)
    factor_one = norm_factor(in_float)
    unit_one = in_float * factor_one
    dqkv, (owned, moe_rows, unit_one) = after(dqkv, (owned, scatter_tensor(moe_part), unit_one))
    grad_in_part = dot(dqkv, w_all, NT)
    gain_one_part = jnp.sum(grad_in_part * unit_one, axis=0)
    small = jnp.concatenate([router_part, gain_two_part[None], gain_one_part[None]], 0)
    small = total(small.reshape(-1, 128), "dp")
    weight_keep, weight_send = weight_parts(place & 1, normed_in, dqkv, dp)
    weight_pair, (owned, small, grad_in_part) = after(
        pair_sum(weight_keep, weight_send), (owned, small, grad_in_part)
    )
    small = total(small, "tensor")
    owner_outs, small, grad_in_rows = lax.optimization_barrier(
        (owner_grads(owned), small, scatter_tensor(grad_in_part))
    )
    (gate_out, up_out, down_out), weight_got = after(owner_outs, send_rows(weight_pair))
    weight_grad = jnp.sum(weight_got.astype(F32), axis=0)
    layer_out = (hidden + moe_rows).astype(BF)
    ends = [0]
    for size in (lines * q_cols, lines * HD, lines * HD):
        ends.append(ends[-1] + size)
    query_out, key_out, value_out = (weight_grad[:, a:b] for a, b in zip(ends[:-1], ends[1:]))

    factor_rows = lax.dynamic_slice_in_dim(factor_one, first, part, 0)
    unit_rows = lax.dynamic_slice_in_dim(in_float, first, part, 0) * factor_rows
    input_grad = grad_hidden + norm_back(unit_rows, factor_rows, norm1_gain, grad_in_rows)
    small = small.reshape(-1, width)
    gain_one_grad = small[experts + 1]
    gain_two_grad = small[experts]
    router_grad = small[:experts].T

    return (
        layer_out,
        input_grad,
        gain_one_grad,
        query_out,
        key_out,
        value_out,
        proj_out,
        gain_two_grad,
        router_grad,
        gate_out,
        up_out,
        down_out,
    )


def solution(mesh):
    in_specs = (
        P("dp", None),
        P(),
        P(None, "tensor"),
        P(None, "tensor"),
        P(None, "tensor"),
        P("tensor", None),
        P(),
        P(),
        P(None, None, "tensor"),
        P(None, None, "tensor"),
        P(None, "tensor", None),
        P(),
        P("dp", None),
        P("dp", None),
    )
    out_specs = (
        P(("dp", "tensor"), None),
        P(("dp", "tensor"), None),
        P(),
        P("dp", "tensor"),
        P("dp", "tensor"),
        P("dp", "tensor"),
        P("tensor", "dp"),
        P(),
        P(),
        P("dp", None, "tensor"),
        P("dp", None, "tensor"),
        P("dp", "tensor", None),
    )
    return jax.shard_map(shards, mesh=mesh, in_specs=in_specs, out_specs=out_specs, check_vma=False)
```

```python
import functools

import jax
import jax.numpy as jnp
from jax import lax
from jax.experimental import pallas as pl
from jax.experimental.pallas import tpu as pltpu
from jax.sharding import PartitionSpec as P

HD = 64
PAIR = 2 * HD
CAP = 128
DOCS = 8
EPS = 1e-05
HIGH = lax.Precision.HIGHEST
NEG = -1000000000.0
BF = jnp.bfloat16
F32 = jnp.float32

NT = (((1,), (1,)), ((), ()))
TN = (((0,), (0,)), ((), ()))


def dot(a, b, dims=None):
    if dims is None:
        return jnp.dot(a, b, preferred_element_type=F32)
    return lax.dot_general(a, b, dims, preferred_element_type=F32)


def across(x, axis, mask):
    n = lax.axis_size(axis)
    return lax.ppermute(x, axis, [(i, i ^ mask) for i in range(n)])


def bits_of(n):
    return [1 << k for k in range(n.bit_length() - 1)]


def after(x, y):
    return lax.optimization_barrier((x, y))


def to_owner(x):
    return lax.all_to_all(x, "dp", 0, 0, tiled=True)


def norm_factor(value):
    return lax.rsqrt(jnp.mean(value * value, axis=-1, keepdims=True) + EPS)


def norm_back(unit, factor, gain, grad):
    inner = gain * grad
    return factor * (inner - unit * jnp.mean(unit * inner, axis=-1, keepdims=True))


def total(x, axis):
    bits = bits_of(lax.axis_size(axis))

    def met(low, bit):
        return across(low, axis, bit).astype(F32)

    while bits:
        one, *bits = bits
        low = x.astype(BF)
        if bits:
            two, *bits = bits
            far, both = met(low, two), met(low, one | two)
            x = (low.astype(F32) + met(low, one)) + (far + both)
        else:
            x = low.astype(F32) + met(low, one)
    return x


def scatter_tensor(x):
    n = lax.axis_size("tensor")
    if n != 2:
        return lax.psum_scatter(x.astype(BF), "tensor", scatter_dimension=0, tiled=True).astype(F32)
    me = lax.axis_index("tensor")
    part = x.shape[0] // 2
    sent = lax.dynamic_slice_in_dim(x, (1 - me) * part, part, 0).astype(BF)
    own = lax.dynamic_slice_in_dim(x, me * part, part, 0)
    return own.astype(F32) + across(sent, "tensor", 1).astype(F32)


def swap_tensor(x, dim):
    if lax.axis_size("tensor") != 2:
        return (lax.all_gather(x, "tensor", axis=dim, tiled=True),)
    return x, across(x, "tensor", 1)


def assemble(parts, dim):
    if len(parts) == 1:
        return parts[0]
    own, other = parts
    low = lax.axis_index("tensor") == 0
    return jnp.concatenate([jnp.where(low, own, other), jnp.where(low, other, own)], dim)


def gather_tensor(x, dim):
    return assemble(swap_tensor(x, dim), dim)


def xor_blocks(blocks, index):
    for bit in bits_of(len(blocks)):
        crossed = (index & bit) != 0
        blocks = [jnp.where(crossed, blocks[s ^ bit], block) for s, block in enumerate(blocks)]
    return blocks


def columns_of(x, count):
    size = x.shape[1] // count
    return [x[:, s * size : (s + 1) * size] for s in range(count)]


def pair_sum(keep, send):
    return keep + across(send, "dp", 1)


def send_rows(x):
    n = lax.axis_size("dp")
    groups = [list(range(first, n, 2)) for first in range(2)]
    return lax.all_to_all(x, "dp", 0, 0, tiled=True, axis_index_groups=groups)


def project_kernel(lines, q_cols, at, x_ref, gain_ref, wq_ref, wk_ref, wv_ref, normed_ref, *rest):
    kv_refs, q_refs = rest[:lines], rest[lines : 2 * lines]
    kv_s, q_s = rest[2 * lines :]
    x = x_ref[...].astype(F32)
    scale = lax.rsqrt(jnp.mean(x * x, axis=-1, keepdims=True) + EPS)
    normed = (x * scale * gain_ref[...]).astype(BF)
    normed_ref[...] = normed
    key = dot(normed, wk_ref[...])
    value = dot(normed, wv_ref[...])
    query = dot(normed, wq_ref[...])
    for c in range(lines):
        pair = [key[:, c * HD : (c + 1) * HD], value[:, c * HD : (c + 1) * HD]]
        kv_s[c] = jnp.concatenate(pair, 1).astype(BF)
        q_s[c] = query[:, c * q_cols : (c + 1) * q_cols].astype(BF) * jnp.asarray(0.125, BF)
    for s in range(lines):
        kv_refs[s][...] = kv_s[s ^ at[0]]
        q_refs[s][...] = q_s[s ^ at[0]]


def project(line, x, gain, w_query, w_key, w_value, lines):
    rows, width = x.shape
    q_cols = w_query.shape[1] // lines

    def whole(*shape):
        return pl.BlockSpec(shape, lambda i, m: (0,) * len(shape))

    out = [(rows, width)] + [(rows, PAIR)] * lines + [(rows, q_cols)] * lines
    outs = pl.pallas_call(
        functools.partial(project_kernel, lines, q_cols),
        grid_spec=pltpu.PrefetchScalarGridSpec(
            num_scalar_prefetch=1,
            grid=(1,),
            in_specs=[
                whole(rows, width),
                whole(1, width),
                whole(*w_query.shape),
                whole(*w_key.shape),
                whole(*w_value.shape),
            ],
            out_specs=[whole(*shape) for shape in out],
            scratch_shapes=[
                pltpu.VMEM((lines, rows, PAIR), BF),
                pltpu.VMEM((lines, rows, q_cols), BF),
            ],
        ),
        out_shape=[jax.ShapeDtypeStruct(shape, BF) for shape in out],
        compiler_params=pltpu.CompilerParams(vmem_limit_bytes=48 * 1024 * 1024),
        cost_estimate=pl.CostEstimate(
            flops=2 * rows * width * (w_query.shape[1] + 2 * w_key.shape[1]),
            bytes_accessed=8 << 20,
            transcendentals=0,
        ),
        name="project",
    )(line[None], x, gain[None], w_query, w_key, w_value)
    return outs[0], outs[1 : 1 + lines], outs[1 + lines :]


def spread_heads(refs, out, heads, high):
    for s, ref in enumerate(refs):
        x = ref[...]
        zero = jnp.zeros((x.shape[0], HD), BF)
        for h in range(heads):
            one = x[:, h * HD : (h + 1) * HD]
            out[s, h] = jnp.concatenate([zero, one] if high else [one, zero], 1)


def gather_blocks(refs, out, lines):
    for m, ref in enumerate(refs):
        out[m * lines : (m + 1) * lines] = ref[...]


def position(meta, lines):
    slot = pl.program_id(0)
    return slot, meta[0], meta[1 + slot], meta[1 + lines + slot], meta[1 + 2 * lines + slot]


def walk(low, clear, own, step):
    def body(blk, carry):
        full = (blk >= clear) & (blk < own)

        @pl.when(full)
        def _():
            step(blk, False)

        @pl.when(jnp.logical_not(full))
        def _():
            step(blk, True)

        return carry

    lax.fori_loop(low, own + 1, body, 0)


def visible(blk, own, rows, start):
    key_pos = lax.broadcasted_iota(jnp.int32, (rows, rows), 0) + blk * rows
    q_pos = lax.broadcasted_iota(jnp.int32, (rows, rows), 1) + own * rows
    return (key_pos >= start) & (key_pos <= q_pos)


def attend_kernel(heads, rows, lines, stride, meta, *refs):
    q_refs, kv_refs, start_ref = refs[:lines], refs[lines : lines + stride], refs[lines + stride]
    outs = refs[lines + stride + 1 :]
    mixed_refs, (raw_ref, log_ref, q_s, kv_s, m_s, l_s, acc_s) = outs[:lines], outs[lines:]
    slot, place, own, low, clear = position(meta, lines)

    @pl.when(slot == 0)
    def _():
        spread_heads(q_refs, q_s, heads, False)
        gather_blocks(kv_refs, kv_s, lines)

    m_s[...] = jnp.full_like(m_s, -3e38)
    l_s[...] = jnp.zeros_like(l_s)
    acc_s[...] = jnp.zeros_like(acc_s)

    def step(blk, masked):
        x = blk ^ place
        index = (x % stride) * lines + x // stride
        kv = kv_s[index]
        if masked:
            seen = visible(blk, own, rows, start_ref[0])
        each = range(heads)
        scores = [dot(kv, q_s[slot, h], NT) for h in each]
        if masked:
            scores = [jnp.where(seen, s, NEG) for s in scores]
        m_old = [m_s[h : h + 1, :] for h in each]
        m_new = [jnp.maximum(m_old[h], jnp.max(scores[h], axis=0, keepdims=True)) for h in each]
        p = [jnp.exp(scores[h] - m_new[h]) for h in each]
        alpha = [jnp.exp(m_old[h] - m_new[h]) for h in each]
        added = [dot(kv, p[h].astype(BF), TN) for h in each]
        for h in each:
            l_s[h : h + 1, :] = l_s[h : h + 1, :] * alpha[h] + jnp.sum(p[h], axis=0, keepdims=True)
            acc_s[h] = acc_s[h] * alpha[h] + added[h]
            m_s[h : h + 1, :] = m_new[h]

    walk(low, clear, own, step)
    parts = []
    for h in range(heads):
        out = (acc_s[h] / l_s[h : h + 1, :]).T
        raw_ref[0, h] = out
        parts.append(out[:, HD:])
    log_ref[0] = m_s[...] + jnp.log(l_s[...])
    mixed = jnp.concatenate(parts, 1).astype(BF)
    for s in range(lines):

        @pl.when(slot == s)
        def _(s=s):
            mixed_refs[s][...] = mixed


def whole_block(shape):
    return pl.BlockSpec(shape, lambda i, m: (0,) * len(shape))


def attend(meta, q, kv, start_row, heads):
    lines, stride = len(q), len(kv)
    rows, q_cols = q[0].shape
    narrow = whole_block((rows, q_cols))
    return pl.pallas_call(
        functools.partial(attend_kernel, heads, rows, lines, stride),
        grid_spec=pltpu.PrefetchScalarGridSpec(
            num_scalar_prefetch=1,
            grid=(lines,),
            in_specs=[narrow] * lines
            + [whole_block((lines, rows, PAIR))] * stride
            + [pl.BlockSpec((1, 1, rows), lambda i, m: (i, 0, 0))],
            out_specs=[narrow] * lines
            + [
                pl.BlockSpec((1, heads, rows, PAIR), lambda i, m: (i, 0, 0, 0)),
                pl.BlockSpec((1, 8, rows), lambda i, m: (i, 0, 0)),
            ],
            scratch_shapes=[
                pltpu.VMEM((lines, heads, rows, PAIR), BF),
                pltpu.VMEM((stride * lines, rows, PAIR), BF),
                pltpu.VMEM((8, rows), F32),
                pltpu.VMEM((8, rows), F32),
                pltpu.VMEM((heads, PAIR, rows), F32),
            ],
        ),
        out_shape=[jax.ShapeDtypeStruct((rows, q_cols), BF)] * lines
        + [
            jax.ShapeDtypeStruct((lines, heads, rows, PAIR), F32),
            jax.ShapeDtypeStruct((lines, 8, rows), F32),
        ],
        compiler_params=pltpu.CompilerParams(vmem_limit_bytes=48 * 1024 * 1024),
        cost_estimate=pl.CostEstimate(
            flops=36 * 4 * rows * rows * PAIR * 2, bytes_accessed=8 << 20, transcendentals=36 * rows * rows
        ),
        name="attend",
    )(meta, *q, *kv, start_row)


def attend_back_kernel(heads, rows, lines, stride, meta, *refs):
    q_refs, g_ref, kv_refs = refs[:lines], refs[lines], refs[lines + 1 : lines + 1 + stride]
    raw_ref, log_ref, start_ref = refs[lines + 1 + stride : lines + stride + 4]
    outs = refs[lines + stride + 4 :]
    dq_ref, keep_ref, send_ref, q_s, g_s, kv_s, dq_s, dkv_s, delta_s = outs
    slot, place, own, low, clear = position(meta, lines)

    @pl.when(slot == 0)
    def _():
        spread_heads(q_refs, q_s, heads, False)
        spread_heads([g_ref.at[s ^ (place // stride)] for s in range(lines)], g_s, heads, True)
        gather_blocks(kv_refs, kv_s, lines)
        dkv_s[...] = jnp.zeros_like(dkv_s)

    dq_s[...] = jnp.zeros_like(dq_s)
    for h in range(heads):
        prod = raw_ref[0, h] * g_s[slot, h].astype(F32)
        delta_s[h : h + 1, :] = jnp.sum(prod.T, axis=0, keepdims=True)

    def step(blk, masked):
        x = blk ^ place
        index = (x % stride) * lines + x // stride
        kv = kv_s[index]
        if masked:
            seen = visible(blk, own, rows, start_ref[0])
        for h in range(heads):
            q = q_s[slot, h]
            g = g_s[slot, h]
            s = dot(kv, q, NT)
            if masked:
                s = jnp.where(seen, s, NEG)
            p = jnp.exp(s - log_ref[0, h : h + 1, :])
            gp = dot(kv, g, NT)
            gs = (p * (gp - delta_s[h : h + 1, :])).astype(BF)
            part = dot(gs, q) + dot(p.astype(BF), g)
            dkv_s[index] += part
            dq_s[h] += dot(gs, kv, TN)

    walk(low, clear, own, step)
    dq_ref[0] = jnp.concatenate([dq_s[h][:, :HD] * 0.125 for h in range(heads)], 1).astype(BF)

    @pl.when(slot == lines - 1)
    def _():
        for m in range(stride):
            half = m // 2
            out = send_ref if m % 2 else keep_ref
            out[half * lines : (half + 1) * lines] = dkv_s[m * lines : (m + 1) * lines].astype(BF)


def attend_back(meta, q, g, kv, raw, logs, start_row, heads):
    lines, stride = len(q), len(kv)
    rows, q_cols = q[0].shape
    blocks = lines * stride
    narrow = whole_block((rows, q_cols))
    half = whole_block((blocks // 2, rows, PAIR))
    shift = stride.bit_length() - 1

    def own_line(i, m):
        return i ^ (m[0] >> shift), 0, 0

    return pl.pallas_call(
        functools.partial(attend_back_kernel, heads, rows, lines, stride),
        grid_spec=pltpu.PrefetchScalarGridSpec(
            num_scalar_prefetch=1,
            grid=(lines,),
            in_specs=[narrow] * lines
            + [whole_block((lines, rows, q_cols))]
            + [whole_block((lines, rows, PAIR))] * stride
            + [
                pl.BlockSpec((1, heads, rows, PAIR), lambda i, m: (i, 0, 0, 0)),
                pl.BlockSpec((1, 8, rows), lambda i, m: (i, 0, 0)),
                pl.BlockSpec((1, 1, rows), lambda i, m: (i, 0, 0)),
            ],
            out_specs=[pl.BlockSpec((1, rows, q_cols), own_line)] + [half] * 2,
            scratch_shapes=[
                pltpu.VMEM((lines, heads, rows, PAIR), BF),
                pltpu.VMEM((lines, heads, rows, PAIR), BF),
                pltpu.VMEM((blocks, rows, PAIR), BF),
                pltpu.VMEM((heads, rows, PAIR), F32),
                pltpu.VMEM((blocks, rows, PAIR), F32),
                pltpu.VMEM((8, rows), F32),
            ],
        ),
        out_shape=[jax.ShapeDtypeStruct((lines, rows, q_cols), BF)]
        + [jax.ShapeDtypeStruct((blocks // 2, rows, PAIR), BF)] * 2,
        compiler_params=pltpu.CompilerParams(vmem_limit_bytes=56 * 1024 * 1024),
        cost_estimate=pl.CostEstimate(
            flops=36 * 10 * rows * rows * PAIR * 2, bytes_accessed=10 << 20, transcendentals=36 * rows * rows
        ),
        name="attend_back",
    )(meta, *q, g, *kv, raw, logs, start_row)


def experts_kernel(x_ref, g_ref, gate_ref, wg_ref, wu_ref, wd_ref, out_ref, back_ref, inner_ref):
    each = range(x_ref.shape[0])
    cap = x_ref.shape[1]
    gate_pre = [dot(x_ref[i], wg_ref[i]) for i in each]
    grad_expert = [(gate_ref[i] * g_ref[i].astype(F32)).astype(BF) for i in each]
    grad_act = [dot(grad_expert[i], wd_ref[i], NT) for i in each]
    up_pre = [dot(x_ref[i], wu_ref[i]) for i in each]
    sigma = [jax.nn.sigmoid(gate_pre[i]) for i in each]
    silu = [gate_pre[i] * sigma[i] for i in each]
    act = [(silu[i] * up_pre[i]).astype(BF) for i in each]
    grad_gate = [
        (grad_act[i] * up_pre[i] * sigma[i] * (1.0 + gate_pre[i] * (1.0 - sigma[i]))).astype(BF)
        for i in each
    ]
    grad_up = [(grad_act[i] * silu[i]).astype(BF) for i in each]
    for i in each:
        out = dot(act[i], wd_ref[i])
        inner = jnp.sum(out * g_ref[i].astype(F32), axis=-1, keepdims=True)
        inner_ref[i] = jnp.broadcast_to(inner, (cap, 128)).T[:8]
        out_ref[i] = (gate_ref[i] * out).astype(BF)
        back_ref[i] = (dot(grad_gate[i], wg_ref[i], NT) + dot(grad_up[i], wu_ref[i], NT)).astype(BF)


def run_experts(x, g, gate, w_gate, w_up, w_down):
    experts, cap, width = x.shape
    hidden = w_gate.shape[2]
    at_once = 2 if experts % 2 == 0 else 1

    def of(*shape):
        return pl.BlockSpec((at_once,) + shape, lambda e: (e, 0, 0))

    return pl.pallas_call(
        experts_kernel,
        grid=(experts // at_once,),
        in_specs=[
            of(cap, width),
            of(cap, width),
            of(cap, 1),
            of(width, hidden),
            of(width, hidden),
            of(hidden, width),
        ],
        out_specs=[of(cap, width), of(cap, width), of(8, cap)],
        out_shape=[
            jax.ShapeDtypeStruct((experts, cap, width), BF),
            jax.ShapeDtypeStruct((experts, cap, width), BF),
            jax.ShapeDtypeStruct((experts, 8, cap), F32),
        ],
        compiler_params=pltpu.CompilerParams(vmem_limit_bytes=56 * 1024 * 1024),
        cost_estimate=pl.CostEstimate(
            flops=experts * cap * width * hidden * 12,
            bytes_accessed=experts * width * (hidden * 6 + cap * 8),
            transcendentals=experts * cap * hidden,
        ),
        name="experts",
    )(x, g, gate, w_gate, w_up, w_down)


def weights_kernel(dp, at, a_ref, b_ref, keep_ref, send_ref):
    size = a_ref.shape[1] // dp
    chunk = 4
    odd = at[0] != 0
    for part in range(dp // chunk):
        span = slice(part * chunk * size, (part + 1) * chunk * size)
        block = dot(a_ref[:, span], b_ref[...], TN).astype(BF)
        for pair in range(chunk // 2):
            one = block[2 * pair * size : (2 * pair + 1) * size]
            two = block[(2 * pair + 1) * size : (2 * pair + 2) * size]
            at_pair = part * (chunk // 2) + pair
            keep_ref[at_pair] = jnp.where(odd, two, one)
            send_ref[at_pair] = jnp.where(odd, one, two)


def weight_parts(bit, a, b, dp):
    rows, width = a.shape
    columns = b.shape[1]
    out = (dp // 2, width // dp, columns)
    return pl.pallas_call(
        functools.partial(weights_kernel, dp),
        grid_spec=pltpu.PrefetchScalarGridSpec(
            num_scalar_prefetch=1,
            grid=(1,),
            in_specs=[whole_block(x.shape) for x in (a, b)],
            out_specs=[whole_block(out)] * 2,
        ),
        out_shape=[jax.ShapeDtypeStruct(out, BF)] * 2,
        compiler_params=pltpu.CompilerParams(vmem_limit_bytes=48 * 1024 * 1024),
        cost_estimate=pl.CostEstimate(
            flops=2 * rows * width * columns, bytes_accessed=8 << 20, transcendentals=0
        ),
        name="weights",
    )(bit[None], a, b)


def flat(x):
    return x.reshape(x.shape[0] * x.shape[1], x.shape[2])


def owner_forward_kernel(n_x, n_g, at, gate_ref, wg_ref, wu_ref, wd_ref, *refs):
    x_refs, g_refs, outs = refs[:n_x], refs[n_x : n_x + n_g], refs[n_x + n_g :]
    act_ref, grad_gate_ref, grad_up_ref = outs

    def span(i, ref):
        return pl.ds(pl.multiple_of(at[1 + i], ref.shape[2]), ref.shape[2])

    gate_pre = sum(dot(flat(x[...]), wg_ref[0, span(i, x), :]) for i, x in enumerate(x_refs))
    up_pre = sum(dot(flat(x[...]), wu_ref[0, span(i, x), :]) for i, x in enumerate(x_refs))
    grad_act = sum(
        dot(
            (gate_ref[...] * flat(g[...]).astype(F32)).astype(BF),
            wd_ref[0, :, span(n_x + i, g)],
            NT,
        )
        for i, g in enumerate(g_refs)
    )
    sigma = jax.nn.sigmoid(gate_pre)
    silu = gate_pre * sigma
    act_ref[...] = (silu * up_pre).astype(BF)
    grad_gate_ref[...] = (
        grad_act * up_pre * sigma * (1.0 + gate_pre * (1.0 - sigma))
    ).astype(BF)
    grad_up_ref[...] = (grad_act * silu).astype(BF)


def owner_grads_kernel(n_x, n_g, at, gate_ref, act_ref, grad_gate_ref, grad_up_ref, *refs):
    x_refs, g_refs, outs = refs[:n_x], refs[n_x : n_x + n_g], refs[n_x + n_g :]
    gate_out, up_out, down_out = outs

    def span(i, ref):
        return pl.ds(pl.multiple_of(at[1 + i], ref.shape[2]), ref.shape[2])

    @pl.when(pl.program_id(0) == 0)
    def _():
        for out in outs:
            out[...] = jnp.zeros_like(out)

    for i, ref in enumerate(x_refs):
        x = flat(ref[...])
        gate_out[0, span(i, ref), :] += dot(x, grad_gate_ref[...], TN)
        up_out[0, span(i, ref), :] += dot(x, grad_up_ref[...], TN)
    for i, ref in enumerate(g_refs):
        grad_expert = (gate_ref[...] * flat(ref[...]).astype(F32)).astype(BF)
        down_out[0, :, span(n_x + i, ref)] += dot(act_ref[...], grad_expert, TN)


def owner_call(kernel, name, at, gate, given, x, g, weights, outs, steps):
    dp, cap, _ = x[0].shape
    rows = dp * cap // steps

    def rowwise(a):
        return pl.BlockSpec((rows, a.shape[1]), lambda i, m: (i, 0))

    def piece(a):
        return pl.BlockSpec((dp // steps, cap, a.shape[2]), lambda i, m: (i, 0, 0))

    def weight(a):
        return pl.BlockSpec((1,) + a.shape[1:], lambda i, m: (m[0], 0, 0))

    out_specs = [rowwise(o) if len(o.shape) == 2 else whole_block(o.shape) for o in outs]
    return pl.pallas_call(
        functools.partial(kernel, len(x), len(g)),
        grid_spec=pltpu.PrefetchScalarGridSpec(
            num_scalar_prefetch=1,
            grid=(steps,),
            in_specs=[rowwise(gate)]
            + [rowwise(a) for a in given]
            + [weight(w) for w in weights]
            + [piece(a) for a in list(x) + list(g)],
            out_specs=out_specs,
        ),
        out_shape=outs,
        compiler_params=pltpu.CompilerParams(vmem_limit_bytes=58 * 1024 * 1024),
        cost_estimate=pl.CostEstimate(flops=10 << 30, bytes_accessed=24 << 20, transcendentals=1 << 20),
        name=name,
    )(at, gate, *given, *weights, *x, *g)


def shards(
    layer_in,
    norm1_gain,
    w_query,
    w_key,
    w_value,
    w_out,
    norm2_gain,
    router,
    w_gate,
    w_up,
    w_down,
    segments,
    routes,
    out_grad,
):
    rows, width = layer_in.shape
    kv_heads = w_key.shape[1] // HD
    group = w_query.shape[1] // HD // kv_heads
    q_cols = group * HD
    experts = w_gate.shape[0]
    dp = lax.axis_size("dp")
    place = lax.axis_index("dp")
    tensor_size = lax.axis_size("tensor")
    tensor_at = lax.axis_index("tensor")
    lines = kv_heads
    stride = dp // lines
    line = place >> (stride.bit_length() - 1)
    part = rows // tensor_size
    first = tensor_at * part
    held = experts // dp
    cols = width // tensor_size
    first_col = tensor_at * cols

    names = jnp.arange(experts, dtype=jnp.int32)
    named = jnp.any(routes[:, :, None] == names[None, None, :], axis=1)
    earlier = jnp.tril(jnp.ones((rows, rows), BF), -1)
    slots = jnp.where(named, dot(earlier, named.astype(BF)).astype(jnp.int32), -1)
    in_slot = slots.T[:, None, :] == jnp.arange(CAP, dtype=jnp.int32)[None, :, None]
    to_slots = in_slot.astype(BF).reshape(experts * CAP, rows)
    from_slots = (
        (slots[:, :, None] == jnp.arange(CAP, dtype=jnp.int32)[None, None, :])
        .astype(BF)
        .reshape(rows, experts * CAP)
    )

    def to_experts(x):
        return dot(to_slots, x).astype(BF).reshape(experts, CAP, -1)

    def half(x, i):
        size = cols // 2
        return to_experts(lax.dynamic_slice_in_dim(x, tensor_at * cols + i * size, size, 1))

    q_blocks = place ^ (jnp.arange(lines, dtype=jnp.int32) * stride)
    seg_query = jnp.stack(
        [lax.dynamic_slice_in_dim(segments, q_blocks[s] * rows, rows, 0) for s in range(lines)]
    )
    documents = jnp.arange(DOCS, dtype=jnp.int32)
    lengths_before = jnp.sum(
        (segments[None, :] < documents[:, None]).astype(jnp.int32), axis=1
    )
    starts = jnp.sum(
        jnp.where(seg_query[None] == documents[:, None, None], lengths_before[:, None, None], 0),
        axis=0,
    )
    shift = rows.bit_length() - 1
    meta = jnp.concatenate(
        [place[None], q_blocks, starts[:, 0] >> shift, (starts[:, -1] + rows - 1) >> shift]
    ).astype(jnp.int32)

    normed_in, kv_mine, q_mine = project(line, layer_in, norm1_gain, w_query, w_key, w_value, lines)

    def to_lines(blocks):
        return [b if s == 0 else across(b, "dp", s * stride) for s, b in enumerate(blocks)]

    kv = [jnp.stack(to_lines(kv_mine))]
    q = to_lines(q_mine)
    for bit in reversed(bits_of(stride)):
        kv = [piece for one in kv for piece in (one, across(one, "dp", bit))]
    g_sent, (kv, q, starts, meta) = after([half(out_grad, i) for i in range(2)], (kv, q, starts, meta))
    g_first = to_owner(g_sent[0])
    *mixed_far, raw, logs = attend(meta, q, kv, starts[:, None, :], group)
    mixed_far, g_first = after(mixed_far, g_first)

    def between_lines(x):
        if lines == 1:
            return x
        groups = [[low + j * stride for j in range(lines)] for low in range(stride)]
        return lax.all_to_all(x, "dp", 0, 0, tiled=True, axis_index_groups=groups)

    def from_lines(blocks):
        return xor_blocks(to_lines(blocks), line)

    mixed = jnp.concatenate(from_lines(mixed_far), 1)
    g_late, (mixed, g_slots) = after(g_sent[1], (mixed, to_experts(out_grad)))
    g_second = to_owner(g_late)
    attn = scatter_tensor(dot(mixed, w_out))
    hidden = lax.dynamic_slice_in_dim(layer_in, first, part, 0).astype(F32) + attn
    factor_two = norm_factor(hidden)
    unit_two = hidden * factor_two
    normed_mid = gather_tensor((unit_two * norm2_gain).astype(BF), 0)
    normed_mid, g_second = after(normed_mid, g_second)

    logits = dot(normed_mid, router)
    peak = jnp.max(jnp.where(named, logits, -jnp.inf), axis=1, keepdims=True)
    expo = jnp.where(named, jnp.exp(jnp.where(named, logits - peak, 0.0)), 0.0)
    gates = expo / jnp.sum(expo, axis=1, keepdims=True)
    slot_gate = jnp.sum(jnp.where(in_slot, gates.T[:, None, :], 0.0), axis=-1)

    x_slots = to_experts(normed_mid)
    gate_high = lax.reduce_precision(slot_gate, 8, 7)
    gate_mid = lax.reduce_precision(slot_gate - gate_high, 8, 7)
    gate_pieces = jnp.stack([gate_high, gate_mid, slot_gate - gate_high - gate_mid], 2)
    x_mine = lax.dynamic_slice_in_dim(x_slots, first_col, cols, 2)
    early = cols // 2
    x_late = x_mine[..., early:]
    x_first = to_owner(x_mine[..., :early])
    g_owned = swap_tensor(jnp.concatenate([g_first, g_second], 2), 2)

    out_slots, back_slots, inner_slots = run_experts(
        x_slots, g_slots, slot_gate[:, :, None], w_gate, w_up, w_down
    )
    back_slots, (x_first, g_owned) = after(back_slots, (x_first, g_owned))
    moe_part = dot(from_slots, out_slots.reshape(experts * CAP, width))
    grad_gates = jnp.sum(
        jnp.where(
            slots[:, :, None] == jnp.arange(CAP, dtype=jnp.int32)[None, None, :],
            inner_slots[None, :, 0, :],
            0.0,
        ),
        axis=-1,
    )
    grad_logits = gates * (grad_gates - jnp.sum(gates * grad_gates, axis=-1, keepdims=True))
    grad_mid_part = dot(from_slots, back_slots.reshape(experts * CAP, width)) + lax.dot_general(
        grad_logits, router.astype(F32), NT, precision=HIGH, preferred_element_type=F32
    )
    (x_late, gate_pieces, router_part), grad_mid_part = after(
        (x_late, gate_pieces, (grad_logits, normed_mid)), grad_mid_part
    )
    x_second = to_owner(
        jnp.concatenate([x_late, jnp.pad(gate_pieces.astype(BF), ((0, 0), (0, 0), (0, 125)))], 2)
    )
    router_part = lax.dot_general(
        router_part[0], router_part[1].astype(F32), TN, precision=HIGH, preferred_element_type=F32
    )
    grad_mid, moe_part = after(scatter_tensor(grad_mid_part), moe_part)
    gain_two_part = jnp.sum(grad_mid * unit_two, axis=0)
    grad_rows = lax.dynamic_slice_in_dim(out_grad, first, part, 0).astype(F32)
    grad_hidden = grad_rows + norm_back(unit_two, factor_two, norm2_gain, grad_mid)
    hidden_low = gather_tensor(grad_hidden.astype(BF), 0)
    grad_mixed = dot(hidden_low, w_out, NT).astype(BF)
    g = jnp.stack(columns_of(grad_mixed, lines))
    g, (x_first, x_second, hidden_late) = after(g, (x_first, x_second, hidden_low))
    g = between_lines(g)
    gate_owned = jnp.sum(x_second[..., cols - early : cols - early + 3].astype(F32), axis=2)
    x_owned = swap_tensor(jnp.concatenate([x_first, x_second[..., : cols - early]], 2), 2)
    proj_part = dot(hidden_late, mixed, TN).astype(BF).reshape(dp // 2, 2, width // dp, -1)
    proj_keep, proj_send = (
        lax.dynamic_index_in_dim(proj_part, (place & 1) ^ other, 1, keepdims=False)
        for other in (0, 1)
    )
    proj_got = send_rows(pair_sum(proj_keep, proj_send))
    dq, keep, send = attend_back(meta, q, g, kv, raw, logs, starts[:, None, :], group)

    dkv = (keep + across(send, "dp", 1)).reshape(stride // 2, lines, rows, PAIR)
    dkv, dq, proj_got = lax.optimization_barrier((dkv, dq, proj_got))
    proj_out = jnp.sum(proj_got.astype(F32), axis=0).T
    for bit in bits_of(stride)[1:]:
        view = dkv.reshape((dkv.shape[0] // 2, 2) + dkv.shape[1:])
        dkv = view[:, 0] + across(view[:, 1], "dp", bit)
    dkv, (moe_part, x_owned, g_owned) = after(dkv[0], (moe_part, x_owned, g_owned))
    dq = between_lines(dq)
    dq = [dq[c] for c in range(lines)]
    dkv = from_lines([dkv[s] for s in range(lines)])
    def mine(x, e):
        return x.reshape((dp, held, CAP) + x.shape[2:])[:, e]

    def pieces_of(parts):
        return [(parts[0], first_col), (parts[1], cols - first_col)]

    def owner_work(x_parts, g_parts):
        if tensor_size == 2:
            x, g = pieces_of(x_parts), pieces_of(g_parts)
        else:
            x, g = [(assemble(x_parts, 2), 0)], [(assemble(g_parts, 2), 0)]
        results = []
        for e in range(held):
            at = jnp.stack([jnp.int32(place * held + e)] + [jnp.int32(o) for _, o in x + g])
            tokens = [mine(a, e) for a, _ in x], [mine(a, e) for a, _ in g]
            gate = mine(gate_owned, e).reshape(dp * CAP, 1)
            hidden_shape = jax.ShapeDtypeStruct((dp * CAP, w_gate.shape[2]), BF)
            given_back = owner_call(
                owner_forward_kernel,
                "owner_forward",
                at,
                gate,
                [],
                *tokens,
                [w_gate, w_up, w_down],
                [hidden_shape] * 3,
                4,
            )
            results.append((at, gate, given_back, *tokens))
        return results

    def owner_grads(owned):
        shapes = [
            jax.ShapeDtypeStruct((1,) + w.shape[1:], F32) for w in (w_gate, w_up, w_down)
        ]
        grad_outs = [
            owner_call(owner_grads_kernel, "owner_grads", at, gate, given, x, g, [], shapes, 2)
            for at, gate, given, x, g in owned
        ]
        return [jnp.concatenate(each, 0) for each in zip(*grad_outs)]

    owned = owner_work(x_owned, g_owned)
    w_all = jnp.concatenate([w_query, w_key, w_value], 1)
    dqkv = jnp.concatenate(dq + [b[:, :HD] for b in dkv] + [b[:, HD:] for b in dkv], 1)
    in_float = layer_in.astype(F32)
    factor_one = norm_factor(in_float)
    unit_one = in_float * factor_one
    dqkv, (owned, moe_rows, unit_one) = after(dqkv, (owned, scatter_tensor(moe_part), unit_one))
    grad_in_part = dot(dqkv, w_all, NT)
    gain_one_part = jnp.sum(grad_in_part * unit_one, axis=0)
    small = jnp.concatenate([router_part, gain_two_part[None], gain_one_part[None]], 0)
    small = total(small.reshape(-1, 128), "dp")
    weight_keep, weight_send = weight_parts(place & 1, normed_in, dqkv, dp)
    weight_pair, (owned, small, grad_in_part) = after(
        pair_sum(weight_keep, weight_send), (owned, small, grad_in_part)
    )
    small = total(small, "tensor")
    owner_outs, small, grad_in_rows = lax.optimization_barrier(
        (owner_grads(owned), small, scatter_tensor(grad_in_part))
    )
    (gate_out, up_out, down_out), weight_got = after(owner_outs, send_rows(weight_pair))
    weight_grad = jnp.sum(weight_got.astype(F32), axis=0)
    layer_out = (hidden + moe_rows).astype(BF)
    ends = [0]
    for size in (lines * q_cols, lines * HD, lines * HD):
        ends.append(ends[-1] + size)
    query_out, key_out, value_out = (weight_grad[:, a:b] for a, b in zip(ends[:-1], ends[1:]))

    factor_rows = lax.dynamic_slice_in_dim(factor_one, first, part, 0)
    unit_rows = lax.dynamic_slice_in_dim(in_float, first, part, 0) * factor_rows
    input_grad = grad_hidden + norm_back(unit_rows, factor_rows, norm1_gain, grad_in_rows)
    small = small.reshape(-1, width)
    gain_one_grad = small[experts + 1]
    gain_two_grad = small[experts]
    router_grad = small[:experts].T

    return (
        layer_out,
        input_grad,
        gain_one_grad,
        query_out,
        key_out,
        value_out,
        proj_out,
        gain_two_grad,
        router_grad,
        gate_out,
        up_out,
        down_out,
    )


def solution(mesh):
    in_specs = (
        P("dp", None),
        P(),
        P(None, "tensor"),
        P(None, "tensor"),
        P(None, "tensor"),
        P("tensor", None),
        P(),
        P(),
        P(None, None, "tensor"),
        P(None, None, "tensor"),
        P(None, "tensor", None),
        P(),
        P("dp", None),
        P("dp", None),
    )
    out_specs = (
        P(("dp", "tensor"), None),
        P(("dp", "tensor"), None),
        P(),
        P("dp", "tensor"),
        P("dp", "tensor"),
        P("dp", "tensor"),
        P("tensor", "dp"),
        P(),
        P(),
        P("dp", None, "tensor"),
        P("dp", None, "tensor"),
        P("dp", "tensor", None),
    )
    return jax.shard_map(shards, mesh=mesh, in_specs=in_specs, out_specs=out_specs, check_vma=False)
```

```python
import functools

import jax
import jax.numpy as jnp
from jax import lax
from jax.experimental import pallas as pl
from jax.experimental.pallas import tpu as pltpu
from jax.sharding import PartitionSpec as P

HD = 64
PAIR = 2 * HD
CAP = 128
DOCS = 8
EPS = 1e-05
HIGH = lax.Precision.HIGHEST
NEG = -1000000000.0
BF = jnp.bfloat16
F32 = jnp.float32

NT = (((1,), (1,)), ((), ()))
TN = (((0,), (0,)), ((), ()))


def dot(a, b, dims=None):
    if dims is None:
        return jnp.dot(a, b, preferred_element_type=F32)
    return lax.dot_general(a, b, dims, preferred_element_type=F32)


def across(x, axis, mask):
    n = lax.axis_size(axis)
    return lax.ppermute(x, axis, [(i, i ^ mask) for i in range(n)])


def bits_of(n):
    return [1 << k for k in range(n.bit_length() - 1)]


def after(x, y):
    return lax.optimization_barrier((x, y))


def to_owner(x):
    return lax.all_to_all(x, "dp", 0, 0, tiled=True)


def norm_factor(value):
    return lax.rsqrt(jnp.mean(value * value, axis=-1, keepdims=True) + EPS)


def norm_back(unit, factor, gain, grad):
    inner = gain * grad
    return factor * (inner - unit * jnp.mean(unit * inner, axis=-1, keepdims=True))


def total(x, axis):
    bits = bits_of(lax.axis_size(axis))

    def met(low, bit):
        return across(low, axis, bit).astype(F32)

    while bits:
        one, *bits = bits
        low = x.astype(BF)
        if bits:
            two, *bits = bits
            far, both = met(low, two), met(low, one | two)
            x = (low.astype(F32) + met(low, one)) + (far + both)
        else:
            x = low.astype(F32) + met(low, one)
    return x


def scatter_tensor(x):
    n = lax.axis_size("tensor")
    if n != 2:
        return lax.psum_scatter(x.astype(BF), "tensor", scatter_dimension=0, tiled=True).astype(F32)
    me = lax.axis_index("tensor")
    part = x.shape[0] // 2
    sent = lax.dynamic_slice_in_dim(x, (1 - me) * part, part, 0).astype(BF)
    own = lax.dynamic_slice_in_dim(x, me * part, part, 0)
    return own.astype(F32) + across(sent, "tensor", 1).astype(F32)


def swap_tensor(x, dim):
    if lax.axis_size("tensor") != 2:
        return (lax.all_gather(x, "tensor", axis=dim, tiled=True),)
    return x, across(x, "tensor", 1)


def assemble(parts, dim):
    if len(parts) == 1:
        return parts[0]
    own, other = parts
    low = lax.axis_index("tensor") == 0
    return jnp.concatenate([jnp.where(low, own, other), jnp.where(low, other, own)], dim)


def gather_tensor(x, dim):
    return assemble(swap_tensor(x, dim), dim)


def xor_blocks(blocks, index):
    for bit in bits_of(len(blocks)):
        crossed = (index & bit) != 0
        blocks = [jnp.where(crossed, blocks[s ^ bit], block) for s, block in enumerate(blocks)]
    return blocks


def columns_of(x, count):
    size = x.shape[1] // count
    return [x[:, s * size : (s + 1) * size] for s in range(count)]


def pair_sum(keep, send):
    return keep + across(send, "dp", 1)


def send_rows(x):
    n = lax.axis_size("dp")
    groups = [list(range(first, n, 2)) for first in range(2)]
    return lax.all_to_all(x, "dp", 0, 0, tiled=True, axis_index_groups=groups)


def project_kernel(lines, q_cols, at, x_ref, gain_ref, wq_ref, wk_ref, wv_ref, normed_ref, *rest):
    kv_refs, q_refs = rest[:lines], rest[lines : 2 * lines]
    kv_s, q_s = rest[2 * lines :]
    x = x_ref[...].astype(F32)
    scale = lax.rsqrt(jnp.mean(x * x, axis=-1, keepdims=True) + EPS)
    normed = (x * scale * gain_ref[...]).astype(BF)
    normed_ref[...] = normed
    key = dot(normed, wk_ref[...])
    value = dot(normed, wv_ref[...])
    query = dot(normed, wq_ref[...])
    for c in range(lines):
        pair = [key[:, c * HD : (c + 1) * HD], value[:, c * HD : (c + 1) * HD]]
        kv_s[c] = jnp.concatenate(pair, 1).astype(BF)
        q_s[c] = query[:, c * q_cols : (c + 1) * q_cols].astype(BF) * jnp.asarray(0.125, BF)
    for s in range(lines):
        kv_refs[s][...] = kv_s[s ^ at[0]]
        q_refs[s][...] = q_s[s ^ at[0]]


def project(line, x, gain, w_query, w_key, w_value, lines):
    rows, width = x.shape
    q_cols = w_query.shape[1] // lines

    def whole(*shape):
        return pl.BlockSpec(shape, lambda i, m: (0,) * len(shape))

    out = [(rows, width)] + [(rows, PAIR)] * lines + [(rows, q_cols)] * lines
    outs = pl.pallas_call(
        functools.partial(project_kernel, lines, q_cols),
        grid_spec=pltpu.PrefetchScalarGridSpec(
            num_scalar_prefetch=1,
            grid=(1,),
            in_specs=[
                whole(rows, width),
                whole(1, width),
                whole(*w_query.shape),
                whole(*w_key.shape),
                whole(*w_value.shape),
            ],
            out_specs=[whole(*shape) for shape in out],
            scratch_shapes=[
                pltpu.VMEM((lines, rows, PAIR), BF),
                pltpu.VMEM((lines, rows, q_cols), BF),
            ],
        ),
        out_shape=[jax.ShapeDtypeStruct(shape, BF) for shape in out],
        compiler_params=pltpu.CompilerParams(vmem_limit_bytes=48 * 1024 * 1024),
        cost_estimate=pl.CostEstimate(
            flops=2 * rows * width * (w_query.shape[1] + 2 * w_key.shape[1]),
            bytes_accessed=8 << 20,
            transcendentals=0,
        ),
        name="project",
    )(line[None], x, gain[None], w_query, w_key, w_value)
    return outs[0], outs[1 : 1 + lines], outs[1 + lines :]


def spread_heads(refs, out, heads, high):
    for s, ref in enumerate(refs):
        x = ref[...]
        zero = jnp.zeros((x.shape[0], HD), BF)
        for h in range(heads):
            one = x[:, h * HD : (h + 1) * HD]
            out[s, h] = jnp.concatenate([zero, one] if high else [one, zero], 1)


def gather_blocks(refs, out, lines):
    for m, ref in enumerate(refs):
        out[m * lines : (m + 1) * lines] = ref[...]


def position(meta, lines):
    slot = pl.program_id(0)
    return slot, meta[0], meta[1 + slot], meta[1 + lines + slot], meta[1 + 2 * lines + slot]


def walk(low, clear, own, step):
    def body(blk, carry):
        full = (blk >= clear) & (blk < own)

        @pl.when(full)
        def _():
            step(blk, False)

        @pl.when(jnp.logical_not(full))
        def _():
            step(blk, True)

        return carry

    lax.fori_loop(low, own + 1, body, 0)


def visible(blk, own, rows, start):
    key_pos = lax.broadcasted_iota(jnp.int32, (rows, rows), 0) + blk * rows
    q_pos = lax.broadcasted_iota(jnp.int32, (rows, rows), 1) + own * rows
    return (key_pos >= start) & (key_pos <= q_pos)


def attend_kernel(heads, rows, lines, stride, meta, *refs):
    q_refs, kv_refs, start_ref = refs[:lines], refs[lines : lines + stride], refs[lines + stride]
    outs = refs[lines + stride + 1 :]
    mixed_refs, (raw_ref, log_ref, q_s, kv_s, m_s, l_s, acc_s) = outs[:lines], outs[lines:]
    slot, place, own, low, clear = position(meta, lines)

    @pl.when(slot == 0)
    def _():
        spread_heads(q_refs, q_s, heads, False)
        gather_blocks(kv_refs, kv_s, lines)

    m_s[...] = jnp.full_like(m_s, -3e38)
    l_s[...] = jnp.zeros_like(l_s)
    acc_s[...] = jnp.zeros_like(acc_s)

    def step(blk, masked):
        x = blk ^ place
        index = (x % stride) * lines + x // stride
        kv = kv_s[index]
        if masked:
            seen = visible(blk, own, rows, start_ref[0])
        each = range(heads)
        scores = [dot(kv, q_s[slot, h], NT) for h in each]
        if masked:
            scores = [jnp.where(seen, s, NEG) for s in scores]
        m_old = [m_s[h : h + 1, :] for h in each]
        m_new = [jnp.maximum(m_old[h], jnp.max(scores[h], axis=0, keepdims=True)) for h in each]
        p = [jnp.exp(scores[h] - m_new[h]) for h in each]
        alpha = [jnp.exp(m_old[h] - m_new[h]) for h in each]
        added = [dot(kv, p[h].astype(BF), TN) for h in each]
        for h in each:
            l_s[h : h + 1, :] = l_s[h : h + 1, :] * alpha[h] + jnp.sum(p[h], axis=0, keepdims=True)
            acc_s[h] = acc_s[h] * alpha[h] + added[h]
            m_s[h : h + 1, :] = m_new[h]

    walk(low, clear, own, step)
    parts = []
    for h in range(heads):
        out = (acc_s[h] / l_s[h : h + 1, :]).T
        raw_ref[0, h] = out
        parts.append(out[:, HD:])
    log_ref[0] = m_s[...] + jnp.log(l_s[...])
    mixed = jnp.concatenate(parts, 1).astype(BF)
    for s in range(lines):

        @pl.when(slot == s)
        def _(s=s):
            mixed_refs[s][...] = mixed


def whole_block(shape):
    return pl.BlockSpec(shape, lambda i, m: (0,) * len(shape))


def attend(meta, q, kv, start_row, heads):
    lines, stride = len(q), len(kv)
    rows, q_cols = q[0].shape
    narrow = whole_block((rows, q_cols))
    return pl.pallas_call(
        functools.partial(attend_kernel, heads, rows, lines, stride),
        grid_spec=pltpu.PrefetchScalarGridSpec(
            num_scalar_prefetch=1,
            grid=(lines,),
            in_specs=[narrow] * lines
            + [whole_block((lines, rows, PAIR))] * stride
            + [pl.BlockSpec((1, 1, rows), lambda i, m: (i, 0, 0))],
            out_specs=[narrow] * lines
            + [
                pl.BlockSpec((1, heads, rows, PAIR), lambda i, m: (i, 0, 0, 0)),
                pl.BlockSpec((1, 8, rows), lambda i, m: (i, 0, 0)),
            ],
            scratch_shapes=[
                pltpu.VMEM((lines, heads, rows, PAIR), BF),
                pltpu.VMEM((stride * lines, rows, PAIR), BF),
                pltpu.VMEM((8, rows), F32),
                pltpu.VMEM((8, rows), F32),
                pltpu.VMEM((heads, PAIR, rows), F32),
            ],
        ),
        out_shape=[jax.ShapeDtypeStruct((rows, q_cols), BF)] * lines
        + [
            jax.ShapeDtypeStruct((lines, heads, rows, PAIR), F32),
            jax.ShapeDtypeStruct((lines, 8, rows), F32),
        ],
        compiler_params=pltpu.CompilerParams(vmem_limit_bytes=48 * 1024 * 1024),
        cost_estimate=pl.CostEstimate(
            flops=36 * 4 * rows * rows * PAIR * 2, bytes_accessed=8 << 20, transcendentals=36 * rows * rows
        ),
        name="attend",
    )(meta, *q, *kv, start_row)


def attend_back_kernel(heads, rows, lines, stride, meta, *refs):
    q_refs, g_ref, kv_refs = refs[:lines], refs[lines], refs[lines + 1 : lines + 1 + stride]
    raw_ref, log_ref, start_ref = refs[lines + 1 + stride : lines + stride + 4]
    outs = refs[lines + stride + 4 :]
    dq_ref, keep_ref, send_ref, q_s, g_s, kv_s, dq_s, dkv_s, delta_s = outs
    slot, place, own, low, clear = position(meta, lines)

    @pl.when(slot == 0)
    def _():
        spread_heads(q_refs, q_s, heads, False)
        spread_heads([g_ref.at[s ^ (place // stride)] for s in range(lines)], g_s, heads, True)
        gather_blocks(kv_refs, kv_s, lines)
        dkv_s[...] = jnp.zeros_like(dkv_s)

    dq_s[...] = jnp.zeros_like(dq_s)
    for h in range(heads):
        prod = raw_ref[0, h] * g_s[slot, h].astype(F32)
        delta_s[h : h + 1, :] = jnp.sum(prod.T, axis=0, keepdims=True)

    def step(blk, masked):
        x = blk ^ place
        index = (x % stride) * lines + x // stride
        kv = kv_s[index]
        if masked:
            seen = visible(blk, own, rows, start_ref[0])
        for h in range(heads):
            q = q_s[slot, h]
            g = g_s[slot, h]
            s = dot(kv, q, NT)
            if masked:
                s = jnp.where(seen, s, NEG)
            p = jnp.exp(s - log_ref[0, h : h + 1, :])
            gp = dot(kv, g, NT)
            gs = (p * (gp - delta_s[h : h + 1, :])).astype(BF)
            part = dot(gs, q) + dot(p.astype(BF), g)
            dkv_s[index] += part
            dq_s[h] += dot(gs, kv, TN)

    walk(low, clear, own, step)
    dq_ref[0] = jnp.concatenate([dq_s[h][:, :HD] * 0.125 for h in range(heads)], 1).astype(BF)

    @pl.when(slot == lines - 1)
    def _():
        for m in range(stride):
            half = m // 2
            out = send_ref if m % 2 else keep_ref
            out[half * lines : (half + 1) * lines] = dkv_s[m * lines : (m + 1) * lines].astype(BF)


def attend_back(meta, q, g, kv, raw, logs, start_row, heads):
    lines, stride = len(q), len(kv)
    rows, q_cols = q[0].shape
    blocks = lines * stride
    narrow = whole_block((rows, q_cols))
    half = whole_block((blocks // 2, rows, PAIR))
    shift = stride.bit_length() - 1

    def own_line(i, m):
        return i ^ (m[0] >> shift), 0, 0

    return pl.pallas_call(
        functools.partial(attend_back_kernel, heads, rows, lines, stride),
        grid_spec=pltpu.PrefetchScalarGridSpec(
            num_scalar_prefetch=1,
            grid=(lines,),
            in_specs=[narrow] * lines
            + [whole_block((lines, rows, q_cols))]
            + [whole_block((lines, rows, PAIR))] * stride
            + [
                pl.BlockSpec((1, heads, rows, PAIR), lambda i, m: (i, 0, 0, 0)),
                pl.BlockSpec((1, 8, rows), lambda i, m: (i, 0, 0)),
                pl.BlockSpec((1, 1, rows), lambda i, m: (i, 0, 0)),
            ],
            out_specs=[pl.BlockSpec((1, rows, q_cols), own_line)] + [half] * 2,
            scratch_shapes=[
                pltpu.VMEM((lines, heads, rows, PAIR), BF),
                pltpu.VMEM((lines, heads, rows, PAIR), BF),
                pltpu.VMEM((blocks, rows, PAIR), BF),
                pltpu.VMEM((heads, rows, PAIR), F32),
                pltpu.VMEM((blocks, rows, PAIR), F32),
                pltpu.VMEM((8, rows), F32),
            ],
        ),
        out_shape=[jax.ShapeDtypeStruct((lines, rows, q_cols), BF)]
        + [jax.ShapeDtypeStruct((blocks // 2, rows, PAIR), BF)] * 2,
        compiler_params=pltpu.CompilerParams(vmem_limit_bytes=56 * 1024 * 1024),
        cost_estimate=pl.CostEstimate(
            flops=36 * 10 * rows * rows * PAIR * 2, bytes_accessed=10 << 20, transcendentals=36 * rows * rows
        ),
        name="attend_back",
    )(meta, *q, g, *kv, raw, logs, start_row)


def experts_kernel(x_ref, g_ref, gate_ref, wg_ref, wu_ref, wd_ref, out_ref, back_ref, inner_ref):
    each = range(x_ref.shape[0])
    cap = x_ref.shape[1]
    gate_pre = [dot(x_ref[i], wg_ref[i]) for i in each]
    grad_expert = [(gate_ref[i] * g_ref[i].astype(F32)).astype(BF) for i in each]
    grad_act = [dot(grad_expert[i], wd_ref[i], NT) for i in each]
    up_pre = [dot(x_ref[i], wu_ref[i]) for i in each]
    sigma = [jax.nn.sigmoid(gate_pre[i]) for i in each]
    silu = [gate_pre[i] * sigma[i] for i in each]
    act = [(silu[i] * up_pre[i]).astype(BF) for i in each]
    grad_gate = [
        (grad_act[i] * up_pre[i] * sigma[i] * (1.0 + gate_pre[i] * (1.0 - sigma[i]))).astype(BF)
        for i in each
    ]
    grad_up = [(grad_act[i] * silu[i]).astype(BF) for i in each]
    for i in each:
        out = dot(act[i], wd_ref[i])
        inner = jnp.sum(out * g_ref[i].astype(F32), axis=-1, keepdims=True)
        inner_ref[i] = jnp.broadcast_to(inner, (cap, 128)).T[:8]
        out_ref[i] = (gate_ref[i] * out).astype(BF)
        back_ref[i] = (dot(grad_gate[i], wg_ref[i], NT) + dot(grad_up[i], wu_ref[i], NT)).astype(BF)


def run_experts(x, g, gate, w_gate, w_up, w_down):
    experts, cap, width = x.shape
    hidden = w_gate.shape[2]
    at_once = 2 if experts % 2 == 0 else 1

    def of(*shape):
        return pl.BlockSpec((at_once,) + shape, lambda e: (e, 0, 0))

    return pl.pallas_call(
        experts_kernel,
        grid=(experts // at_once,),
        in_specs=[
            of(cap, width),
            of(cap, width),
            of(cap, 1),
            of(width, hidden),
            of(width, hidden),
            of(hidden, width),
        ],
        out_specs=[of(cap, width), of(cap, width), of(8, cap)],
        out_shape=[
            jax.ShapeDtypeStruct((experts, cap, width), BF),
            jax.ShapeDtypeStruct((experts, cap, width), BF),
            jax.ShapeDtypeStruct((experts, 8, cap), F32),
        ],
        compiler_params=pltpu.CompilerParams(vmem_limit_bytes=56 * 1024 * 1024),
        cost_estimate=pl.CostEstimate(
            flops=experts * cap * width * hidden * 12,
            bytes_accessed=experts * width * (hidden * 6 + cap * 8),
            transcendentals=experts * cap * hidden,
        ),
        name="experts",
    )(x, g, gate, w_gate, w_up, w_down)


def weights_kernel(dp, at, a_ref, b_ref, keep_ref, send_ref):
    size = a_ref.shape[1] // dp
    chunk = 4
    odd = at[0] != 0
    for part in range(dp // chunk):
        span = slice(part * chunk * size, (part + 1) * chunk * size)
        block = dot(a_ref[:, span], b_ref[...], TN).astype(BF)
        for pair in range(chunk // 2):
            one = block[2 * pair * size : (2 * pair + 1) * size]
            two = block[(2 * pair + 1) * size : (2 * pair + 2) * size]
            at_pair = part * (chunk // 2) + pair
            keep_ref[at_pair] = jnp.where(odd, two, one)
            send_ref[at_pair] = jnp.where(odd, one, two)


def weight_parts(bit, a, b, dp):
    rows, width = a.shape
    columns = b.shape[1]
    out = (dp // 2, width // dp, columns)
    return pl.pallas_call(
        functools.partial(weights_kernel, dp),
        grid_spec=pltpu.PrefetchScalarGridSpec(
            num_scalar_prefetch=1,
            grid=(1,),
            in_specs=[whole_block(x.shape) for x in (a, b)],
            out_specs=[whole_block(out)] * 2,
        ),
        out_shape=[jax.ShapeDtypeStruct(out, BF)] * 2,
        compiler_params=pltpu.CompilerParams(vmem_limit_bytes=48 * 1024 * 1024),
        cost_estimate=pl.CostEstimate(
            flops=2 * rows * width * columns, bytes_accessed=8 << 20, transcendentals=0
        ),
        name="weights",
    )(bit[None], a, b)


def flat(x):
    return x.reshape(x.shape[0] * x.shape[1], x.shape[2])


def owner_forward_kernel(n_x, n_g, at, gate_ref, wg_ref, wu_ref, wd_ref, *refs):
    x_refs, g_refs, outs = refs[:n_x], refs[n_x : n_x + n_g], refs[n_x + n_g :]
    act_ref, grad_gate_ref, grad_up_ref = outs

    def span(i, ref):
        return pl.ds(pl.multiple_of(at[1 + i], ref.shape[2]), ref.shape[2])

    gate_pre = sum(dot(flat(x[...]), wg_ref[0, span(i, x), :]) for i, x in enumerate(x_refs))
    up_pre = sum(dot(flat(x[...]), wu_ref[0, span(i, x), :]) for i, x in enumerate(x_refs))
    grad_act = sum(
        dot(
            (gate_ref[...] * flat(g[...]).astype(F32)).astype(BF),
            wd_ref[0, :, span(n_x + i, g)],
            NT,
        )
        for i, g in enumerate(g_refs)
    )
    sigma = jax.nn.sigmoid(gate_pre)
    silu = gate_pre * sigma
    act_ref[...] = (silu * up_pre).astype(BF)
    grad_gate_ref[...] = (
        grad_act * up_pre * sigma * (1.0 + gate_pre * (1.0 - sigma))
    ).astype(BF)
    grad_up_ref[...] = (grad_act * silu).astype(BF)


def owner_grads_kernel(n_x, n_g, at, gate_ref, act_ref, grad_gate_ref, grad_up_ref, *refs):
    x_refs, g_refs, outs = refs[:n_x], refs[n_x : n_x + n_g], refs[n_x + n_g :]
    gate_out, up_out, down_out = outs

    def span(i, ref):
        return pl.ds(pl.multiple_of(at[1 + i], ref.shape[2]), ref.shape[2])

    @pl.when(pl.program_id(0) == 0)
    def _():
        for out in outs:
            out[...] = jnp.zeros_like(out)

    for i, ref in enumerate(x_refs):
        x = flat(ref[...])
        gate_out[0, span(i, ref), :] += dot(x, grad_gate_ref[...], TN)
        up_out[0, span(i, ref), :] += dot(x, grad_up_ref[...], TN)
    for i, ref in enumerate(g_refs):
        grad_expert = (gate_ref[...] * flat(ref[...]).astype(F32)).astype(BF)
        down_out[0, :, span(n_x + i, ref)] += dot(act_ref[...], grad_expert, TN)


def owner_call(kernel, name, at, gate, given, x, g, weights, outs, steps):
    dp, cap, _ = x[0].shape
    rows = dp * cap // steps

    def rowwise(a):
        return pl.BlockSpec((rows, a.shape[1]), lambda i, m: (i, 0))

    def piece(a):
        return pl.BlockSpec((dp // steps, cap, a.shape[2]), lambda i, m: (i, 0, 0))

    def weight(a):
        return pl.BlockSpec((1,) + a.shape[1:], lambda i, m: (m[0], 0, 0))

    out_specs = [rowwise(o) if len(o.shape) == 2 else whole_block(o.shape) for o in outs]
    return pl.pallas_call(
        functools.partial(kernel, len(x), len(g)),
        grid_spec=pltpu.PrefetchScalarGridSpec(
            num_scalar_prefetch=1,
            grid=(steps,),
            in_specs=[rowwise(gate)]
            + [rowwise(a) for a in given]
            + [weight(w) for w in weights]
            + [piece(a) for a in list(x) + list(g)],
            out_specs=out_specs,
        ),
        out_shape=outs,
        compiler_params=pltpu.CompilerParams(vmem_limit_bytes=58 * 1024 * 1024),
        cost_estimate=pl.CostEstimate(flops=10 << 30, bytes_accessed=24 << 20, transcendentals=1 << 20),
        name=name,
    )(at, gate, *given, *weights, *x, *g)


def shards(
    layer_in,
    norm1_gain,
    w_query,
    w_key,
    w_value,
    w_out,
    norm2_gain,
    router,
    w_gate,
    w_up,
    w_down,
    segments,
    routes,
    out_grad,
):
    rows, width = layer_in.shape
    kv_heads = w_key.shape[1] // HD
    group = w_query.shape[1] // HD // kv_heads
    q_cols = group * HD
    experts = w_gate.shape[0]
    dp = lax.axis_size("dp")
    place = lax.axis_index("dp")
    tensor_size = lax.axis_size("tensor")
    tensor_at = lax.axis_index("tensor")
    lines = kv_heads
    stride = dp // lines
    line = place >> (stride.bit_length() - 1)
    part = rows // tensor_size
    first = tensor_at * part
    held = experts // dp
    cols = width // tensor_size
    first_col = tensor_at * cols

    names = jnp.arange(experts, dtype=jnp.int32)
    named = jnp.any(routes[:, :, None] == names[None, None, :], axis=1)
    earlier = jnp.tril(jnp.ones((rows, rows), BF), -1)
    slots = jnp.where(named, dot(earlier, named.astype(BF)).astype(jnp.int32), -1)
    in_slot = slots.T[:, None, :] == jnp.arange(CAP, dtype=jnp.int32)[None, :, None]
    to_slots = in_slot.astype(BF).reshape(experts * CAP, rows)
    from_slots = (
        (slots[:, :, None] == jnp.arange(CAP, dtype=jnp.int32)[None, None, :])
        .astype(BF)
        .reshape(rows, experts * CAP)
    )

    def to_experts(x):
        return dot(to_slots, x).astype(BF).reshape(experts, CAP, -1)

    def half(x, i):
        size = cols // 2
        return to_experts(lax.dynamic_slice_in_dim(x, tensor_at * cols + i * size, size, 1))

    q_blocks = place ^ (jnp.arange(lines, dtype=jnp.int32) * stride)
    seg_query = jnp.stack(
        [lax.dynamic_slice_in_dim(segments, q_blocks[s] * rows, rows, 0) for s in range(lines)]
    )
    documents = jnp.arange(DOCS, dtype=jnp.int32)
    lengths_before = jnp.sum(
        (segments[None, :] < documents[:, None]).astype(jnp.int32), axis=1
    )
    starts = jnp.sum(
        jnp.where(seg_query[None] == documents[:, None, None], lengths_before[:, None, None], 0),
        axis=0,
    )
    shift = rows.bit_length() - 1
    meta = jnp.concatenate(
        [place[None], q_blocks, starts[:, 0] >> shift, (starts[:, -1] + rows - 1) >> shift]
    ).astype(jnp.int32)

    normed_in, kv_mine, q_mine = project(line, layer_in, norm1_gain, w_query, w_key, w_value, lines)

    def to_lines(blocks):
        return [b if s == 0 else across(b, "dp", s * stride) for s, b in enumerate(blocks)]

    kv = [jnp.stack(to_lines(kv_mine))]
    q = to_lines(q_mine)
    for bit in reversed(bits_of(stride)):
        kv = [piece for one in kv for piece in (one, across(one, "dp", bit))]
    g_sent, (kv, q, starts, meta) = after([half(out_grad, i) for i in range(2)], (kv, q, starts, meta))
    g_first = to_owner(g_sent[0])
    *mixed_far, raw, logs = attend(meta, q, kv, starts[:, None, :], group)
    mixed_far, g_first = after(mixed_far, g_first)

    def between_lines(x):
        if lines == 1:
            return x
        groups = [[low + j * stride for j in range(lines)] for low in range(stride)]
        return lax.all_to_all(x, "dp", 0, 0, tiled=True, axis_index_groups=groups)

    def from_lines(blocks):
        return xor_blocks(to_lines(blocks), line)

    mixed = jnp.concatenate(from_lines(mixed_far), 1)
    g_late, (mixed, g_slots) = after(g_sent[1], (mixed, to_experts(out_grad)))
    g_second = to_owner(g_late)
    attn = scatter_tensor(dot(mixed, w_out))
    hidden = lax.dynamic_slice_in_dim(layer_in, first, part, 0).astype(F32) + attn
    factor_two = norm_factor(hidden)
    unit_two = hidden * factor_two
    normed_mid = gather_tensor((unit_two * norm2_gain).astype(BF), 0)
    normed_mid, g_second = after(normed_mid, g_second)

    logits = dot(normed_mid, router)
    peak = jnp.max(jnp.where(named, logits, -jnp.inf), axis=1, keepdims=True)
    expo = jnp.where(named, jnp.exp(jnp.where(named, logits - peak, 0.0)), 0.0)
    gates = expo / jnp.sum(expo, axis=1, keepdims=True)
    slot_gate = jnp.sum(jnp.where(in_slot, gates.T[:, None, :], 0.0), axis=-1)

    x_slots = to_experts(normed_mid)
    gate_high = lax.reduce_precision(slot_gate, 8, 7)
    gate_mid = lax.reduce_precision(slot_gate - gate_high, 8, 7)
    gate_pieces = jnp.stack([gate_high, gate_mid, slot_gate - gate_high - gate_mid], 2)
    x_mine = lax.dynamic_slice_in_dim(x_slots, first_col, cols, 2)
    early = cols // 2
    x_late = x_mine[..., early:]
    x_first = to_owner(x_mine[..., :early])
    g_owned = swap_tensor(jnp.concatenate([g_first, g_second], 2), 2)

    out_slots, back_slots, inner_slots = run_experts(
        x_slots, g_slots, slot_gate[:, :, None], w_gate, w_up, w_down
    )
    back_slots, (x_first, g_owned) = after(back_slots, (x_first, g_owned))
    moe_part = dot(from_slots, out_slots.reshape(experts * CAP, width))
    grad_gates = jnp.sum(
        jnp.where(
            slots[:, :, None] == jnp.arange(CAP, dtype=jnp.int32)[None, None, :],
            inner_slots[None, :, 0, :],
            0.0,
        ),
        axis=-1,
    )
    grad_logits = gates * (grad_gates - jnp.sum(gates * grad_gates, axis=-1, keepdims=True))
    high = lax.reduce_precision(grad_logits, 8, 7)
    mid = lax.reduce_precision(grad_logits - high, 8, 7)
    pieces = jnp.concatenate([high, mid, grad_logits - high - mid], 1).astype(BF)
    grad_mid_part = dot(from_slots, back_slots.reshape(experts * CAP, width)) + dot(
        pieces, jnp.concatenate([router] * 3, 1), NT
    )
    (x_late, gate_pieces, router_part), grad_mid_part = after(
        (x_late, gate_pieces, (grad_logits, normed_mid)), grad_mid_part
    )
    x_second = to_owner(
        jnp.concatenate([x_late, jnp.pad(gate_pieces.astype(BF), ((0, 0), (0, 0), (0, 125)))], 2)
    )
    router_part = lax.dot_general(
        router_part[0], router_part[1].astype(F32), TN, precision=HIGH, preferred_element_type=F32
    )
    grad_mid, moe_part = after(scatter_tensor(grad_mid_part), moe_part)
    gain_two_part = jnp.sum(grad_mid * unit_two, axis=0)
    grad_rows = lax.dynamic_slice_in_dim(out_grad, first, part, 0).astype(F32)
    grad_hidden = grad_rows + norm_back(unit_two, factor_two, norm2_gain, grad_mid)
    hidden_low = gather_tensor(grad_hidden.astype(BF), 0)
    grad_mixed = dot(hidden_low, w_out, NT).astype(BF)
    g = jnp.stack(columns_of(grad_mixed, lines))
    g, (x_first, x_second, hidden_late) = after(g, (x_first, x_second, hidden_low))
    g = between_lines(g)
    gate_owned = jnp.sum(x_second[..., cols - early : cols - early + 3].astype(F32), axis=2)
    x_owned = swap_tensor(jnp.concatenate([x_first, x_second[..., : cols - early]], 2), 2)
    proj_part = dot(hidden_late, mixed, TN).astype(BF).reshape(dp // 2, 2, width // dp, -1)
    proj_keep, proj_send = (
        lax.dynamic_index_in_dim(proj_part, (place & 1) ^ other, 1, keepdims=False)
        for other in (0, 1)
    )
    proj_got = send_rows(pair_sum(proj_keep, proj_send))
    dq, keep, send = attend_back(meta, q, g, kv, raw, logs, starts[:, None, :], group)

    dkv = (keep + across(send, "dp", 1)).reshape(stride // 2, lines, rows, PAIR)
    dkv, dq, proj_got = lax.optimization_barrier((dkv, dq, proj_got))
    proj_out = jnp.sum(proj_got.astype(F32), axis=0).T
    for bit in bits_of(stride)[1:]:
        view = dkv.reshape((dkv.shape[0] // 2, 2) + dkv.shape[1:])
        dkv = view[:, 0] + across(view[:, 1], "dp", bit)
    dkv, (moe_part, x_owned, g_owned) = after(dkv[0], (moe_part, x_owned, g_owned))
    dq = between_lines(dq)
    dq = [dq[c] for c in range(lines)]
    dkv = from_lines([dkv[s] for s in range(lines)])
    def mine(x, e):
        return x.reshape((dp, held, CAP) + x.shape[2:])[:, e]

    def pieces_of(parts):
        return [(parts[0], first_col), (parts[1], cols - first_col)]

    def owner_work(x_parts, g_parts):
        if tensor_size == 2:
            x, g = pieces_of(x_parts), pieces_of(g_parts)
        else:
            x, g = [(assemble(x_parts, 2), 0)], [(assemble(g_parts, 2), 0)]
        results = []
        for e in range(held):
            at = jnp.stack([jnp.int32(place * held + e)] + [jnp.int32(o) for _, o in x + g])
            tokens = [mine(a, e) for a, _ in x], [mine(a, e) for a, _ in g]
            gate = mine(gate_owned, e).reshape(dp * CAP, 1)
            hidden_shape = jax.ShapeDtypeStruct((dp * CAP, w_gate.shape[2]), BF)
            given_back = owner_call(
                owner_forward_kernel,
                "owner_forward",
                at,
                gate,
                [],
                *tokens,
                [w_gate, w_up, w_down],
                [hidden_shape] * 3,
                4,
            )
            results.append((at, gate, given_back, *tokens))
        return results

    def owner_grads(owned):
        shapes = [
            jax.ShapeDtypeStruct((1,) + w.shape[1:], F32) for w in (w_gate, w_up, w_down)
        ]
        grad_outs = [
            owner_call(owner_grads_kernel, "owner_grads", at, gate, given, x, g, [], shapes, 2)
            for at, gate, given, x, g in owned
        ]
        return [jnp.concatenate(each, 0) for each in zip(*grad_outs)]

    owned = owner_work(x_owned, g_owned)
    w_all = jnp.concatenate([w_query, w_key, w_value], 1)
    dqkv = jnp.concatenate(dq + [b[:, :HD] for b in dkv] + [b[:, HD:] for b in dkv], 1)
    in_float = layer_in.astype(F32)
    factor_one = norm_factor(in_float)
    unit_one = in_float * factor_one
    dqkv, (owned, moe_rows, unit_one) = after(dqkv, (owned, scatter_tensor(moe_part), unit_one))
    grad_in_part = dot(dqkv, w_all, NT)
    gain_one_part = jnp.sum(grad_in_part * unit_one, axis=0)
    small = jnp.concatenate([router_part, gain_two_part[None], gain_one_part[None]], 0)
    small = total(small.reshape(-1, 128), "dp")
    weight_keep, weight_send = weight_parts(place & 1, normed_in, dqkv, dp)
    weight_pair, (owned, small, grad_in_part) = after(
        pair_sum(weight_keep, weight_send), (owned, small, grad_in_part)
    )
    small = total(small, "tensor")
    owner_outs, small, grad_in_rows = lax.optimization_barrier(
        (owner_grads(owned), small, scatter_tensor(grad_in_part))
    )
    (gate_out, up_out, down_out), weight_got = after(owner_outs, send_rows(weight_pair))
    weight_grad = jnp.sum(weight_got.astype(F32), axis=0)
    layer_out = (hidden + moe_rows).astype(BF)
    ends = [0]
    for size in (lines * q_cols, lines * HD, lines * HD):
        ends.append(ends[-1] + size)
    query_out, key_out, value_out = (weight_grad[:, a:b] for a, b in zip(ends[:-1], ends[1:]))

    factor_rows = lax.dynamic_slice_in_dim(factor_one, first, part, 0)
    unit_rows = lax.dynamic_slice_in_dim(in_float, first, part, 0) * factor_rows
    input_grad = grad_hidden + norm_back(unit_rows, factor_rows, norm1_gain, grad_in_rows)
    small = small.reshape(-1, width)
    gain_one_grad = small[experts + 1]
    gain_two_grad = small[experts]
    router_grad = small[:experts].T

    return (
        layer_out,
        input_grad,
        gain_one_grad,
        query_out,
        key_out,
        value_out,
        proj_out,
        gain_two_grad,
        router_grad,
        gate_out,
        up_out,
        down_out,
    )


def solution(mesh):
    in_specs = (
        P("dp", None),
        P(),
        P(None, "tensor"),
        P(None, "tensor"),
        P(None, "tensor"),
        P("tensor", None),
        P(),
        P(),
        P(None, None, "tensor"),
        P(None, None, "tensor"),
        P(None, "tensor", None),
        P(),
        P("dp", None),
        P("dp", None),
    )
    out_specs = (
        P(("dp", "tensor"), None),
        P(("dp", "tensor"), None),
        P(),
        P("dp", "tensor"),
        P("dp", "tensor"),
        P("dp", "tensor"),
        P("tensor", "dp"),
        P(),
        P(),
        P("dp", None, "tensor"),
        P("dp", None, "tensor"),
        P("dp", "tensor", None),
    )
    return jax.shard_map(shards, mesh=mesh, in_specs=in_specs, out_specs=out_specs, check_vma=False)
```
